256 devices in a mesh: role: 2 (over core), dp: 16 (over z, x_hi), mp: 8 (over x_lo, y).
Axes of the slice: x: 4 (x_hi: 2, x_lo: 2; x = x_hi * 2 + x_lo), y: 4, z: 8, core: 2. Of those that a mesh axis runs over, the one named last changes fastest.
Arguments:
- tokens: bfloat16 [384, 8192], P('mp', 'dp'), may hold values from -50 to 50
- gate_up: bfloat16 [2, 8192, 2, 14336], P('role', 'dp', None, 'mp'), may hold values from -0.0625 to 0.0625
- down: bfloat16 [2, 14336, 8192], P('role', 'mp', 'dp'), may hold values from -0.046875 to 0.046875
- linear: bfloat16 [8192, 8192], P('dp', 'mp'), may hold values from -0.0625 to 0.0625
Outputs:
- gate_up_grad: bfloat16 [2, 8192, 14336], P('role', 'dp', 'mp')
- down_grad: bfloat16 [14336, 8192], P('mp', 'dp')
- linear_grad: bfloat16 [8192, 8192], P('dp', 'mp')
- losses: float32 [2], replicated
The draws below stay inside these ranges and needn't reach their ends.
All inputs are finite; a program needn't handle non-finite values.
Results may differ from the reference program's by a relative error of at most 0.015.
Values may be sent and summed in bfloat16 or wider, within the bound.
A program may use at most 128 MiB of HBM per device.

```python
import jax
import jax.numpy as jnp
from jax import lax

D = 8192
FF = 14336
TOKENS = 384


def draw_tokens(key, part):
    key = jax.random.fold_in(key, 11)
    key_base, key_rows, key_cols = jax.random.split(key, 3)
    place = jnp.arange(TOKENS, dtype=jnp.float32) / TOKENS
    row_power = 0.5 * place + 0.5 * jax.random.uniform(key_rows, (TOKENS,), dtype=jnp.float32)
    col_power = jax.random.uniform(key_cols, (D,), dtype=jnp.float32)
    base = jnp.clip(jax.random.normal(key_base, (TOKENS, D), dtype=jnp.float32), -4.5, 4.5)
    scale = 0.1 * jnp.power(10.0, row_power)[:, None] * jnp.power(10.0, col_power)[None, :]
    return (base * scale).astype(jnp.bfloat16)


def block_scale(key, extent, cuts, least, largest):
    loudness, own = 1.0, jax.random.fold_in(key, 6)
    for position, parts in cuts:
        steps = jnp.exp(jax.random.uniform(jax.random.fold_in(own, position), (parts,), jnp.float32, least / len(cuts), largest / len(cuts)))
        loudness = loudness * jnp.repeat(steps, extent[position] // parts).reshape([-1 if axis == position else 1 for axis in range(len(extent))])
    return loudness


def centred(rng, extent, scale, reach, cuts=(), held_as=jnp.bfloat16):
    drawn = jax.random.normal(rng, extent, jnp.float32) * scale
    if len(cuts) > 0:
        drawn = block_scale(rng, extent, cuts, -0.22, 0.18) * drawn
    return jnp.clip(drawn, min=-reach, max=reach).astype(held_as)


def setup_inputs(seed: int = 0) -> dict:
    keys = jax.random.split(jax.random.key(seed), 5)
    return {
        "tokens": draw_tokens(jax.random.fold_in(keys[4], 71), 0),
        "gate_up": centred(keys[1], (2, D, 2, FF), D ** -0.5, 0.0625, ((0, 2), (1, 16), (3, 8))),
        "down": centred(keys[2], (2, FF, D), FF ** -0.5, 0.046875, ((0, 2), (1, 8), (2, 16))),
        "linear": centred(keys[3], (D, D), D ** -0.5, 0.0625, ((0, 16), (1, 8))),
    }


def contract_rows(left, right):
    return lax.dot_general(left, right, (((0,), (0,)), ((), ())), preferred_element_type=jnp.float32)


def reference(tokens, gate_up, down, linear):
    pre_teacher = jnp.dot(tokens, gate_up[0].reshape(D, 2 * FF), preferred_element_type=jnp.float32).reshape(TOKENS, 2, FF)
    gate_teacher = pre_teacher[:, 0]
    hidden_teacher = (gate_teacher * jax.nn.sigmoid(gate_teacher) * pre_teacher[:, 1]).astype(jnp.bfloat16)
    teacher_rows = jnp.dot(hidden_teacher, down[0], preferred_element_type=jnp.float32).astype(jnp.bfloat16)
    pre_student = jnp.dot(tokens, gate_up[1].reshape(D, 2 * FF), preferred_element_type=jnp.float32).reshape(TOKENS, 2, FF)
    gate_pre = pre_student[:, 0]
    up_pre = pre_student[:, 1]
    gate_sig = jax.nn.sigmoid(gate_pre)
    hidden_student = (gate_pre * gate_sig * up_pre).astype(jnp.bfloat16)
    student_rows = jnp.dot(hidden_student, down[1], preferred_element_type=jnp.float32).astype(jnp.bfloat16)
    linear_rows = jnp.dot(tokens, linear, preferred_element_type=jnp.float32)
    teacher_float = teacher_rows.astype(jnp.float32)
    error_ffn = student_rows.astype(jnp.float32) - teacher_float
    error_lin = linear_rows - teacher_float
    target_norm = jnp.sum(teacher_float * teacher_float)
    losses = jnp.stack([jnp.sum(error_ffn * error_ffn) / target_norm, jnp.sum(error_lin * error_lin) / target_norm])
    factor = 16.0 * D / target_norm
    cot_ffn = (factor * error_ffn).astype(jnp.bfloat16)
    cot_lin = (factor * error_lin).astype(jnp.bfloat16)
    hidden_cot = lax.dot_general(cot_ffn, down[1], (((1,), (1,)), ((), ())), preferred_element_type=jnp.float32)
    gate_cot = (hidden_cot * up_pre * gate_sig * (1.0 + gate_pre * (1.0 - gate_sig))).astype(jnp.bfloat16)
    up_cot = (hidden_cot * gate_pre * gate_sig).astype(jnp.bfloat16)
    gate_up_grad = jnp.stack([contract_rows(tokens, gate_cot), contract_rows(tokens, up_cot)]).astype(jnp.bfloat16)
    down_grad = contract_rows(hidden_student, cot_ffn).astype(jnp.bfloat16)
    linear_grad = contract_rows(tokens, cot_lin).astype(jnp.bfloat16)
    return (gate_up_grad, down_grad, linear_grad, losses)
```

```python
import jax
import jax.numpy as jnp
from jax import lax
from jax.experimental import pallas as pl
from jax.experimental.pallas import tpu as pltpu
from jax.sharding import PartitionSpec as P

MESH = pl.DeviceIdType.MESH
BF16, F32 = jnp.bfloat16, jnp.float32
MODEL = 8192
Z = 8
ROWS = 48
WIDTH = 512
UNITS = 1792
HALF = UNITS // 2
LIN = 1024
QUARTER = LIN // 4


def remote(src, dst, send, recv, device):
    return pltpu.make_async_remote_copy(
        src_ref=src, dst_ref=dst, send_sem=send, recv_sem=recv, device_id=device, device_id_type=MESH
    )


class RingSum:
    def __init__(self, place, part, out, into, send, recv, tags, long_way):
        self.place, self.part, self.out, self.into = place, part, out, into
        self.send, self.recv, self.tags, self.long_way = send, recv, tags, long_way

    def copy(self, way, step, tag):
        at = (way, step - 1) + tag
        return remote(
            self.out.at[at], self.into.at[at], self.send.at[at], self.recv.at[at], self.place.z_next[way]
        )

    def push(self, way, step, tag, first):
        sign = 1 - 2 * way
        block = lax.rem(self.place.z + sign * (5 - step) + Z, Z)
        total = self.part[tag + (block,)]
        if not first:
            self.copy(way, step - 1, tag).wait_recv()
            total = total + self.into[(way, step - 2) + tag].astype(F32)
        self.out[(way, step - 1) + tag] = total.astype(BF16)
        self.copy(way, step, tag).start()

    def begin(self, tag):
        far = self.long_way(tag)
        self.push(far, 1, tag, True)
        self.push(1 - far, 2, tag, True)

    def step(self, step):
        for tag in self.tags:
            for way in (0, 1):
                if step > 2 or way == self.long_way(tag):
                    self.push(way, step, tag, False)

    def result(self, tag):
        total = self.part[tag + (self.place.z,)]
        for way in (0, 1):
            self.copy(way, 4, tag).wait_recv()
            total = total + self.into[(way, 3) + tag].astype(F32)
        return total

    def drain(self):
        for tag in self.tags:
            for way in (0, 1):
                for step in range(1 if way == self.long_way(tag) else 2, 5):
                    self.copy(way, step, tag).wait_send()


class RingGather:
    def __init__(self, place, buf, send, recv, x_send, x_recv):
        self.place, self.buf, self.send, self.recv = place, buf, send, recv
        self.x_send, self.x_recv = x_send, x_recv

    def copy(self, way, step, mine, arriving=False):
        place = self.place
        sign = 1 - 2 * way
        block = lax.rem(place.z - sign * (step if arriving else step - 1) + Z, Z)
        x = place.x if mine else 1 - place.x
        part = self.buf.at[block, x]
        at = (way, step - 1, mine)
        return remote(part, part, self.send.at[at], self.recv.at[at], place.z_next[way])

    def x_copy(self, arriving=False):
        place = self.place
        part = self.buf.at[place.z, 1 - place.x if arriving else place.x]
        return remote(part, part, self.x_send, self.x_recv, place.x_other)

    def begin(self):
        self.copy(0, 1, 1).start()
        self.copy(1, 1, 1).start()
        self.x_copy().start()

    def begin_other(self):
        self.x_copy(True).wait_recv()
        self.copy(0, 1, 0).start()
        self.copy(1, 1, 0).start()

    def step(self, step):
        for mine in (1, 0):
            for way in (0, 1):
                self.copy(way, step, mine, True).wait_recv()
                if step < 3 or way == 1 - mine:
                    self.copy(way, step + 1, mine).start()

    def last(self):
        for mine in (1, 0):
            self.copy(1 - mine, 4, mine, True).wait_recv()

    def drain(self):
        self.x_copy().wait_send()
        for mine in (1, 0):
            for way in (0, 1):
                for step in range(1, 5 if way == 1 - mine else 4):
                    self.copy(way, step, mine).wait_send()


class Direct:
    def __init__(self, me, device_of, out, into, send, recv):
        self.me, self.device_of, self.out, self.into, self.send, self.recv = me, device_of, out, into, send, recv

    def copy(self, apart):
        peer = lax.rem(self.me + apart, 8)
        return remote(
            self.out(peer), self.into(self.me), self.send.at[apart - 1], self.recv.at[apart - 1], self.device_of(peer)
        )

    def start(self):
        for apart in (4, 3, 5, 2, 6, 1, 7):
            self.copy(apart).start()

    def wait(self):
        for apart in (1, 7, 2, 6, 3, 5, 4):
            source = lax.rem(self.me - apart + 8, 8)
            part = self.into(source)
            remote(
                part, part, self.send.at[apart - 1], self.recv.at[apart - 1], self.device_of(source)
            ).wait_recv()

    def drain(self):
        for apart in range(1, 8):
            self.copy(apart).wait_send()


class Place:
    def __init__(self):
        self.role, self.mp = lax.axis_index("role"), lax.axis_index("mp")
        dp = lax.axis_index("dp")
        self.z, self.x = dp // 2, lax.rem(dp, 2)
        role, mp, z, x = self.role, self.mp, self.z, self.x
        self.z_next = ((role, lax.rem(z + 1, Z) * 2 + x, mp), (role, lax.rem(z + Z - 1, Z) * 2 + x, mp))
        self.x_other = (role, z * 2 + 1 - x, mp)
        self.partner = (1 - role, dp, mp)
        self.across = (role, mp * 2 + x, z)
        self.of_z = lambda peer: (role, peer * 2 + x, mp)
        self.of_mp = lambda peer: (role, dp, peer)


def exchange_kernel(
    tok_in, w_in, down_in, lin_in,
    tok_out, cot_out, hid_out, err_out, lin_out, stat_out,
    tok, w, down, lin,
    part, b_out, b_into, bx_out, bx_into, pre, hid,
    d_out, d_into, rows, rows_other, err, target_out, target,
    lin_part, e_out, e_into, ex_out, ex_into, lin_err,
    k_out, k_into, kx_out, kx_into, gate_out, cot,
    m_stat, z_stat, x_stat, x_stat_other, r_stat, r_stat_other,
    load_sem, store_sem,
    tok_s, tok_r, b_s, b_r, bx_s, bx_r, c_s, c_r, cx_s, cx_r,
    d_s, d_r, one_s, one_r, i_s, i_r, e_s, e_r, k_s, k_r,
    j_s, j_r, l_s, l_r, m_s, m_r, z_s, z_r, share_s, share_r,
):
    place = Place()
    role, mp, z, x = place.role, place.mp, place.z, place.x
    student, teacher = role == 1, role == 0
    x_of = (1 - x, x)

    loads = [
        pltpu.make_async_copy(tok_in, tok.at[mp], load_sem.at[0]),
        pltpu.make_async_copy(w_in, w, load_sem.at[1]),
        pltpu.make_async_copy(down_in, down, load_sem.at[2]),
    ] + [
        pltpu.make_async_copy(
            lin_in.at[:, pl.ds(pl.multiple_of(b * 2 * QUARTER + role * QUARTER, QUARTER), QUARTER)],
            lin.at[b],
            load_sem.at[3 + b],
        )
        for b in (0, 1)
    ]
    for load in loads:
        load.start()

    barrier = pltpu.get_barrier_semaphore()

    def greet(device):
        pl.semaphore_signal(barrier, inc=1, device_id=device, device_id_type=MESH)

    for apart in range(1, 8):
        greet(place.of_mp(lax.rem(mp + apart, 8)))
        greet(place.of_z(lax.rem(z + apart, 8)))
    greet(place.x_other)
    greet(place.partner)

    @pl.when(z != mp)
    def _():
        greet(place.across)
        pl.semaphore_wait(barrier, 17)

    @pl.when(z == mp)
    def _():
        pl.semaphore_wait(barrier, 16)

    loads[0].wait()
    tokens = Direct(mp, place.of_mp, lambda peer: tok.at[mp], lambda source: tok.at[source], tok_s, tok_r)
    tokens.start()
    loads[1].wait()
    tokens.wait()
    stores = [pltpu.make_async_copy(tok, tok_out, store_sem.at[0])]
    stores[0].start()
    all_tok = tok[...].reshape(Z * ROWS, WIDTH)

    tags = [(q, g) for q in (0, 1) for g in (0, 1)]
    b_sum = RingSum(place, part, b_out, b_into, b_s, b_r, tags, lambda tag: tag[1])
    for q, g in tags:
        column = pl.multiple_of(g * UNITS + x_of[q] * HALF, 128)
        part[q, g] = jnp.dot(
            tok[...].reshape(Z * ROWS, WIDTH), w[:, pl.ds(column, HALF)], preferred_element_type=F32
        ).reshape(Z, ROWS, HALF)
        b_sum.begin((q, g))
    b_sum.step(2)
    for load in loads[2:]:
        load.wait()
    for q in (0, 1):
        lin_part[q] = jnp.dot(
            tok[...].reshape(Z * ROWS, WIDTH), lin[x_of[q]], preferred_element_type=F32
        ).reshape(Z, ROWS, QUARTER)
    b_sum.step(3)
    b_sum.step(4)

    def bx_copy(g):
        return remote(bx_out.at[g], bx_into.at[g], bx_s.at[g], bx_r.at[g], place.x_other)

    for g in (0, 1):
        bx_out[g] = b_sum.result((0, g)).astype(BF16)
        bx_copy(g).start()
    for g in (0, 1):
        pre[g] = b_sum.result((1, g))
    for g in (0, 1):
        bx_copy(g).wait_recv()
        pre[g] = pre[g] + bx_into[g].astype(F32)
    gate = pre[0]
    hid[z, x] = (gate * jax.nn.sigmoid(gate) * pre[1]).astype(BF16)

    c_all = RingGather(place, hid, c_s, c_r, cx_s.at[0], cx_r.at[0])
    c_all.begin()
    c_all.begin_other()
    for step in (1, 2, 3):
        c_all.step(step)
    e_sum = RingSum(place, lin_part, e_out, e_into, e_s, e_r, [(0,), (1,)], lambda tag: tag[0])
    for tag in e_sum.tags:
        e_sum.begin(tag)
    c_all.last()

    outputs = jnp.zeros((Z * ROWS, WIDTH), F32)
    for b in (0, 1):
        outputs += jnp.dot(
            hid[:, b].reshape(Z * ROWS, HALF), down[b * HALF : (b + 1) * HALF], preferred_element_type=F32
        )
    d_out[...] = outputs.reshape(Z, ROWS, WIDTH).astype(BF16)
    d_sum = Direct(mp, place.of_mp, lambda peer: d_out.at[peer], lambda source: d_into.at[source], d_s, d_r)
    d_sum.start()
    d_into[mp] = d_out[mp]
    e_sum.step(2)

    def hid_share(b):
        return remote(
            hid.at[:, b], hid_out.at[:, :, b * HALF : (b + 1) * HALF], share_s.at[b], share_r.at[b], place.partner
        )

    def hid_store(b):
        return pltpu.make_async_copy(hid.at[:, b], hid_out.at[:, :, b * HALF : (b + 1) * HALF], store_sem.at[1 + b])

    @pl.when(student)
    def _():
        for b in (0, 1):
            hid_share(b).start()
            hid_store(b).start()

    d_sum.wait()
    own = d_into[0].astype(F32)
    for source in range(1, 8):
        own = own + d_into[source].astype(F32)
    rows[...] = own.astype(BF16)

    def rows_copy():
        return remote(rows, rows_other, one_s.at[0], one_r.at[0], place.partner)

    rows_copy().start()
    e_sum.step(3)
    rows_copy().wait_recv()
    mine, other = rows[...].astype(F32), rows_other[...].astype(F32)
    teacher_rows = jnp.where(student, other, mine)
    error = jnp.where(student, mine - other, other - mine)
    err[mp] = error.astype(BF16)
    err_all = Direct(mp, place.of_mp, lambda peer: err.at[mp], lambda source: err.at[source], i_s, i_r)

    @pl.when(student)
    def _():
        err_all.start()

    for b in (0, 1):
        target_out[b] = teacher_rows[:, b * QUARTER : (b + 1) * QUARTER].astype(BF16)

    def target_copy():
        return remote(target_out.at[role], target, one_s.at[1], one_r.at[1], place.across)

    @pl.when(z != mp)
    def _():
        target_copy().start()

    @pl.when(z == mp)
    def _():
        target[...] = target_out[role]

    target_square = jnp.sum(teacher_rows * teacher_rows)
    error_square = jnp.sum(error * error)
    e_sum.step(4)

    def err_share():
        return remote(err, err_out, share_s.at[2], share_r.at[2], place.partner)

    def err_store():
        return pltpu.make_async_copy(err, err_out, store_sem.at[3])

    k_sum = RingSum(place, part.at[:, 0], k_out, k_into, k_s, k_r, [(0,), (1,)], lambda tag: tag[0])

    @pl.when(student)
    def _():
        err_all.wait()
        err_share().start()
        err_store().start()
        for q in (0, 1):
            start = pl.multiple_of(x_of[q] * HALF, 128)
            part[q, 0] = lax.dot_general(
                err[...].reshape(Z * ROWS, WIDTH),
                down[pl.ds(start, HALF)],
                (((1,), (1,)), ((), ())),
                preferred_element_type=F32,
            ).reshape(Z, ROWS, HALF)
            k_sum.begin((q,))

    def ex_copy():
        return remote(ex_out, ex_into, one_s.at[2], one_r.at[2], place.x_other)

    ex_out[...] = e_sum.result((0,)).astype(BF16)
    ex_copy().start()
    linear_rows = e_sum.result((1,))

    @pl.when(student)
    def _():
        k_sum.step(2)

    ex_copy().wait_recv()

    @pl.when(z != mp)
    def _():
        target_copy().wait_recv()

    linear_error = linear_rows + ex_into[...].astype(F32) - target[...].astype(F32)
    lin_err[z, x] = linear_error.astype(BF16)
    linear_square = jnp.sum(linear_error * linear_error)
    row = lax.broadcasted_iota(jnp.int32, (8, 128), 0)
    m_stat[mp] = jnp.where(row == 0, target_square, jnp.where(row == 1, error_square, linear_square))
    m_all = Direct(mp, place.of_mp, lambda peer: m_stat.at[mp], lambda source: m_stat.at[source], m_s, m_r)
    m_all.start()

    @pl.when(student)
    def _():
        k_sum.step(3)

    def in_order(slots):
        total = slots[0]
        for source in range(1, 8):
            total = total + slots[source]
        return total

    def x_stat_copy():
        return remote(x_stat, x_stat_other, one_s.at[3], one_r.at[3], place.x_other)

    m_all.wait()
    x_stat[...] = in_order(m_stat)
    x_stat_copy().start()

    @pl.when(student)
    def _():
        k_sum.step(4)

    x_stat_copy().wait_recv()
    z_stat[z] = x_stat[...] + x_stat_other[...]
    z_all = Direct(z, place.of_z, lambda peer: z_stat.at[z], lambda source: z_stat.at[source], z_s, z_r)
    z_all.start()
    j_all = RingGather(place, lin_err, j_s, j_r, cx_s.at[1], cx_r.at[1])

    def kx_copy():
        return remote(kx_out, kx_into, one_s.at[4], one_r.at[4], place.x_other)

    @pl.when(student)
    def _():
        kx_out[...] = k_sum.result((0,)).astype(BF16)
        kx_copy().start()

    def r_stat_copy():
        return remote(r_stat, r_stat_other, one_s.at[5], one_r.at[5], place.partner)

    z_all.wait()
    r_stat[...] = in_order(z_stat)
    r_stat_copy().start()
    r_stat_copy().wait_recv()
    row_total = r_stat[...] + r_stat_other[...]
    stat = jnp.where(row == 2, row_total, jnp.where(student, r_stat_other[...], r_stat[...]))
    x_stat_other[...] = stat
    stat_store = pltpu.make_async_copy(x_stat_other, stat_out, store_sem.at[4])
    stat_store.start()
    factor = (16.0 * MODEL) / stat[0:1, 0:1]

    def gate_copy():
        return remote(gate_out, cot.at[z, x], one_s.at[6], one_r.at[6], place.partner)

    @pl.when(student)
    def _():
        total = k_sum.result((1,))
        kx_copy().wait_recv()
        hidden_cot = (total + kx_into[...].astype(F32)) * factor
        gate_pre, up_pre = pre[0], pre[1]
        sig = jax.nn.sigmoid(gate_pre)
        gate_out[...] = (hidden_cot * up_pre * sig * (1.0 + gate_pre * (1.0 - sig))).astype(BF16)
        gate_copy().start()
        cot[z, x] = (hidden_cot * gate_pre * sig).astype(BF16)

    @pl.when(teacher)
    def _():
        gate_copy().wait_recv()

    l_all = RingGather(place, cot, l_s, l_r, cx_s.at[2], cx_r.at[2])
    l_all.begin()
    j_all.begin()
    l_all.begin_other()
    j_all.begin_other()
    for step in (1, 2, 3):
        l_all.step(step)
        j_all.step(step)
    j_all.last()

    def lin_columns(b):
        start = pl.multiple_of(b * 2 * QUARTER + role * QUARTER, QUARTER)
        return lin_out.at[:, :, pl.ds(start, QUARTER)]

    def lin_share(b):
        return remote(lin_err.at[:, b], lin_columns(b), share_s.at[3 + b], share_r.at[3 + b], place.partner)

    for b in (0, 1):
        lin_share(b).start()
        stores.append(pltpu.make_async_copy(lin_err.at[:, b], lin_columns(b), store_sem.at[5 + b]))
        stores[-1].start()
    l_all.last()
    for b in (0, 1):
        stores.append(
            pltpu.make_async_copy(cot.at[:, b], cot_out.at[:, :, b * HALF : (b + 1) * HALF], store_sem.at[7 + b])
        )
        stores[-1].start()

    tokens.drain()
    b_sum.drain()
    for g in (0, 1):
        bx_copy(g).wait_send()
    c_all.drain()
    d_sum.drain()
    rows_copy().wait_send()
    e_sum.drain()
    ex_copy().wait_send()
    m_all.drain()
    x_stat_copy().wait_send()
    z_all.drain()
    r_stat_copy().wait_send()
    j_all.drain()
    l_all.drain()
    for b in (0, 1):
        lin_share(b).wait_send()

    @pl.when(z != mp)
    def _():
        target_copy().wait_send()

    @pl.when(student)
    def _():
        err_all.drain()
        k_sum.drain()
        kx_copy().wait_send()
        gate_copy().wait_send()
        err_share().wait_send()
        err_store().wait()
        for b in (0, 1):
            hid_share(b).wait_send()
            hid_store(b).wait()

    @pl.when(teacher)
    def _():
        err_share().wait_recv()
        for b in (0, 1):
            hid_share(b).wait_recv()

    for b in (0, 1):
        lin_share(b).wait_recv()
    stat_store.wait()
    for store in stores:
        store.wait()


def exchange(tokens, w, down, linear):
    def vmem(*shape, dtype=BF16):
        return pltpu.VMEM(shape, dtype)

    def sems(*shape):
        return pltpu.SemaphoreType.DMA(shape)

    def array(*shape, dtype=BF16):
        return jax.ShapeDtypeStruct(shape, dtype)

    anywhere = pl.BlockSpec(memory_space=pl.ANY)
    return pl.pallas_call(
        exchange_kernel,
        out_shape=[
            array(Z, ROWS, WIDTH),
            array(Z, ROWS, UNITS),
            array(Z, ROWS, UNITS),
            array(Z, ROWS, WIDTH),
            array(Z, ROWS, LIN),
            array(8, 128, dtype=F32),
        ],
        in_specs=[anywhere] * 4,
        out_specs=[anywhere] * 6,
        scratch_shapes=[
            vmem(Z, ROWS, WIDTH), vmem(WIDTH, 2 * UNITS), vmem(UNITS, WIDTH), vmem(2, WIDTH, QUARTER),
            vmem(2, 2, Z, ROWS, HALF, dtype=F32), vmem(2, 4, 2, 2, ROWS, HALF), vmem(2, 4, 2, 2, ROWS, HALF),
            vmem(2, ROWS, HALF), vmem(2, ROWS, HALF), vmem(2, ROWS, HALF, dtype=F32), vmem(Z, 2, ROWS, HALF),
            vmem(8, ROWS, WIDTH), vmem(8, ROWS, WIDTH), vmem(ROWS, WIDTH), vmem(ROWS, WIDTH),
            vmem(8, ROWS, WIDTH), vmem(2, ROWS, QUARTER), vmem(ROWS, QUARTER),
            vmem(2, Z, ROWS, QUARTER, dtype=F32), vmem(2, 4, 2, ROWS, QUARTER), vmem(2, 4, 2, ROWS, QUARTER),
            vmem(ROWS, QUARTER), vmem(ROWS, QUARTER), vmem(Z, 2, ROWS, QUARTER),
            vmem(2, 4, 2, ROWS, HALF), vmem(2, 4, 2, ROWS, HALF), vmem(ROWS, HALF), vmem(ROWS, HALF),
            vmem(ROWS, HALF), vmem(Z, 2, ROWS, HALF),
            vmem(8, 8, 128, dtype=F32), vmem(8, 8, 128, dtype=F32),
            vmem(8, 128, dtype=F32), vmem(8, 128, dtype=F32), vmem(8, 128, dtype=F32), vmem(8, 128, dtype=F32),
            sems(5), sems(9),
            sems(7), sems(7), sems(2, 4, 2, 2), sems(2, 4, 2, 2), sems(2), sems(2), sems(2, 4, 2), sems(2, 4, 2),
            sems(3), sems(3),
            sems(7), sems(7), sems(7), sems(7), sems(7), sems(7), sems(2, 4, 2), sems(2, 4, 2),
            sems(2, 4, 2), sems(2, 4, 2),
            sems(2, 4, 2), sems(2, 4, 2), sems(2, 4, 2), sems(2, 4, 2), sems(7), sems(7), sems(7), sems(7),
            sems(5), sems(5),
        ],
        compiler_params=pltpu.CompilerParams(
            collective_id=0, has_side_effects=True, vmem_limit_bytes=56 * 1024 * 1024
        ),
        name="exchange",
    )(tokens, w, down, linear)


def contract_rows(left, right):
    return lax.dot_general(left, right, (((0,), (0,)), ((), ())), preferred_element_type=F32)


def body(tokens, gate_up, down, linear):
    w = gate_up.reshape(WIDTH, 2 * UNITS)
    tok, cot, hid, err, lin_err, stat = exchange(tokens, w, down[0], linear)
    tok, cot = tok.reshape(Z * ROWS, WIDTH), cot.reshape(Z * ROWS, UNITS)
    hid, err = hid.reshape(Z * ROWS, UNITS), err.reshape(Z * ROWS, WIDTH)
    lin_err = lin_err.reshape(Z * ROWS, LIN)
    target_norm = stat[0, 0]
    factor = 16.0 * MODEL / target_norm
    gate_up_grad = contract_rows(tok, cot).astype(BF16)[None]
    down_grad = (factor * contract_rows(hid, err)).astype(BF16)
    linear_grad = (factor * contract_rows(tok, lin_err)).astype(BF16)
    losses = jnp.stack([stat[1, 0] / target_norm, stat[2, 0] / target_norm])
    return (gate_up_grad, down_grad, linear_grad, losses)


def solution(mesh):
    return jax.shard_map(
        body,
        mesh=mesh,
        in_specs=(P("mp", "dp"), P("role", "dp", None, "mp"), P("role", "mp", "dp"), P("dp", "mp")),
        out_specs=(P("role", "dp", "mp"), P("mp", "dp"), P("dp", "mp"), P()),
        check_vma=False,
    )
```

```python
import jax
import jax.numpy as jnp
from jax import lax
from jax.experimental import pallas as pl
from jax.experimental.pallas import tpu as pltpu
from jax.sharding import PartitionSpec as P

MESH = pl.DeviceIdType.MESH
BF16, F32 = jnp.bfloat16, jnp.float32
MODEL = 8192
Z = 8
ROWS = 48
WIDTH = 512
UNITS = 1792
HALF = UNITS // 2
LIN = 1024
QUARTER = LIN // 4


def remote(src, dst, send, recv, device):
    return pltpu.make_async_remote_copy(
        src_ref=src, dst_ref=dst, send_sem=send, recv_sem=recv, device_id=device, device_id_type=MESH
    )


class RingSum:
    def __init__(self, place, part, out, into, send, recv, tags, long_way):
        self.place, self.part, self.out, self.into = place, part, out, into
        self.send, self.recv, self.tags, self.long_way = send, recv, tags, long_way

    def copy(self, way, step, tag):
        at = (way, step - 1) + tag
        return remote(
            self.out.at[at], self.into.at[at], self.send.at[at], self.recv.at[at], self.place.z_next[way]
        )

    def push(self, way, step, tag, first):
        sign = 1 - 2 * way
        block = lax.rem(self.place.z + sign * (5 - step) + Z, Z)
        total = self.part[tag + (block,)]
        if not first:
            self.copy(way, step - 1, tag).wait_recv()
            total = total + self.into[(way, step - 2) + tag].astype(F32)
        self.out[(way, step - 1) + tag] = total.astype(BF16)
        self.copy(way, step, tag).start()

    def begin(self, tag):
        far = self.long_way(tag)
        self.push(far, 1, tag, True)
        self.push(1 - far, 2, tag, True)

    def step(self, step, tags=None):
        for tag in tags or self.tags:
            for way in (0, 1):
                if step > 2 or way == self.long_way(tag):
                    self.push(way, step, tag, False)

    def result(self, tag):
        total = self.part[tag + (self.place.z,)]
        for way in (0, 1):
            self.copy(way, 4, tag).wait_recv()
            total = total + self.into[(way, 3) + tag].astype(F32)
        return total

    def drain(self):
        for tag in self.tags:
            for way in (0, 1):
                for step in range(1 if way == self.long_way(tag) else 2, 5):
                    self.copy(way, step, tag).wait_send()


class RingGather:
    def __init__(self, place, buf, send, recv, x_send, x_recv):
        self.place, self.buf, self.send, self.recv = place, buf, send, recv
        self.x_send, self.x_recv = x_send, x_recv

    def copy(self, way, step, mine, arriving=False):
        place = self.place
        sign = 1 - 2 * way
        block = lax.rem(place.z - sign * (step if arriving else step - 1) + Z, Z)
        x = place.x if mine else 1 - place.x
        part = self.buf.at[block, x]
        at = (way, step - 1, mine)
        return remote(part, part, self.send.at[at], self.recv.at[at], place.z_next[way])

    def x_copy(self, arriving=False):
        place = self.place
        part = self.buf.at[place.z, 1 - place.x if arriving else place.x]
        return remote(part, part, self.x_send, self.x_recv, place.x_other)

    def begin(self):
        self.copy(0, 1, 1).start()
        self.copy(1, 1, 1).start()
        self.x_copy().start()

    def begin_other(self):
        self.x_copy(True).wait_recv()
        self.copy(0, 1, 0).start()
        self.copy(1, 1, 0).start()

    def step(self, step):
        for mine in (1, 0):
            for way in (0, 1):
                self.copy(way, step, mine, True).wait_recv()
                if step < 3 or way == 1 - mine:
                    self.copy(way, step + 1, mine).start()

    def last(self):
        for mine in (1, 0):
            self.copy(1 - mine, 4, mine, True).wait_recv()

    def drain(self):
        self.x_copy().wait_send()
        for mine in (1, 0):
            for way in (0, 1):
                for step in range(1, 5 if way == 1 - mine else 4):
                    self.copy(way, step, mine).wait_send()


class HalfGather:
    def __init__(self, place, buf, send, recv):
        self.place, self.buf, self.send, self.recv = place, buf, send, recv

    def copy(self, way, step, half, arriving=False):
        place = self.place
        sign = 1 - 2 * way
        block = lax.rem(place.z - sign * (step if arriving else step - 1) + Z, Z)
        part = self.buf.at[block, half]
        at = (way, step - 1, half)
        return remote(part, part, self.send.at[at], self.recv.at[at], place.z_next[way])

    def begin(self, half):
        for way in (0, 1):
            self.copy(way, 1, half).start()

    def step(self, step):
        for half in (0, 1):
            for way in (0, 1):
                self.copy(way, step, half, True).wait_recv()
                if step < 3 or way == half:
                    self.copy(way, step + 1, half).start()

    def last(self, half):
        self.copy(half, 4, half, True).wait_recv()

    def drain(self, first=1):
        for half in (0, 1):
            for way in (0, 1):
                for step in range(first, 5 if way == half else 4):
                    self.copy(way, step, half).wait_send()


class Direct:
    def __init__(self, me, device_of, out, into, send, recv):
        self.me, self.device_of, self.out, self.into, self.send, self.recv = me, device_of, out, into, send, recv

    def copy(self, apart):
        peer = lax.rem(self.me + apart, 8)
        return remote(
            self.out(peer), self.into(self.me), self.send.at[apart - 1], self.recv.at[apart - 1], self.device_of(peer)
        )

    def start(self):
        for apart in (4, 3, 5, 2, 6, 1, 7):
            self.copy(apart).start()

    def wait_one(self, apart):
        source = lax.rem(self.me - apart + 8, 8)
        part = self.into(source)
        remote(part, part, self.send.at[apart - 1], self.recv.at[apart - 1], self.device_of(source)).wait_recv()

    def wait(self):
        for apart in (1, 7, 2, 6, 3, 5, 4):
            self.wait_one(apart)

    def drain(self):
        for apart in range(1, 8):
            self.copy(apart).wait_send()


class Total:
    def __init__(self, place, m, zs, x, x_got, r, r_got, m_s, m_r, z_s, z_r, one_s, one_r):
        self.place, self.m, self.zs, self.x, self.x_got, self.r, self.r_got = place, m, zs, x, x_got, r, r_got
        self.m_all = Direct(place.mp, place.of_mp, lambda peer: m.at[place.mp], lambda source: m.at[source], m_s, m_r)
        self.z_all = Direct(place.z, place.of_z, lambda peer: zs.at[place.z], lambda source: zs.at[source], z_s, z_r)
        self.one_s, self.one_r = one_s, one_r

    def x_copy(self):
        return remote(self.x, self.x_got, self.one_s.at[0], self.one_r.at[0], self.place.x_other)

    def r_copy(self):
        return remote(self.r, self.r_got, self.one_s.at[1], self.one_r.at[1], self.place.partner)

    def in_order(self, slots):
        total = slots[0]
        for source in range(1, 8):
            total = total + slots[source]
        return total

    def start(self, tile):
        self.m[self.place.mp] = tile
        self.m_all.start()

    def over_x(self):
        self.m_all.wait()
        self.x[...] = self.in_order(self.m)
        self.x_copy().start()

    def over_z(self):
        self.x_copy().wait_recv()
        self.zs[self.place.z] = self.x[...] + self.x_got[...]
        self.z_all.start()

    def over_role(self):
        self.z_all.wait()
        self.r[...] = self.in_order(self.zs)
        self.r_copy().start()

    def result(self):
        self.r_copy().wait_recv()
        return self.r[...] + self.r_got[...]

    def drain(self):
        self.m_all.drain()
        self.x_copy().wait_send()
        self.z_all.drain()
        self.r_copy().wait_send()


class Place:
    def __init__(self):
        self.role, self.mp, self.dp = lax.axis_index("role"), lax.axis_index("mp"), lax.axis_index("dp")
        dp = self.dp
        self.z, self.x = dp // 2, lax.rem(dp, 2)
        role, mp, z, x = self.role, self.mp, self.z, self.x
        up, down = lax.rem(z + 1, Z) * 2 + x, lax.rem(z + Z - 1, Z) * 2 + x
        self.z_next = ((role, up, mp), (role, down, mp))
        self.z_next_cross = ((1 - role, up, mp), (1 - role, down, mp))
        self.x_other = (role, z * 2 + 1 - x, mp)
        self.partner = (1 - role, dp, mp)
        self.across = (role, mp * 2 + x, z)
        self.of_z = lambda peer: (role, peer * 2 + x, mp)
        self.of_mp = lambda peer: (role, dp, peer)


def exchange_kernel(
    tok_in, w_in, down_in, lin_in,
    tok_out, cot_out, hid_out, err_out, lin_out, stat_out,
    tok, w, down, lin,
    part, b_out, b_into, bx_out, bx_into, pre, hid,
    d_part, d_out, d_into, err, target_out, target,
    lin_part, e_out, e_into, ex_out, ex_into, lin_err,
    k_out, k_into, kx_out, kx_into, gate_out, cot,
    m1, z1, x1, x1_got, r1, r1_got, m2, z2, x2, x2_got, r2, r2_got, stat,
    load_sem, store_sem,
    tok_s, tok_r, hand_s, hand_r, b_s, b_r, bx_s, bx_r, c_s, c_r,
    d_s, d_r, one_s, one_r, i_s, i_r, e_s, e_r, k_s, k_r,
    j_s, j_r, jx_s, jx_r, l_s, l_r, g_s, g_r, gn_s,
    m1_s, m1_r, z1_s, z1_r, o1_s, o1_r, m2_s, m2_r, z2_s, z2_r, o2_s, o2_r,
    share_s, share_r,
):
    place = Place()
    role, mp, dp, z, x = place.role, place.mp, place.dp, place.z, place.x
    student, teacher = role == 1, role == 0
    x_of = (1 - x, x)
    halves = (0, 1)

    loads = [
        pltpu.make_async_copy(tok_in.at[:, b * QUARTER : (b + 1) * QUARTER], tok.at[b, mp], load_sem.at[b])
        for b in halves
    ]
    loads += [
        pltpu.make_async_copy(w_in, w, load_sem.at[2]),
        pltpu.make_async_copy(down_in, down, load_sem.at[3]),
    ]
    loads += [
        pltpu.make_async_copy(
            lin_in.at[:, pl.ds(pl.multiple_of(b * 2 * QUARTER + role * QUARTER, QUARTER), QUARTER)],
            lin.at[b],
            load_sem.at[4 + b],
        )
        for b in halves
    ]
    for load in loads:
        load.start()

    barrier = pltpu.get_barrier_semaphore()

    def greet(device):
        pl.semaphore_signal(barrier, inc=1, device_id=device, device_id_type=MESH)

    for apart in range(1, 8):
        greet(place.of_mp(lax.rem(mp + apart, 8)))
        greet((1 - role, dp, lax.rem(mp + apart, 8)))
        greet(place.of_z(lax.rem(z + apart, 8)))
    greet(place.x_other)
    greet(place.partner)
    for way in (0, 1):
        greet(place.z_next_cross[way])

    @pl.when(z != mp)
    def _():
        greet(place.across)
        pl.semaphore_wait(barrier, 26)

    @pl.when(z == mp)
    def _():
        pl.semaphore_wait(barrier, 25)

    for load in loads[:2]:
        load.wait()
    tokens = Direct(mp, place.of_mp, lambda peer: tok.at[role, mp], lambda source: tok.at[role, source], tok_s, tok_r)
    tokens.start()

    def hand(apart, arriving=False):
        source = lax.rem(mp - apart + 8, 8)
        part_of = tok.at[1 - role if arriving else role, source]
        return remote(part_of, part_of, hand_s.at[apart - 1], hand_r.at[apart - 1], place.partner)

    for apart in (1, 7, 2, 6, 3, 5, 4):
        tokens.wait_one(apart)
        hand(apart).start()
    loads[2].wait()
    for apart in (1, 7, 2, 6, 3, 5, 4):
        hand(apart, True).wait_recv()
    stores = [pltpu.make_async_copy(tok, tok_out, store_sem.at[0])]
    stores[0].start()

    def all_tokens():
        return jnp.concatenate([tok[b].reshape(Z * ROWS, QUARTER) for b in halves], axis=1)

    tags = [(h, g) for h in halves for g in (0, 1)]
    b_sum = RingSum(place, part, b_out, b_into, b_s, b_r, tags, lambda tag: tag[1])
    for h, g in tags:
        column = g * UNITS + h * HALF
        part[h, g] = jnp.dot(
            all_tokens(), w[:, column : column + HALF], preferred_element_type=F32
        ).reshape(Z, ROWS, HALF)
        b_sum.begin((h, g))
    b_sum.step(2)
    for load in loads[3:]:
        load.wait()
    for q in (0, 1):
        lin_part[q] = jnp.dot(all_tokens(), lin[x_of[q]], preferred_element_type=F32).reshape(Z, ROWS, QUARTER)
    b_sum.step(3)
    b_sum.step(4)

    def bx_copy(h, g):
        return remote(bx_out.at[h, g], bx_into.at[h, g], bx_s.at[h, g], bx_r.at[h, g], place.x_other)

    for h, g in tags:
        bx_out[h, g] = b_sum.result((h, g)).astype(BF16)
        bx_copy(h, g).start()

    c_all = HalfGather(place, hid, c_s, c_r)
    for h in halves:
        for g in (0, 1):
            bx_copy(h, g).wait_recv()
            pre[h, g] = bx_out[h, g].astype(F32) + bx_into[h, g].astype(F32)
        gate = pre[h, 0]
        hid[z, h] = (gate * jax.nn.sigmoid(gate) * pre[h, 1]).astype(BF16)
        c_all.begin(h)
    e_sum = RingSum(place, lin_part, e_out, e_into, e_s, e_r, [(0,), (1,)], lambda tag: tag[0])
    for step in (1, 2, 3):
        c_all.step(step)
    for tag in e_sum.tags:
        e_sum.begin(tag)

    c_all.last(0)
    d_part[...] = jnp.dot(hid[:, 0].reshape(Z * ROWS, HALF), down[:HALF], preferred_element_type=F32)
    c_all.last(1)

    def d_copy(b, apart):
        peer = lax.rem(mp + apart, 8)
        return remote(
            d_out.at[b, peer], d_into.at[role, mp], d_s.at[b, apart - 1], d_r.at[role, apart - 1], (b, dp, peer)
        )

    def d_arrival(source_role, apart):
        source = lax.rem(mp - apart + 8, 8)
        got = d_into.at[source_role, source]
        return remote(got, got, d_s.at[0, apart - 1], d_r.at[source_role, apart - 1], (source_role, dp, source))

    def d_partner(arriving=False):
        return remote(
            d_out.at[1 - role, mp],
            d_into.at[1 - role if arriving else role, mp],
            one_s.at[0],
            one_r.at[0],
            place.partner,
        )

    for b in halves:
        columns = slice(b * QUARTER, (b + 1) * QUARTER)
        total = d_part[:, columns] + jnp.dot(
            hid[:, 1].reshape(Z * ROWS, HALF), down[HALF:, columns], preferred_element_type=F32
        )
        d_out[b] = total.reshape(Z, ROWS, QUARTER).astype(BF16)
        for apart in (4, 3, 5, 2, 6, 1, 7):
            d_copy(b, apart).start()
    d_partner().start()
    d_into[role, mp] = d_out[role, mp]
    e_sum.step(2)
    for apart in (1, 7, 2, 6, 3, 5, 4):
        for source_role in (0, 1):
            d_arrival(source_role, apart).wait_recv()
    d_partner(True).wait_recv()

    def summed(source_role):
        own = d_into[source_role, 0].astype(F32)
        for source in range(1, 8):
            own = own + d_into[source_role, source].astype(F32)
        return own.astype(BF16)

    teacher_rows = summed(0)
    error = summed(1).astype(F32) - teacher_rows.astype(F32)
    err[role, mp] = error.astype(BF16)

    def err_copy(apart):
        peer = lax.rem(mp + apart, 8)
        return remote(
            err.at[role, mp], err.at[role, mp], i_s.at[apart - 1], i_r.at[role, apart - 1], (1, dp, peer)
        )

    def err_arrival(source_role, apart):
        source = lax.rem(mp - apart + 8, 8)
        got = err.at[source_role, source]
        return remote(got, got, i_s.at[apart - 1], i_r.at[source_role, apart - 1], (source_role, dp, source))

    def err_partner():
        return remote(err.at[0, mp], err.at[0, mp], one_s.at[1], one_r.at[1], place.partner)

    for apart in (4, 3, 5, 2, 6, 1, 7):
        err_copy(apart).start()

    @pl.when(teacher)
    def _():
        err_partner().start()

    target_out[...] = teacher_rows

    def target_copy():
        return remote(target_out, target, one_s.at[2], one_r.at[2], place.across)

    @pl.when(z != mp)
    def _():
        target_copy().start()

    @pl.when(z == mp)
    def _():
        target[...] = target_out[...]

    row = lax.broadcasted_iota(jnp.int32, (8, 128), 0)
    teacher_float = teacher_rows.astype(F32)
    target_square = jnp.sum(teacher_float * teacher_float)
    error_square = jnp.sum(error * error)
    norm = Total(place, m1, z1, x1, x1_got, r1, r1_got, m1_s, m1_r, z1_s, z1_r, o1_s, o1_r)
    norm.start(jnp.where(row == 0, target_square, jnp.where(row == 1, error_square, 0.0)))
    e_sum.step(3)

    k_sum = RingSum(place, part.at[:, 0], k_out, k_into, k_s, k_r, [(0,), (1,)], lambda tag: tag[0])

    def err_share():
        return remote(err, err_out, share_s.at[2], share_r.at[2], place.partner)

    def err_store():
        return pltpu.make_async_copy(err, err_out, store_sem.at[3])

    def hid_share(h):
        return remote(
            hid.at[:, h], hid_out.at[:, :, h * HALF : (h + 1) * HALF], share_s.at[h], share_r.at[h], place.partner
        )

    def hid_store(h):
        return pltpu.make_async_copy(hid.at[:, h], hid_out.at[:, :, h * HALF : (h + 1) * HALF], store_sem.at[1 + h])

    @pl.when(student)
    def _():
        for apart in (1, 7, 2, 6, 3, 5, 4):
            for source_role in (0, 1):
                err_arrival(source_role, apart).wait_recv()
        err_partner().wait_recv()
        for h in halves:
            part[h, 0] = lax.dot_general(
                jnp.concatenate([err[b].reshape(Z * ROWS, QUARTER) for b in halves], axis=1),
                down[h * HALF : (h + 1) * HALF],
                (((1,), (1,)), ((), ())),
                preferred_element_type=F32,
            ).reshape(Z, ROWS, HALF)
            k_sum.begin((h,))
        err_share().start()
        err_store().start()
        for h in halves:
            hid_share(h).start()
            hid_store(h).start()

    norm.over_x()
    e_sum.step(4)
    norm.over_z()

    @pl.when(student)
    def _():
        k_sum.step(2)

    def ex_copy():
        return remote(ex_out, ex_into, one_s.at[3], one_r.at[3], place.x_other)

    ex_out[...] = e_sum.result((0,)).astype(BF16)
    ex_copy().start()
    linear_rows = e_sum.result((1,))
    norm.over_role()

    @pl.when(student)
    def _():
        k_sum.step(3)

    ex_copy().wait_recv()

    @pl.when(z != mp)
    def _():
        target_copy().wait_recv()

    linear_error = linear_rows + ex_into[...].astype(F32) - target[...].astype(F32)
    lin_err[z, x] = linear_error.astype(BF16)
    j_all = RingGather(place, lin_err, j_s, j_r, jx_s.at[0], jx_r.at[0])
    j_all.begin()
    loss = Total(place, m2, z2, x2, x2_got, r2, r2_got, m2_s, m2_r, z2_s, z2_r, o2_s, o2_r)
    loss.start(jnp.where(row == 2, jnp.sum(linear_error * linear_error), 0.0))

    @pl.when(student)
    def _():
        k_sum.step(4)

    stat[...] = norm.result()
    j_all.begin_other()
    loss.over_x()

    def kx_copy(h):
        return remote(kx_out.at[h], kx_into.at[h], bx_s.at[2, h], bx_r.at[2, h], place.x_other)

    def gate_copy(h):
        return remote(gate_out.at[h], cot.at[z, h], g_s.at[h], g_r.at[h], place.partner)

    l_all = HalfGather(place, cot, l_s, l_r)

    def gate_next(way, h):
        return remote(
            gate_out.at[h], cot.at[z, h], gn_s.at[way, h], l_r.at[way, 0, h], place.z_next_cross[way]
        )

    @pl.when(student)
    def _():
        for h in halves:
            kx_out[h] = k_sum.result((h,)).astype(BF16)
            kx_copy(h).start()
        factor = (16.0 * MODEL) / stat[0:1, 0:1]
        for h in halves:
            kx_copy(h).wait_recv()
            hidden_cot = (kx_out[h].astype(F32) + kx_into[h].astype(F32)) * factor
            gate_pre, up_pre = pre[h, 0], pre[h, 1]
            sig = jax.nn.sigmoid(gate_pre)
            gate_out[h] = (hidden_cot * up_pre * sig * (1.0 + gate_pre * (1.0 - sig))).astype(BF16)
            for way in (0, 1):
                gate_next(way, h).start()
            cot[z, h] = (hidden_cot * gate_pre * sig).astype(BF16)
            l_all.begin(h)
            gate_copy(h).start()

    j_all.step(1)
    loss.over_z()
    l_all.step(1)
    j_all.step(2)
    loss.over_role()
    l_all.step(2)
    j_all.step(3)
    stat[...] = stat[...] + loss.result()
    stores.append(pltpu.make_async_copy(stat, stat_out, store_sem.at[4]))
    stores[-1].start()
    l_all.step(3)
    j_all.last()

    def lin_columns(b):
        start = pl.multiple_of(b * 2 * QUARTER + role * QUARTER, QUARTER)
        return lin_out.at[:, :, pl.ds(start, QUARTER)]

    def lin_share(b):
        return remote(lin_err.at[:, b], lin_columns(b), share_s.at[3 + b], share_r.at[3 + b], place.partner)

    def lin_arrival(b):
        start = pl.multiple_of(b * 2 * QUARTER + (1 - role) * QUARTER, QUARTER)
        got = lin_out.at[:, :, pl.ds(start, QUARTER)]
        return remote(lin_err.at[:, b], got, share_s.at[3 + b], share_r.at[3 + b], place.partner)

    for b in halves:
        lin_share(b).start()
        stores.append(pltpu.make_async_copy(lin_err.at[:, b], lin_columns(b), store_sem.at[5 + b]))
        stores[-1].start()

    @pl.when(teacher)
    def _():
        for h in halves:
            gate_copy(h).wait_recv()

    for h in halves:
        l_all.last(h)
        stores.append(
            pltpu.make_async_copy(cot.at[:, h], cot_out.at[:, :, h * HALF : (h + 1) * HALF], store_sem.at[7 + h])
        )
        stores[-1].start()

    tokens.drain()
    for apart in range(1, 8):
        hand(apart).wait_send()
        err_copy(apart).wait_send()
        for b in halves:
            d_copy(b, apart).wait_send()
    d_partner().wait_send()
    b_sum.drain()
    for h, g in tags:
        bx_copy(h, g).wait_send()
    c_all.drain()
    e_sum.drain()
    ex_copy().wait_send()
    norm.drain()
    loss.drain()
    j_all.drain()
    for b in halves:
        lin_share(b).wait_send()

    @pl.when(z != mp)
    def _():
        target_copy().wait_send()

    @pl.when(student)
    def _():
        k_sum.drain()
        l_all.drain()
        err_share().wait_send()
        err_store().wait()
        for h in halves:
            kx_copy(h).wait_send()
            gate_copy(h).wait_send()
            for way in (0, 1):
                gate_next(way, h).wait_send()
            hid_share(h).wait_send()
            hid_store(h).wait()

    @pl.when(teacher)
    def _():
        l_all.drain(2)
        err_partner().wait_send()
        err_share().wait_recv()
        for h in halves:
            hid_share(h).wait_recv()

    for b in halves:
        lin_arrival(b).wait_recv()
    for store in stores:
        store.wait()


def exchange(tokens, w, down, linear):
    def vmem(*shape, dtype=BF16):
        return pltpu.VMEM(shape, dtype)

    def sems(*shape):
        return pltpu.SemaphoreType.DMA(shape)

    def array(*shape, dtype=BF16):
        return jax.ShapeDtypeStruct(shape, dtype)

    def total_tiles():
        return [vmem(8, 8, 128, dtype=F32)] * 2 + [vmem(8, 128, dtype=F32)] * 4

    anywhere = pl.BlockSpec(memory_space=pl.ANY)
    return pl.pallas_call(
        exchange_kernel,
        out_shape=[
            array(2, Z, ROWS, QUARTER),
            array(Z, ROWS, UNITS),
            array(Z, ROWS, UNITS),
            array(2, Z, ROWS, QUARTER),
            array(Z, ROWS, LIN),
            array(8, 128, dtype=F32),
        ],
        in_specs=[anywhere] * 4,
        out_specs=[anywhere] * 6,
        scratch_shapes=[
            vmem(2, Z, ROWS, QUARTER), vmem(WIDTH, 2 * UNITS), vmem(UNITS, WIDTH), vmem(2, WIDTH, QUARTER),
            vmem(2, 2, Z, ROWS, HALF, dtype=F32), vmem(2, 4, 2, 2, ROWS, HALF), vmem(2, 4, 2, 2, ROWS, HALF),
            vmem(2, 2, ROWS, HALF), vmem(2, 2, ROWS, HALF), vmem(2, 2, ROWS, HALF, dtype=F32), vmem(Z, 2, ROWS, HALF),
            vmem(Z * ROWS, WIDTH, dtype=F32), vmem(2, 8, ROWS, QUARTER), vmem(2, 8, ROWS, QUARTER),
            vmem(2, 8, ROWS, QUARTER), vmem(ROWS, QUARTER), vmem(ROWS, QUARTER),
            vmem(2, Z, ROWS, QUARTER, dtype=F32), vmem(2, 4, 2, ROWS, QUARTER), vmem(2, 4, 2, ROWS, QUARTER),
            vmem(ROWS, QUARTER), vmem(ROWS, QUARTER), vmem(Z, 2, ROWS, QUARTER),
            vmem(2, 4, 2, ROWS, HALF), vmem(2, 4, 2, ROWS, HALF), vmem(2, ROWS, HALF), vmem(2, ROWS, HALF),
            vmem(2, ROWS, HALF), vmem(Z, 2, ROWS, HALF),
            *total_tiles(), *total_tiles(), vmem(8, 128, dtype=F32),
            sems(6), sems(9),
            sems(7), sems(7), sems(7), sems(7), sems(2, 4, 2, 2), sems(2, 4, 2, 2), sems(3, 2), sems(3, 2),
            sems(2, 4, 2), sems(2, 4, 2),
            sems(2, 7), sems(2, 7), sems(4), sems(4), sems(7), sems(2, 7), sems(2, 4, 2), sems(2, 4, 2),
            sems(2, 4, 2), sems(2, 4, 2),
            sems(2, 4, 2), sems(2, 4, 2), sems(1), sems(1), sems(2, 4, 2), sems(2, 4, 2), sems(2), sems(2), sems(2, 2),
            sems(7), sems(7), sems(7), sems(7), sems(2), sems(2),
            sems(7), sems(7), sems(7), sems(7), sems(2), sems(2),
            sems(5), sems(5),
        ],
        compiler_params=pltpu.CompilerParams(
            collective_id=0, has_side_effects=True, vmem_limit_bytes=34 * 1024 * 1024
        ),
        name="exchange",
    )(tokens, w, down, linear)


def contract_rows(left, right):
    return lax.dot_general(left, right, (((0,), (0,)), ((), ())), preferred_element_type=F32)


BLOCK = 256


def gradients_kernel(tok, cot, hid, err, lin_err, stat, unit_grad, down_grad, linear_grad, losses, turned):
    step = pl.program_id(0)
    factor = (16.0 * MODEL) / stat[0:1, 0:1]

    @pl.when(step == 0)
    def _():
        for b in (0, 1):
            turned[b * QUARTER : (b + 1) * QUARTER] = tok[b].T
        share = stat[...] / stat[0:1, 0:1]
        losses[0] = share[1, 0]
        losses[1] = share[2, 0]

    unit_grad[...] = jnp.dot(turned[...], cot[...], preferred_element_type=F32).astype(BF16)
    for b in (0, 1):
        down_grad[:, b * QUARTER : (b + 1) * QUARTER] = (factor * contract_rows(hid[...], err[b])).astype(BF16)

    @pl.when(step < LIN // BLOCK)
    def _():
        linear_grad[...] = (factor * jnp.dot(turned[...], lin_err[...], preferred_element_type=F32)).astype(BF16)


def gradients(tok, cot, hid, err, lin_err, stat):
    tokens = Z * ROWS
    last = LIN // BLOCK - 1
    halves = pl.BlockSpec((2, tokens, QUARTER), lambda i: (0, 0, 0))
    return pl.pallas_call(
        gradients_kernel,
        grid=(UNITS // BLOCK,),
        out_shape=[
            jax.ShapeDtypeStruct((WIDTH, UNITS), BF16),
            jax.ShapeDtypeStruct((UNITS, WIDTH), BF16),
            jax.ShapeDtypeStruct((WIDTH, LIN), BF16),
            jax.ShapeDtypeStruct((2,), F32),
        ],
        in_specs=[
            halves,
            pl.BlockSpec((tokens, BLOCK), lambda i: (0, i)),
            pl.BlockSpec((tokens, BLOCK), lambda i: (0, i)),
            halves,
            pl.BlockSpec((tokens, BLOCK), lambda i: (0, jnp.minimum(i, last))),
            pl.BlockSpec((8, 128), lambda i: (0, 0)),
        ],
        out_specs=[
            pl.BlockSpec((WIDTH, BLOCK), lambda i: (0, i)),
            pl.BlockSpec((BLOCK, WIDTH), lambda i: (i, 0)),
            pl.BlockSpec((WIDTH, BLOCK), lambda i: (0, jnp.minimum(i, last))),
            pl.BlockSpec(memory_space=pltpu.SMEM),
        ],
        scratch_shapes=[pltpu.VMEM((WIDTH, tokens), BF16)],
        compiler_params=pltpu.CompilerParams(vmem_limit_bytes=16 * 1024 * 1024),
        name="gradients",
    )(tok, cot, hid, err, lin_err, stat)


def body(tokens, gate_up, down, linear):
    w = gate_up.reshape(WIDTH, 2 * UNITS)
    tok, cot, hid, err, lin_err, stat = exchange(tokens, w, down[0], linear)
    rows = Z * ROWS
    unit_grad, down_grad, linear_grad, losses = gradients(
        tok.reshape(2, rows, QUARTER),
        cot.reshape(rows, UNITS),
        hid.reshape(rows, UNITS),
        err.reshape(2, rows, QUARTER),
        lin_err.reshape(rows, LIN),
        stat,
    )
    return (unit_grad[None], down_grad, linear_grad, losses)


def solution(mesh):
    return jax.shard_map(
        body,
        mesh=mesh,
        in_specs=(P("mp", "dp"), P("role", "dp", None, "mp"), P("role", "mp", "dp"), P("dp", "mp")),
        out_specs=(P("role", "dp", "mp"), P("mp", "dp"), P("dp", "mp"), P()),
        check_vma=False,
    )
```

```python
import jax
import jax.numpy as jnp
from jax import lax
from jax.experimental import pallas as pl
from jax.experimental.pallas import tpu as pltpu
from jax.sharding import PartitionSpec as P

MESH = pl.DeviceIdType.MESH
BF16, F32 = jnp.bfloat16, jnp.float32
MODEL = 8192
Z = 8
ROWS = 48
WIDTH = 512
UNITS = 1792
WHOLE = 1024
SPLIT = 384
LIN = 1024
QUARTER = LIN // 4


def remote(src, dst, send, recv, device):
    return pltpu.make_async_remote_copy(
        src_ref=src, dst_ref=dst, send_sem=send, recv_sem=recv, device_id=device, device_id_type=MESH
    )


class RingSum:
    def __init__(self, place, part, out, into, send, recv, tags, long_way):
        self.place, self.part, self.out, self.into = place, part, out, into
        self.send, self.recv, self.tags, self.long_way = send, recv, tags, long_way

    def copy(self, way, step, tag):
        at = (way, step - 1) + tag
        return remote(
            self.out.at[at], self.into.at[at], self.send.at[at], self.recv.at[at], self.place.z_next[way]
        )

    def push(self, way, step, tag, first):
        sign = 1 - 2 * way
        total = self.local(tag, sign * (5 - step))
        if not first:
            self.copy(way, step - 1, tag).wait_recv()
            total = total + self.into[(way, step - 2) + tag].astype(F32)
        self.out[(way, step - 1) + tag] = total.astype(BF16)
        self.copy(way, step, tag).start()

    def local(self, tag, offset):
        return self.part[tag + (lax.rem(self.place.z + offset + Z, Z),)]

    def begin(self, tag):
        far = self.long_way(tag)
        self.push(far, 1, tag, True)
        self.push(1 - far, 2, tag, True)

    def step(self, step, tags=None):
        for tag in tags or self.tags:
            for way in (0, 1):
                if step > 2 or way == self.long_way(tag):
                    self.push(way, step, tag, False)

    def result(self, tag):
        total = self.local(tag, 0)
        for way in (0, 1):
            self.copy(way, 4, tag).wait_recv()
            total = total + self.into[(way, 3) + tag].astype(F32)
        return total

    def drain(self):
        for tag in self.tags:
            for way in (0, 1):
                for step in range(1 if way == self.long_way(tag) else 2, 5):
                    self.copy(way, step, tag).wait_send()


class RingGather:
    def __init__(self, place, buf, send, recv, x_send, x_recv):
        self.place, self.buf, self.send, self.recv = place, buf, send, recv
        self.x_send, self.x_recv = x_send, x_recv

    def copy(self, way, step, mine, arriving=False):
        place = self.place
        sign = 1 - 2 * way
        block = lax.rem(place.z - sign * (step if arriving else step - 1) + Z, Z)
        x = place.x if mine else 1 - place.x
        part = self.buf.at[block, x]
        at = (way, step - 1, mine)
        return remote(part, part, self.send.at[at], self.recv.at[at], place.z_next[way])

    def x_copy(self, arriving=False):
        place = self.place
        part = self.buf.at[place.z, 1 - place.x if arriving else place.x]
        return remote(part, part, self.x_send, self.x_recv, place.x_other)

    def begin(self):
        self.copy(0, 1, 1).start()
        self.copy(1, 1, 1).start()
        self.x_copy().start()

    def begin_other(self):
        self.x_copy(True).wait_recv()
        self.copy(0, 1, 0).start()
        self.copy(1, 1, 0).start()

    def step(self, step):
        for mine in (1, 0):
            for way in (0, 1):
                self.copy(way, step, mine, True).wait_recv()
                if step < 3 or way == 1 - mine:
                    self.copy(way, step + 1, mine).start()

    def last(self):
        for mine in (1, 0):
            self.copy(1 - mine, 4, mine, True).wait_recv()

    def drain(self):
        self.x_copy().wait_send()
        for mine in (1, 0):
            for way in (0, 1):
                for step in range(1, 5 if way == 1 - mine else 4):
                    self.copy(way, step, mine).wait_send()


class PairRingSum(RingSum):
    def pair(self, other, x_out, x_into, x_send, x_recv):
        self.other, self.x_out, self.x_into, self.x_send, self.x_recv = other, x_out, x_into, x_send, x_recv
        self.got = set()

    def block(self, offset):
        return lax.rem(self.place.z + offset, Z)

    def x_copy(self, offset):
        block = self.block(offset)
        return remote(
            self.x_out.at[block], self.x_into.at[block], self.x_send.at[offset], self.x_recv.at[offset], self.place.x_other
        )

    def exchange(self):
        for offset in (4, 3, 5, 2, 6, 1, 7, 0):
            block = self.block(offset)
            for tag in self.tags:
                self.x_out[(block,) + tag] = self.other[tag + (block,)].astype(BF16)
            self.x_copy(offset).start()

    def local(self, tag, offset):
        offset = offset % Z
        if offset not in self.got:
            self.got.add(offset)
            self.x_copy(offset).wait_recv()
        block = self.block(offset)
        return self.part[tag + (block,)] + self.x_into[(block,) + tag].astype(F32)

    def drain(self):
        super().drain()
        for offset in range(Z):
            self.x_copy(offset).wait_send()


class Gather:
    def __init__(self, place, whole, split, w_send, w_recv, s_send, s_recv, x_send, x_recv):
        self.place, self.whole, self.split = place, whole, split
        self.w_send, self.w_recv, self.s_send, self.s_recv = w_send, w_recv, s_send, s_recv
        self.x_send, self.x_recv = x_send, x_recv

    def block(self, way, steps):
        return lax.rem(self.place.z - (1 - 2 * way) * steps + Z, Z)

    def w_copy(self, way, step, arriving=False):
        part = self.whole.at[self.block(way, step if arriving else step - 1)]
        if step == 4:
            part = part.at[:, way * WHOLE // 2 : (way + 1) * WHOLE // 2]
        at = (way, step - 1)
        return remote(part, part, self.w_send.at[at], self.w_recv.at[at], self.place.z_next[way])

    def s_copy(self, way, step, arriving=False):
        part = self.split.at[self.block(way, step if arriving else step - 1), self.place.x]
        at = (way, step - 1)
        return remote(part, part, self.s_send.at[at], self.s_recv.at[at], self.place.z_next[way])

    def x_copy(self, way, steps, arriving=False):
        part = self.split.at[self.block(way, steps), 1 - self.place.x if arriving else self.place.x]
        at = steps + 3 * way if steps else 0
        return remote(part, part, self.x_send.at[at], self.x_recv.at[at], self.place.x_other)

    def begin_split(self):
        for way in (0, 1):
            self.s_copy(way, 1).start()
        self.x_copy(0, 0).start()

    def begin_whole(self):
        for way in (0, 1):
            self.w_copy(way, 1).start()

    def step(self, step):
        for way in (0, 1):
            self.s_copy(way, step, True).wait_recv()
            if step < 3 or way == 1:
                self.s_copy(way, step + 1).start()
            self.x_copy(way, step).start()
        for way in (0, 1):
            self.w_copy(way, step, True).wait_recv()
            self.w_copy(way, step + 1).start()

    def last_split(self):
        self.s_copy(1, 4, True).wait_recv()
        self.x_copy(1, 4).start()

    def last_whole(self):
        for way in (0, 1):
            self.w_copy(way, 4, True).wait_recv()

    def crossings(self):
        return [(0, 0)] + [(way, steps) for steps in (1, 2, 3) for way in (0, 1)] + [(1, 4)]

    def wait_pair(self):
        for way, steps in self.crossings():
            self.x_copy(way, steps, True).wait_recv()

    def drain(self, first=1):
        for way in (0, 1):
            for step in range(first, 5):
                self.w_copy(way, step).wait_send()
                if step < 4 or way == 1:
                    self.s_copy(way, step).wait_send()
        for way, steps in self.crossings():
            self.x_copy(way, steps).wait_send()


class Direct:
    def __init__(self, me, device_of, out, into, send, recv):
        self.me, self.device_of, self.out, self.into, self.send, self.recv = me, device_of, out, into, send, recv

    def copy(self, apart):
        peer = lax.rem(self.me + apart, 8)
        return remote(
            self.out(peer), self.into(self.me), self.send.at[apart - 1], self.recv.at[apart - 1], self.device_of(peer)
        )

    def start(self):
        for apart in (4, 3, 5, 2, 6, 1, 7):
            self.copy(apart).start()

    def wait_one(self, apart):
        source = lax.rem(self.me - apart + 8, 8)
        part = self.into(source)
        remote(part, part, self.send.at[apart - 1], self.recv.at[apart - 1], self.device_of(source)).wait_recv()

    def wait(self):
        for apart in (1, 7, 2, 6, 3, 5, 4):
            self.wait_one(apart)

    def drain(self):
        for apart in range(1, 8):
            self.copy(apart).wait_send()


class Total:
    def __init__(self, place, m, zs, x, x_got, r, r_got, m_s, m_r, z_s, z_r, one_s, one_r):
        self.place, self.m, self.zs, self.x, self.x_got, self.r, self.r_got = place, m, zs, x, x_got, r, r_got
        self.m_all = Direct(place.mp, place.of_mp, lambda peer: m.at[place.mp], lambda source: m.at[source], m_s, m_r)
        self.z_all = Direct(place.z, place.of_z, lambda peer: zs.at[place.z], lambda source: zs.at[source], z_s, z_r)
        self.one_s, self.one_r = one_s, one_r

    def x_copy(self):
        return remote(self.x, self.x_got, self.one_s.at[0], self.one_r.at[0], self.place.x_other)

    def r_copy(self):
        return remote(self.r, self.r_got, self.one_s.at[1], self.one_r.at[1], self.place.partner)

    def in_order(self, slots):
        total = slots[0]
        for source in range(1, 8):
            total = total + slots[source]
        return total

    def start(self, tile):
        self.m[self.place.mp] = tile
        self.m_all.start()

    def over_x(self):
        self.m_all.wait()
        self.x[...] = self.in_order(self.m)
        self.x_copy().start()

    def over_z(self):
        self.x_copy().wait_recv()
        self.zs[self.place.z] = self.x[...] + self.x_got[...]
        self.z_all.start()

    def over_role(self):
        self.z_all.wait()
        self.r[...] = self.in_order(self.zs)
        self.r_copy().start()

    def result(self):
        self.r_copy().wait_recv()
        return self.r[...] + self.r_got[...]

    def drain(self):
        self.m_all.drain()
        self.x_copy().wait_send()
        self.z_all.drain()
        self.r_copy().wait_send()


class Place:
    def __init__(self):
        self.role, self.mp, self.dp = lax.axis_index("role"), lax.axis_index("mp"), lax.axis_index("dp")
        dp = self.dp
        self.z, self.x = dp // 2, lax.rem(dp, 2)
        role, mp, z, x = self.role, self.mp, self.z, self.x
        up, down = lax.rem(z + 1, Z) * 2 + x, lax.rem(z + Z - 1, Z) * 2 + x
        self.z_next = ((role, up, mp), (role, down, mp))
        self.z_next_cross = ((1 - role, up, mp), (1 - role, down, mp))
        self.x_other = (role, z * 2 + 1 - x, mp)
        self.partner = (1 - role, dp, mp)
        self.across = (role, mp * 2 + x, z)
        self.of_z = lambda peer: (role, peer * 2 + x, mp)
        self.of_mp = lambda peer: (role, dp, peer)


def exchange_kernel(
    tok_in, w_in, down_in, lin_in,
    tok_out, cot_out, hid_out, err_out, lin_out, stat_out,
    tok, w, down, lin,
    part, b_out, b_into, bx_out, bx_into, pre, hid,
    s_part, s_out, s_into, sx_out, sx_into, s_pre, s_hid,
    d_part, d_out, d_into, err, target_out, target,
    lin_part, e_out, e_into, ex_out, ex_into, lin_err,
    k_out, k_into, kx_out, kx_into, gate_out, cot,
    ks_out, ks_into, ksx_out, ksx_into, s_gate_out, s_cot,
    m1, z1, x1, x1_got, r1, r1_got, m2, z2, x2, x2_got, r2, r2_got, stat,
    load_sem, store_sem,
    tok_s, tok_r, hand_s, hand_r, b_s, b_r, bx_s, bx_r, s_s, s_r, sx_s, sx_r,
    c_s, c_r, cs_s, cs_r, cx_s, cx_r,
    d_s, d_r, one_s, one_r, i_s, i_r, e_s, e_r, k_s, k_r, ks_s, ks_r, ksx_s, ksx_r,
    j_s, j_r, jx_s, jx_r, l_s, l_r, ls_s, ls_r, lx_s, lx_r, g_s, g_r, gn_s,
    m1_s, m1_r, z1_s, z1_r, o1_s, o1_r, m2_s, m2_r, z2_s, z2_r, o2_s, o2_r,
    share_s, share_r,
):
    place = Place()
    role, mp, dp, z, x = place.role, place.mp, place.dp, place.z, place.x
    student, teacher = role == 1, role == 0
    x_of = (1 - x, x)
    halves = (0, 1)

    loads = [
        pltpu.make_async_copy(tok_in.at[:, b * QUARTER : (b + 1) * QUARTER], tok.at[b, mp], load_sem.at[b])
        for b in halves
    ]
    loads += [
        pltpu.make_async_copy(w_in, w, load_sem.at[2]),
        pltpu.make_async_copy(down_in, down, load_sem.at[3]),
    ]
    loads += [
        pltpu.make_async_copy(
            lin_in.at[:, pl.ds(pl.multiple_of(b * 2 * QUARTER + role * QUARTER, QUARTER), QUARTER)],
            lin.at[b],
            load_sem.at[4 + b],
        )
        for b in halves
    ]
    for load in loads:
        load.start()

    barrier = pltpu.get_barrier_semaphore()

    def greet(device):
        pl.semaphore_signal(barrier, inc=1, device_id=device, device_id_type=MESH)

    for apart in range(1, 8):
        greet(place.of_mp(lax.rem(mp + apart, 8)))
        greet((1 - role, dp, lax.rem(mp + apart, 8)))
        greet(place.of_z(lax.rem(z + apart, 8)))
    greet(place.x_other)
    greet(place.partner)
    for way in (0, 1):
        greet(place.z_next_cross[way])

    @pl.when(z != mp)
    def _():
        greet(place.across)
        pl.semaphore_wait(barrier, 26)

    @pl.when(z == mp)
    def _():
        pl.semaphore_wait(barrier, 25)

    for load in loads[:2]:
        load.wait()
    tokens = Direct(mp, place.of_mp, lambda peer: tok.at[role, mp], lambda source: tok.at[role, source], tok_s, tok_r)
    tokens.start()

    def hand(apart, arriving=False):
        source = lax.rem(mp - apart + 8, 8)
        part_of = tok.at[1 - role if arriving else role, source]
        return remote(part_of, part_of, hand_s.at[apart - 1], hand_r.at[apart - 1], place.partner)

    for apart in (1, 7, 2, 6, 3, 5, 4):
        tokens.wait_one(apart)
        hand(apart).start()
    loads[2].wait()
    for apart in (1, 7, 2, 6, 3, 5, 4):
        hand(apart, True).wait_recv()
    stores = [pltpu.make_async_copy(tok, tok_out, store_sem.at[0])]
    stores[0].start()

    def all_tokens():
        return jnp.concatenate([tok[b].reshape(Z * ROWS, QUARTER) for b in halves], axis=1)

    tags = [(0,), (1,)]
    b_sum = RingSum(place, part, b_out, b_into, b_s, b_r, tags, lambda tag: tag[0])
    s_sum = PairRingSum(place, s_part.at[1], s_out, s_into, s_s, s_r, tags, lambda tag: tag[0])
    s_sum.pair(s_part.at[0], sx_out, sx_into, sx_s, sx_r)

    def split_dot(q):
        for g in (0, 1):
            column = pl.multiple_of(g * UNITS + WHOLE + x_of[q] * SPLIT, 128)
            s_part[q, g] = jnp.dot(
                all_tokens(), w[:, pl.ds(column, SPLIT)], preferred_element_type=F32
            ).reshape(Z, ROWS, SPLIT)

    split_dot(0)
    s_sum.exchange()
    for g in (0, 1):
        part[g] = jnp.dot(
            all_tokens(), w[:, g * UNITS : g * UNITS + WHOLE], preferred_element_type=F32
        ).reshape(Z, ROWS, WHOLE)
        b_sum.begin((g,))
    split_dot(1)
    for tag in tags:
        s_sum.begin(tag)
    b_sum.step(2)
    s_sum.step(2)
    for load in loads[3:]:
        load.wait()
    for q in (0, 1):
        lin_part[q] = jnp.dot(all_tokens(), lin[x_of[q]], preferred_element_type=F32).reshape(Z, ROWS, QUARTER)
    for step in (3, 4):
        b_sum.step(step)
        s_sum.step(step)

    def bx_copy(g):
        return remote(bx_out.at[g], bx_into.at[g], bx_s.at[g], bx_r.at[g], place.x_other)

    for g in (0, 1):
        bx_out[g] = b_sum.result((g,)).astype(BF16)
        bx_copy(g).start()

    def hidden(inputs):
        return (inputs[0] * jax.nn.sigmoid(inputs[0]) * inputs[1]).astype(BF16)

    c_all = Gather(place, hid, s_hid, c_s, c_r, cs_s, cs_r, cx_s, cx_r)
    for g in (0, 1):
        s_pre[g] = s_sum.result((g,))
    s_hid[z, x] = hidden(s_pre)
    c_all.begin_split()
    for g in (0, 1):
        bx_copy(g).wait_recv()
        pre[g] = bx_out[g].astype(F32) + bx_into[g].astype(F32)
    hid[z] = hidden(pre)
    c_all.begin_whole()
    e_sum = RingSum(place, lin_part, e_out, e_into, e_s, e_r, [(0,), (1,)], lambda tag: tag[0])
    for step in (1, 2, 3):
        c_all.step(step)
    for tag in e_sum.tags:
        e_sum.begin(tag)

    c_all.last_split()
    c_all.last_whole()
    d_part[...] = jnp.dot(hid[...].reshape(Z * ROWS, WHOLE), down[:WHOLE], preferred_element_type=F32)
    c_all.wait_pair()

    def d_copy(b, apart):
        peer = lax.rem(mp + apart, 8)
        return remote(
            d_out.at[b, peer], d_into.at[role, mp], d_s.at[b, apart - 1], d_r.at[role, apart - 1], (b, dp, peer)
        )

    def d_arrival(source_role, apart):
        source = lax.rem(mp - apart + 8, 8)
        got = d_into.at[source_role, source]
        return remote(got, got, d_s.at[0, apart - 1], d_r.at[source_role, apart - 1], (source_role, dp, source))

    def d_partner(arriving=False):
        return remote(
            d_out.at[1 - role, mp],
            d_into.at[1 - role if arriving else role, mp],
            one_s.at[0],
            one_r.at[0],
            place.partner,
        )

    for b in halves:
        columns = slice(b * QUARTER, (b + 1) * QUARTER)
        total = d_part[:, columns] + jnp.dot(
            jnp.concatenate([s_hid[:, c].reshape(Z * ROWS, SPLIT) for c in halves], axis=1),
            down[WHOLE:, columns],
            preferred_element_type=F32,
        )
        d_out[b] = total.reshape(Z, ROWS, QUARTER).astype(BF16)
        for apart in (4, 3, 5, 2, 6, 1, 7):
            d_copy(b, apart).start()
    d_partner().start()
    d_into[role, mp] = d_out[role, mp]
    e_sum.step(2)
    for apart in (1, 7, 2, 6, 3, 5, 4):
        for source_role in (0, 1):
            d_arrival(source_role, apart).wait_recv()
    d_partner(True).wait_recv()

    def summed(source_role):
        own = d_into[source_role, 0].astype(F32)
        for source in range(1, 8):
            own = own + d_into[source_role, source].astype(F32)
        return own.astype(BF16)

    teacher_rows = summed(0)
    error = summed(1).astype(F32) - teacher_rows.astype(F32)
    err[role, mp] = error.astype(BF16)

    def err_copy(apart):
        peer = lax.rem(mp + apart, 8)
        return remote(
            err.at[role, mp], err.at[role, mp], i_s.at[apart - 1], i_r.at[role, apart - 1], (1, dp, peer)
        )

    def err_arrival(source_role, apart):
        source = lax.rem(mp - apart + 8, 8)
        got = err.at[source_role, source]
        return remote(got, got, i_s.at[apart - 1], i_r.at[source_role, apart - 1], (source_role, dp, source))

    def err_partner():
        return remote(err.at[0, mp], err.at[0, mp], one_s.at[1], one_r.at[1], place.partner)

    for apart in (4, 3, 5, 2, 6, 1, 7):
        err_copy(apart).start()

    @pl.when(teacher)
    def _():
        err_partner().start()

    target_out[...] = teacher_rows

    def target_copy():
        return remote(target_out, target, one_s.at[2], one_r.at[2], place.across)

    @pl.when(z != mp)
    def _():
        target_copy().start()

    @pl.when(z == mp)
    def _():
        target[...] = target_out[...]

    row = lax.broadcasted_iota(jnp.int32, (8, 128), 0)
    teacher_float = teacher_rows.astype(F32)
    target_square = jnp.sum(teacher_float * teacher_float)
    error_square = jnp.sum(error * error)
    norm = Total(place, m1, z1, x1, x1_got, r1, r1_got, m1_s, m1_r, z1_s, z1_r, o1_s, o1_r)
    norm.start(jnp.where(row == 0, target_square, jnp.where(row == 1, error_square, 0.0)))
    e_sum.step(3)

    k_sum = RingSum(place, part.at[0], k_out, k_into, k_s, k_r, [()], lambda tag: 0)
    ks_sum = PairRingSum(place, s_part.at[1, 0], ks_out, ks_into, ks_s, ks_r, [()], lambda tag: 1)
    ks_sum.pair(s_part.at[0, 0], ksx_out, ksx_into, ksx_s, ksx_r)

    def err_share():
        return remote(err, err_out, share_s.at[2], share_r.at[2], place.partner)

    def err_store():
        return pltpu.make_async_copy(err, err_out, store_sem.at[3])

    def parts_of(whole, split, out):
        yield whole, out.at[:, :, :WHOLE]
        for b in halves:
            yield split.at[:, b], out.at[:, :, WHOLE + b * SPLIT : WHOLE + (b + 1) * SPLIT]

    def hid_shares():
        return [
            remote(here, there, share_s.at[5 + i], share_r.at[5 + i], place.partner)
            for i, (here, there) in enumerate(parts_of(hid, s_hid, hid_out))
        ]

    def hid_stores():
        return [
            pltpu.make_async_copy(here, there, store_sem.at[7 + i])
            for i, (here, there) in enumerate(parts_of(hid, s_hid, hid_out))
        ]

    def cot_dot(start, size):
        return lax.dot_general(
            jnp.concatenate([err[b].reshape(Z * ROWS, QUARTER) for b in halves], axis=1),
            down[pl.ds(start, size)],
            (((1,), (1,)), ((), ())),
            preferred_element_type=F32,
        ).reshape(Z, ROWS, size)

    @pl.when(student)
    def _():
        for apart in (1, 7, 2, 6, 3, 5, 4):
            for source_role in (0, 1):
                err_arrival(source_role, apart).wait_recv()
        err_partner().wait_recv()
        s_part[0, 0] = cot_dot(pl.multiple_of(WHOLE + x_of[0] * SPLIT, 128), SPLIT)
        ks_sum.exchange()
        part[0] = cot_dot(0, WHOLE)
        k_sum.begin(())
        s_part[1, 0] = cot_dot(pl.multiple_of(WHOLE + x_of[1] * SPLIT, 128), SPLIT)
        ks_sum.begin(())
        err_share().start()
        err_store().start()
        for copy in hid_shares() + hid_stores():
            copy.start()

    norm.over_x()
    e_sum.step(4)
    norm.over_z()

    @pl.when(student)
    def _():
        k_sum.step(2)
        ks_sum.step(2)

    def ex_copy():
        return remote(ex_out, ex_into, one_s.at[3], one_r.at[3], place.x_other)

    ex_out[...] = e_sum.result((0,)).astype(BF16)
    ex_copy().start()
    linear_rows = e_sum.result((1,))
    norm.over_role()

    @pl.when(student)
    def _():
        k_sum.step(3)
        ks_sum.step(3)

    ex_copy().wait_recv()

    @pl.when(z != mp)
    def _():
        target_copy().wait_recv()

    linear_error = linear_rows + ex_into[...].astype(F32) - target[...].astype(F32)
    lin_err[z, x] = linear_error.astype(BF16)
    j_all = RingGather(place, lin_err, j_s, j_r, jx_s.at[0], jx_r.at[0])
    j_all.begin()
    loss = Total(place, m2, z2, x2, x2_got, r2, r2_got, m2_s, m2_r, z2_s, z2_r, o2_s, o2_r)
    loss.start(jnp.where(row == 2, jnp.sum(linear_error * linear_error), 0.0))

    @pl.when(student)
    def _():
        k_sum.step(4)
        ks_sum.step(4)

    stat[...] = norm.result()
    j_all.begin_other()

    def kx_copy():
        return remote(kx_out, kx_into, bx_s.at[2], bx_r.at[2], place.x_other)

    def gate_copies():
        return [
            remote(s_gate_out, s_cot.at[z, x], g_s.at[0], g_r.at[0], place.partner),
            remote(gate_out, cot.at[z], g_s.at[1], g_r.at[1], place.partner),
        ]

    l_all = Gather(place, cot, s_cot, l_s, l_r, ls_s, ls_r, lx_s, lx_r)

    def gate_next(way):
        return [
            remote(s_gate_out, s_cot.at[z, x], gn_s.at[way, 0], ls_r.at[way, 0], place.z_next_cross[way]),
            remote(gate_out, cot.at[z], gn_s.at[way, 1], l_r.at[way, 0], place.z_next_cross[way]),
        ]

    def cotangents(total, inputs):
        factor = (16.0 * MODEL) / stat[0:1, 0:1]
        hidden_cot = total * factor
        gate_pre, up_pre = inputs[0], inputs[1]
        sig = jax.nn.sigmoid(gate_pre)
        gate_cot = hidden_cot * up_pre * sig * (1.0 + gate_pre * (1.0 - sig))
        return gate_cot.astype(BF16), (hidden_cot * gate_pre * sig).astype(BF16)

    @pl.when(student)
    def _():
        kx_out[...] = k_sum.result(()).astype(BF16)
        kx_copy().start()
        s_gate_out[...], s_cot[z, x] = cotangents(ks_sum.result(()), s_pre)
        for way in (0, 1):
            gate_next(way)[0].start()
        gate_copies()[0].start()
        l_all.begin_split()
        kx_copy().wait_recv()
        gate_out[...], cot[z] = cotangents(kx_out[...].astype(F32) + kx_into[...].astype(F32), pre)
        for way in (0, 1):
            gate_next(way)[1].start()
        l_all.begin_whole()
        gate_copies()[1].start()

    j_all.step(1)

    @pl.when(teacher)
    def _():
        gate_copies()[0].wait_recv()
        l_all.x_copy(0, 0).start()

    tokens.drain()
    for apart in range(1, 8):
        hand(apart).wait_send()
        for b in halves:
            d_copy(b, apart).wait_send()
    b_sum.drain()
    s_sum.drain()
    for g in (0, 1):
        bx_copy(g).wait_send()
    l_all.step(1)
    loss.over_x()
    j_all.step(2)
    c_all.drain()
    e_sum.drain()
    loss.over_z()
    l_all.step(2)
    j_all.step(3)
    loss.over_role()
    d_partner().wait_send()
    for apart in range(1, 8):
        err_copy(apart).wait_send()
    ex_copy().wait_send()
    norm.drain()
    stat[...] = stat[...] + loss.result()
    stores.append(pltpu.make_async_copy(stat, stat_out, store_sem.at[4]))
    stores[-1].start()
    l_all.step(3)
    j_all.last()

    def lin_columns(b):
        start = pl.multiple_of(b * 2 * QUARTER + role * QUARTER, QUARTER)
        return lin_out.at[:, :, pl.ds(start, QUARTER)]

    def lin_share(b):
        return remote(lin_err.at[:, b], lin_columns(b), share_s.at[3 + b], share_r.at[3 + b], place.partner)

    def lin_arrival(b):
        start = pl.multiple_of(b * 2 * QUARTER + (1 - role) * QUARTER, QUARTER)
        got = lin_out.at[:, :, pl.ds(start, QUARTER)]
        return remote(lin_err.at[:, b], got, share_s.at[3 + b], share_r.at[3 + b], place.partner)

    for b in halves:
        lin_share(b).start()
        stores.append(pltpu.make_async_copy(lin_err.at[:, b], lin_columns(b), store_sem.at[5 + b]))
        stores[-1].start()

    @pl.when(teacher)
    def _():
        gate_copies()[1].wait_recv()

    l_all.last_split()
    l_all.last_whole()
    l_all.wait_pair()
    for i, (here, there) in enumerate(parts_of(cot, s_cot, cot_out)):
        stores.append(pltpu.make_async_copy(here, there, store_sem.at[10 + i]))
        stores[-1].start()

    loss.drain()
    j_all.drain()
    for b in halves:
        lin_share(b).wait_send()

    @pl.when(z != mp)
    def _():
        target_copy().wait_send()

    @pl.when(student)
    def _():
        k_sum.drain()
        ks_sum.drain()
        l_all.drain()
        err_share().wait_send()
        err_store().wait()
        kx_copy().wait_send()
        for copy in gate_copies() + gate_next(0) + gate_next(1) + hid_shares():
            copy.wait_send()
        for copy in hid_stores():
            copy.wait()

    @pl.when(teacher)
    def _():
        l_all.drain(2)
        err_partner().wait_send()
        err_share().wait_recv()
        for copy in hid_shares():
            copy.wait_recv()

    for b in halves:
        lin_arrival(b).wait_recv()
    for store in stores:
        store.wait()


def exchange(tokens, w, down, linear):
    def vmem(*shape, dtype=BF16):
        return pltpu.VMEM(shape, dtype)

    def sems(*shape):
        return pltpu.SemaphoreType.DMA(shape)

    def array(*shape, dtype=BF16):
        return jax.ShapeDtypeStruct(shape, dtype)

    def total_tiles():
        return [vmem(8, 8, 128, dtype=F32)] * 2 + [vmem(8, 128, dtype=F32)] * 4

    anywhere = pl.BlockSpec(memory_space=pl.ANY)
    return pl.pallas_call(
        exchange_kernel,
        out_shape=[
            array(2, Z, ROWS, QUARTER),
            array(Z, ROWS, UNITS),
            array(Z, ROWS, UNITS),
            array(2, Z, ROWS, QUARTER),
            array(Z, ROWS, LIN),
            array(8, 128, dtype=F32),
        ],
        in_specs=[anywhere] * 4,
        out_specs=[anywhere] * 6,
        scratch_shapes=[
            vmem(2, Z, ROWS, QUARTER), vmem(WIDTH, 2 * UNITS), vmem(UNITS, WIDTH), vmem(2, WIDTH, QUARTER),
            vmem(2, Z, ROWS, WHOLE, dtype=F32), vmem(2, 4, 2, ROWS, WHOLE), vmem(2, 4, 2, ROWS, WHOLE),
            vmem(2, ROWS, WHOLE), vmem(2, ROWS, WHOLE), vmem(2, ROWS, WHOLE, dtype=F32), vmem(Z, ROWS, WHOLE),
            vmem(2, 2, Z, ROWS, SPLIT, dtype=F32), vmem(2, 4, 2, ROWS, SPLIT), vmem(2, 4, 2, ROWS, SPLIT),
            vmem(Z, 2, ROWS, SPLIT), vmem(Z, 2, ROWS, SPLIT), vmem(2, ROWS, SPLIT, dtype=F32), vmem(Z, 2, ROWS, SPLIT),
            vmem(Z * ROWS, WIDTH, dtype=F32), vmem(2, 8, ROWS, QUARTER), vmem(2, 8, ROWS, QUARTER),
            vmem(2, 8, ROWS, QUARTER), vmem(ROWS, QUARTER), vmem(ROWS, QUARTER),
            vmem(2, Z, ROWS, QUARTER, dtype=F32), vmem(2, 4, 2, ROWS, QUARTER), vmem(2, 4, 2, ROWS, QUARTER),
            vmem(ROWS, QUARTER), vmem(ROWS, QUARTER), vmem(Z, 2, ROWS, QUARTER),
            vmem(2, 4, ROWS, WHOLE), vmem(2, 4, ROWS, WHOLE), vmem(ROWS, WHOLE), vmem(ROWS, WHOLE),
            vmem(ROWS, WHOLE), vmem(Z, ROWS, WHOLE),
            vmem(2, 4, ROWS, SPLIT), vmem(2, 4, ROWS, SPLIT), vmem(Z, ROWS, SPLIT), vmem(Z, ROWS, SPLIT),
            vmem(ROWS, SPLIT), vmem(Z, 2, ROWS, SPLIT),
            *total_tiles(), *total_tiles(), vmem(8, 128, dtype=F32),
            sems(6), sems(13),
            sems(7), sems(7), sems(7), sems(7), sems(2, 4, 2), sems(2, 4, 2), sems(3), sems(3),
            sems(2, 4, 2), sems(2, 4, 2), sems(8), sems(8),
            sems(2, 4), sems(2, 4), sems(2, 4), sems(2, 4), sems(8), sems(8),
            sems(2, 7), sems(2, 7), sems(4), sems(4), sems(7), sems(2, 7), sems(2, 4, 2), sems(2, 4, 2),
            sems(2, 4), sems(2, 4), sems(2, 4), sems(2, 4), sems(8), sems(8),
            sems(2, 4, 2), sems(2, 4, 2), sems(1), sems(1),
            sems(2, 4), sems(2, 4), sems(2, 4), sems(2, 4), sems(8), sems(8), sems(2), sems(2), sems(2, 2),
            sems(7), sems(7), sems(7), sems(7), sems(2), sems(2),
            sems(7), sems(7), sems(7), sems(7), sems(2), sems(2),
            sems(8), sems(8),
        ],
        compiler_params=pltpu.CompilerParams(
            collective_id=0, has_side_effects=True, vmem_limit_bytes=34 * 1024 * 1024
        ),
        name="exchange",
    )(tokens, w, down, linear)


def contract_rows(left, right):
    return lax.dot_general(left, right, (((0,), (0,)), ((), ())), preferred_element_type=F32)


BLOCK = 256


def gradients_kernel(tok, cot, hid, err, lin_err, stat, unit_grad, down_grad, linear_grad, losses, turned):
    step = pl.program_id(0)
    factor = (16.0 * MODEL) / stat[0:1, 0:1]

    @pl.when(step == 0)
    def _():
        for b in (0, 1):
            turned[b * QUARTER : (b + 1) * QUARTER] = tok[b].T
        share = stat[...] / stat[0:1, 0:1]
        losses[0] = share[1, 0]
        losses[1] = share[2, 0]

    unit_grad[...] = jnp.dot(turned[...], cot[...], preferred_element_type=F32).astype(BF16)
    for b in (0, 1):
        down_grad[:, b * QUARTER : (b + 1) * QUARTER] = (factor * contract_rows(hid[...], err[b])).astype(BF16)

    @pl.when(step < LIN // BLOCK)
    def _():
        linear_grad[...] = (factor * jnp.dot(turned[...], lin_err[...], preferred_element_type=F32)).astype(BF16)


def gradients(tok, cot, hid, err, lin_err, stat):
    tokens = Z * ROWS
    last = LIN // BLOCK - 1
    halves = pl.BlockSpec((2, tokens, QUARTER), lambda i: (0, 0, 0))
    return pl.pallas_call(
        gradients_kernel,
        grid=(UNITS // BLOCK,),
        out_shape=[
            jax.ShapeDtypeStruct((WIDTH, UNITS), BF16),
            jax.ShapeDtypeStruct((UNITS, WIDTH), BF16),
            jax.ShapeDtypeStruct((WIDTH, LIN), BF16),
            jax.ShapeDtypeStruct((2,), F32),
        ],
        in_specs=[
            halves,
            pl.BlockSpec((tokens, BLOCK), lambda i: (0, i)),
            pl.BlockSpec((tokens, BLOCK), lambda i: (0, i)),
            halves,
            pl.BlockSpec((tokens, BLOCK), lambda i: (0, jnp.minimum(i, last))),
            pl.BlockSpec((8, 128), lambda i: (0, 0)),
        ],
        out_specs=[
            pl.BlockSpec((WIDTH, BLOCK), lambda i: (0, i)),
            pl.BlockSpec((BLOCK, WIDTH), lambda i: (i, 0)),
            pl.BlockSpec((WIDTH, BLOCK), lambda i: (0, jnp.minimum(i, last))),
            pl.BlockSpec(memory_space=pltpu.SMEM),
        ],
        scratch_shapes=[pltpu.VMEM((WIDTH, tokens), BF16)],
        compiler_params=pltpu.CompilerParams(vmem_limit_bytes=16 * 1024 * 1024),
        name="gradients",
    )(tok, cot, hid, err, lin_err, stat)


def body(tokens, gate_up, down, linear):
    w = gate_up.reshape(WIDTH, 2 * UNITS)
    tok, cot, hid, err, lin_err, stat = exchange(tokens, w, down[0], linear)
    rows = Z * ROWS
    unit_grad, down_grad, linear_grad, losses = gradients(
        tok.reshape(2, rows, QUARTER),
        cot.reshape(rows, UNITS),
        hid.reshape(rows, UNITS),
        err.reshape(2, rows, QUARTER),
        lin_err.reshape(rows, LIN),
        stat,
    )
    return (unit_grad[None], down_grad, linear_grad, losses)


def solution(mesh):
    return jax.shard_map(
        body,
        mesh=mesh,
        in_specs=(P("mp", "dp"), P("role", "dp", None, "mp"), P("role", "mp", "dp"), P("dp", "mp")),
        out_specs=(P("role", "dp", "mp"), P("mp", "dp"), P("dp", "mp"), P()),
        check_vma=False,
    )
```

```python
import jax
import jax.numpy as jnp
from jax import lax
from jax.experimental import pallas as pl
from jax.experimental.pallas import tpu as pltpu
from jax.sharding import PartitionSpec as P

MESH = pl.DeviceIdType.MESH
BF16, F32 = jnp.bfloat16, jnp.float32
MODEL = 8192
Z = 8
ROWS = 48
WIDTH = 512
UNITS = 1792
WHOLE = 768
SPLIT = 512
LIN = 1024
QUARTER = LIN // 4


def remote(src, dst, send, recv, device):
    return pltpu.make_async_remote_copy(
        src_ref=src, dst_ref=dst, send_sem=send, recv_sem=recv, device_id=device, device_id_type=MESH
    )


class RingSum:
    def __init__(self, place, part, out, into, send, recv, tags, long_way):
        self.place, self.part, self.out, self.into = place, part, out, into
        self.send, self.recv, self.tags, self.long_way = send, recv, tags, long_way

    def copy(self, way, step, tag):
        at = (way, step - 1) + tag
        return remote(
            self.out.at[at], self.into.at[at], self.send.at[at], self.recv.at[at], self.place.z_next[way]
        )

    def push(self, way, step, tag, first):
        sign = 1 - 2 * way
        total = self.local(tag, sign * (5 - step))
        if not first:
            self.copy(way, step - 1, tag).wait_recv()
            total = total + self.into[(way, step - 2) + tag].astype(F32)
        self.out[(way, step - 1) + tag] = total.astype(BF16)
        self.copy(way, step, tag).start()

    def local(self, tag, offset):
        return self.part[tag + (lax.rem(self.place.z + offset + Z, Z),)]

    def begin(self, tag):
        far = self.long_way(tag)
        self.push(far, 1, tag, True)
        self.push(1 - far, 2, tag, True)

    def step(self, step, tags=None):
        for tag in tags or self.tags:
            for way in (0, 1):
                if step > 2 or way == self.long_way(tag):
                    self.push(way, step, tag, False)

    def result(self, tag):
        total = self.local(tag, 0)
        for way in (0, 1):
            self.copy(way, 4, tag).wait_recv()
            total = total + self.into[(way, 3) + tag].astype(F32)
        return total

    def drain(self):
        for tag in self.tags:
            for way in (0, 1):
                for step in range(1 if way == self.long_way(tag) else 2, 5):
                    self.copy(way, step, tag).wait_send()


class RingGather:
    def __init__(self, place, buf, send, recv, x_send, x_recv):
        self.place, self.buf, self.send, self.recv = place, buf, send, recv
        self.x_send, self.x_recv = x_send, x_recv

    def copy(self, way, step, mine, arriving=False):
        place = self.place
        sign = 1 - 2 * way
        block = lax.rem(place.z - sign * (step if arriving else step - 1) + Z, Z)
        x = place.x if mine else 1 - place.x
        part = self.buf.at[block, x]
        at = (way, step - 1, mine)
        return remote(part, part, self.send.at[at], self.recv.at[at], place.z_next[way])

    def x_copy(self, arriving=False):
        place = self.place
        part = self.buf.at[place.z, 1 - place.x if arriving else place.x]
        return remote(part, part, self.x_send, self.x_recv, place.x_other)

    def begin(self):
        self.copy(0, 1, 1).start()
        self.copy(1, 1, 1).start()
        self.x_copy().start()

    def begin_other(self):
        self.x_copy(True).wait_recv()
        self.copy(0, 1, 0).start()
        self.copy(1, 1, 0).start()

    def step(self, step):
        for mine in (1, 0):
            for way in (0, 1):
                self.copy(way, step, mine, True).wait_recv()
                if step < 3 or way == 1 - mine:
                    self.copy(way, step + 1, mine).start()

    def last(self):
        for mine in (1, 0):
            self.copy(1 - mine, 4, mine, True).wait_recv()

    def drain(self):
        self.x_copy().wait_send()
        for mine in (1, 0):
            for way in (0, 1):
                for step in range(1, 5 if way == 1 - mine else 4):
                    self.copy(way, step, mine).wait_send()


class PairRingSum(RingSum):
    def pair(self, other, x_out, x_into, x_send, x_recv):
        self.other, self.x_out, self.x_into, self.x_send, self.x_recv = other, x_out, x_into, x_send, x_recv
        self.got = set()

    def block(self, offset):
        return lax.rem(self.place.z + offset, Z)

    def x_copy(self, offset):
        block = self.block(offset)
        return remote(
            self.x_out.at[block], self.x_into.at[block], self.x_send.at[offset], self.x_recv.at[offset], self.place.x_other
        )

    def exchange(self, offsets):
        for offset in offsets:
            block = self.block(offset)
            for tag in self.tags:
                self.x_out[(block,) + tag] = self.other[tag + (block,)].astype(BF16)
            self.x_copy(offset).start()

    def local(self, tag, offset):
        offset = offset % Z
        if offset not in self.got:
            self.got.add(offset)
            self.x_copy(offset).wait_recv()
        block = self.block(offset)
        return self.part[tag + (block,)] + self.x_into[(block,) + tag].astype(F32)

    def drain(self):
        super().drain()
        for offset in range(Z):
            self.x_copy(offset).wait_send()


class Gather:
    def __init__(self, place, whole, split, w_send, w_recv, s_send, s_recv, x_send, x_recv):
        self.place, self.whole, self.split = place, whole, split
        self.w_send, self.w_recv, self.s_send, self.s_recv = w_send, w_recv, s_send, s_recv
        self.x_send, self.x_recv = x_send, x_recv

    def block(self, way, steps):
        return lax.rem(self.place.z - (1 - 2 * way) * steps + Z, Z)

    def w_copy(self, way, step, arriving=False):
        part = self.whole.at[self.block(way, step if arriving else step - 1)]
        if step == 4:
            part = part.at[:, way * WHOLE // 2 : (way + 1) * WHOLE // 2]
        at = (way, step - 1)
        return remote(part, part, self.w_send.at[at], self.w_recv.at[at], self.place.z_next[way])

    def s_copy(self, way, step, arriving=False):
        part = self.split.at[self.block(way, step if arriving else step - 1), self.place.x]
        at = (way, step - 1)
        return remote(part, part, self.s_send.at[at], self.s_recv.at[at], self.place.z_next[way])

    def x_copy(self, way, steps, arriving=False):
        part = self.split.at[self.block(way, steps), 1 - self.place.x if arriving else self.place.x]
        at = steps + 3 * way if steps else 0
        return remote(part, part, self.x_send.at[at], self.x_recv.at[at], self.place.x_other)

    def begin_split(self):
        for way in (0, 1):
            self.s_copy(way, 1).start()
        self.x_copy(0, 0).start()

    def begin_whole(self):
        for way in (0, 1):
            self.w_copy(way, 1).start()

    def step(self, step):
        for way in (0, 1):
            self.s_copy(way, step, True).wait_recv()
            if step < 3 or way == 1:
                self.s_copy(way, step + 1).start()
            self.x_copy(way, step).start()
        for way in (0, 1):
            self.w_copy(way, step, True).wait_recv()
            self.w_copy(way, step + 1).start()

    def last_split(self):
        self.s_copy(1, 4, True).wait_recv()
        self.x_copy(1, 4).start()

    def last_whole(self):
        for way in (0, 1):
            self.w_copy(way, 4, True).wait_recv()

    def crossings(self):
        return [(0, 0)] + [(way, steps) for steps in (1, 2, 3) for way in (0, 1)] + [(1, 4)]

    def wait_pair(self):
        for way, steps in self.crossings():
            self.x_copy(way, steps, True).wait_recv()

    def drain(self, first=1):
        for way in (0, 1):
            for step in range(first, 5):
                self.w_copy(way, step).wait_send()
                if step < 4 or way == 1:
                    self.s_copy(way, step).wait_send()
        for way, steps in self.crossings():
            self.x_copy(way, steps).wait_send()


class Direct:
    def __init__(self, me, device_of, out, into, send, recv):
        self.me, self.device_of, self.out, self.into, self.send, self.recv = me, device_of, out, into, send, recv

    def copy(self, apart):
        peer = lax.rem(self.me + apart, 8)
        return remote(
            self.out(peer), self.into(self.me), self.send.at[apart - 1], self.recv.at[apart - 1], self.device_of(peer)
        )

    def start(self):
        for apart in (4, 3, 5, 2, 6, 1, 7):
            self.copy(apart).start()

    def wait_one(self, apart):
        source = lax.rem(self.me - apart + 8, 8)
        part = self.into(source)
        remote(part, part, self.send.at[apart - 1], self.recv.at[apart - 1], self.device_of(source)).wait_recv()

    def wait(self):
        for apart in (1, 7, 2, 6, 3, 5, 4):
            self.wait_one(apart)

    def drain(self):
        for apart in range(1, 8):
            self.copy(apart).wait_send()


class Total:
    def __init__(self, place, m, zs, x, x_got, r, r_got, m_s, m_r, z_s, z_r, one_s, one_r):
        self.place, self.m, self.zs, self.x, self.x_got, self.r, self.r_got = place, m, zs, x, x_got, r, r_got
        self.m_all = Direct(place.mp, place.of_mp, lambda peer: m.at[place.mp], lambda source: m.at[source], m_s, m_r)
        self.z_all = Direct(place.z, place.of_z, lambda peer: zs.at[place.z], lambda source: zs.at[source], z_s, z_r)
        self.one_s, self.one_r = one_s, one_r

    def x_copy(self):
        return remote(self.x, self.x_got, self.one_s.at[0], self.one_r.at[0], self.place.x_other)

    def r_copy(self):
        return remote(self.r, self.r_got, self.one_s.at[1], self.one_r.at[1], self.place.partner)

    def in_order(self, slots):
        total = slots[0]
        for source in range(1, 8):
            total = total + slots[source]
        return total

    def start(self, tile):
        self.m[self.place.mp] = tile
        self.m_all.start()

    def over_x(self):
        self.m_all.wait()
        self.x[...] = self.in_order(self.m)
        self.x_copy().start()

    def over_z(self):
        self.x_copy().wait_recv()
        self.zs[self.place.z] = self.x[...] + self.x_got[...]
        self.z_all.start()

    def over_role(self):
        self.z_all.wait()
        self.r[...] = self.in_order(self.zs)
        self.r_copy().start()

    def result(self):
        self.r_copy().wait_recv()
        return self.r[...] + self.r_got[...]

    def drain(self):
        self.m_all.drain()
        self.x_copy().wait_send()
        self.z_all.drain()
        self.r_copy().wait_send()


class Place:
    def __init__(self):
        self.role, self.mp, self.dp = lax.axis_index("role"), lax.axis_index("mp"), lax.axis_index("dp")
        dp = self.dp
        self.z, self.x = dp // 2, lax.rem(dp, 2)
        role, mp, z, x = self.role, self.mp, self.z, self.x
        up, down = lax.rem(z + 1, Z) * 2 + x, lax.rem(z + Z - 1, Z) * 2 + x
        self.z_next = ((role, up, mp), (role, down, mp))
        self.z_next_cross = ((1 - role, up, mp), (1 - role, down, mp))
        self.x_other = (role, z * 2 + 1 - x, mp)
        self.partner = (1 - role, dp, mp)
        self.across = (role, mp * 2 + x, z)
        self.of_z = lambda peer: (role, peer * 2 + x, mp)
        self.of_mp = lambda peer: (role, dp, peer)


def exchange_kernel(
    tok_in, w_in, down_in, lin_in,
    tok_out, cot_out, hid_out, err_out, lin_out, stat_out,
    tok, w, down, lin,
    part, b_out, b_into, bx_out, bx_into, pre, hid,
    s_part, s_out, s_into, sx_out, sx_into, s_pre, s_hid,
    d_part, d_out, d_into, err, target_out, target,
    lin_part, e_out, e_into, ex_out, ex_into, lin_err,
    k_out, k_into, kx_out, kx_into, gate_out, cot,
    ks_out, ks_into, ksx_out, ksx_into, s_gate_out, s_cot,
    m1, z1, x1, x1_got, r1, r1_got, m2, z2, x2, x2_got, r2, r2_got, stat,
    load_sem, store_sem,
    tok_s, tok_r, hand_s, hand_r, b_s, b_r, bx_s, bx_r, s_s, s_r, sx_s, sx_r,
    c_s, c_r, cs_s, cs_r, cx_s, cx_r,
    d_s, d_r, one_s, one_r, i_s, i_r, e_s, e_r, k_s, k_r, ks_s, ks_r, ksx_s, ksx_r,
    j_s, j_r, jx_s, jx_r, l_s, l_r, ls_s, ls_r, lx_s, lx_r, g_s, g_r, gn_s,
    m1_s, m1_r, z1_s, z1_r, o1_s, o1_r, m2_s, m2_r, z2_s, z2_r, o2_s, o2_r,
    share_s, share_r,
):
    place = Place()
    role, mp, dp, z, x = place.role, place.mp, place.dp, place.z, place.x
    student, teacher = role == 1, role == 0
    x_of = (1 - x, x)
    halves = (0, 1)

    loads = [
        pltpu.make_async_copy(tok_in.at[:, b * QUARTER : (b + 1) * QUARTER], tok.at[b, mp], load_sem.at[b])
        for b in halves
    ]
    loads += [
        pltpu.make_async_copy(w_in, w, load_sem.at[2]),
        pltpu.make_async_copy(down_in, down, load_sem.at[3]),
    ]
    loads += [
        pltpu.make_async_copy(
            lin_in.at[:, pl.ds(pl.multiple_of(b * 2 * QUARTER + role * QUARTER, QUARTER), QUARTER)],
            lin.at[b],
            load_sem.at[4 + b],
        )
        for b in halves
    ]
    for load in loads:
        load.start()

    barrier = pltpu.get_barrier_semaphore()

    def greet(device):
        pl.semaphore_signal(barrier, inc=1, device_id=device, device_id_type=MESH)

    for apart in range(1, 8):
        greet(place.of_mp(lax.rem(mp + apart, 8)))
        greet((1 - role, dp, lax.rem(mp + apart, 8)))
        greet(place.of_z(lax.rem(z + apart, 8)))
    greet(place.x_other)
    greet(place.partner)
    for way in (0, 1):
        greet(place.z_next_cross[way])

    @pl.when(z != mp)
    def _():
        greet(place.across)
        pl.semaphore_wait(barrier, 26)

    @pl.when(z == mp)
    def _():
        pl.semaphore_wait(barrier, 25)

    for load in loads[:2]:
        load.wait()
    tokens = Direct(mp, place.of_mp, lambda peer: tok.at[role, mp], lambda source: tok.at[role, source], tok_s, tok_r)
    tokens.start()

    def hand(apart, arriving=False):
        source = lax.rem(mp - apart + 8, 8)
        part_of = tok.at[1 - role if arriving else role, source]
        return remote(part_of, part_of, hand_s.at[apart - 1], hand_r.at[apart - 1], place.partner)

    for apart in (1, 7, 2, 6, 3, 5, 4):
        tokens.wait_one(apart)
        hand(apart).start()
    loads[2].wait()
    for apart in (1, 7, 2, 6, 3, 5, 4):
        hand(apart, True).wait_recv()
    stores = [pltpu.make_async_copy(tok, tok_out, store_sem.at[0])]
    stores[0].start()

    def all_tokens():
        return jnp.concatenate([tok[b].reshape(Z * ROWS, QUARTER) for b in halves], axis=1)

    tags = [(0,), (1,)]
    b_sum = RingSum(place, part, b_out, b_into, b_s, b_r, tags, lambda tag: tag[0])
    s_sum = PairRingSum(place, s_part.at[1], s_out, s_into, s_s, s_r, tags, lambda tag: tag[0])
    s_sum.pair(s_part.at[0], sx_out, sx_into, sx_s, sx_r)

    def split_dot(q):
        for g in (0, 1):
            column = pl.multiple_of(g * UNITS + WHOLE + x_of[q] * SPLIT, 128)
            s_part[q, g] = jnp.dot(
                all_tokens(), w[:, pl.ds(column, SPLIT)], preferred_element_type=F32
            ).reshape(Z, ROWS, SPLIT)

    split_dot(0)
    s_sum.exchange((4, 3, 5))
    for g in (0, 1):
        part[g] = jnp.dot(
            all_tokens(), w[:, g * UNITS : g * UNITS + WHOLE], preferred_element_type=F32
        ).reshape(Z, ROWS, WHOLE)
        b_sum.begin((g,))
    split_dot(1)
    b_sum.step(2)
    s_sum.exchange((2, 6, 1, 7, 0))
    for tag in tags:
        s_sum.begin(tag)
    for load in loads[3:]:
        load.wait()
    for q in (0, 1):
        lin_part[q] = jnp.dot(all_tokens(), lin[x_of[q]], preferred_element_type=F32).reshape(Z, ROWS, QUARTER)
    b_sum.step(3)
    s_sum.step(2)
    b_sum.step(4)
    s_sum.step(3)

    def bx_copy(g):
        return remote(bx_out.at[g], bx_into.at[g], bx_s.at[g], bx_r.at[g], place.x_other)

    for g in (0, 1):
        bx_out[g] = b_sum.result((g,)).astype(BF16)
        bx_copy(g).start()
    s_sum.step(4)

    def hidden(inputs):
        return (inputs[0] * jax.nn.sigmoid(inputs[0]) * inputs[1]).astype(BF16)

    c_all = Gather(place, hid, s_hid, c_s, c_r, cs_s, cs_r, cx_s, cx_r)
    for g in (0, 1):
        s_pre[g] = s_sum.result((g,))
    s_hid[z, x] = hidden(s_pre)
    c_all.begin_split()
    for g in (0, 1):
        bx_copy(g).wait_recv()
        pre[g] = bx_out[g].astype(F32) + bx_into[g].astype(F32)
    hid[z] = hidden(pre)
    c_all.begin_whole()
    e_sum = RingSum(place, lin_part, e_out, e_into, e_s, e_r, [(0,), (1,)], lambda tag: tag[0])
    for step in (1, 2, 3):
        c_all.step(step)
    for tag in e_sum.tags:
        e_sum.begin(tag)

    c_all.last_split()
    c_all.last_whole()
    d_part[...] = jnp.dot(hid[...].reshape(Z * ROWS, WHOLE), down[:WHOLE], preferred_element_type=F32)
    c_all.wait_pair()

    def d_copy(b, apart):
        peer = lax.rem(mp + apart, 8)
        return remote(
            d_out.at[b, peer], d_into.at[role, mp], d_s.at[b, apart - 1], d_r.at[role, apart - 1], (b, dp, peer)
        )

    def d_arrival(source_role, apart):
        source = lax.rem(mp - apart + 8, 8)
        got = d_into.at[source_role, source]
        return remote(got, got, d_s.at[0, apart - 1], d_r.at[source_role, apart - 1], (source_role, dp, source))

    def d_partner(arriving=False):
        return remote(
            d_out.at[1 - role, mp],
            d_into.at[1 - role if arriving else role, mp],
            one_s.at[0],
            one_r.at[0],
            place.partner,
        )

    for b in halves:
        columns = slice(b * QUARTER, (b + 1) * QUARTER)
        total = d_part[:, columns] + jnp.dot(
            jnp.concatenate([s_hid[:, c].reshape(Z * ROWS, SPLIT) for c in halves], axis=1),
            down[WHOLE:, columns],
            preferred_element_type=F32,
        )
        d_out[b] = total.reshape(Z, ROWS, QUARTER).astype(BF16)
        for apart in (4, 3, 5, 2, 6, 1, 7):
            d_copy(b, apart).start()
    d_partner().start()
    d_into[role, mp] = d_out[role, mp]
    e_sum.step(2)
    for apart in (1, 7, 2, 6, 3, 5, 4):
        for source_role in (0, 1):
            d_arrival(source_role, apart).wait_recv()
    d_partner(True).wait_recv()

    def summed(source_role):
        own = d_into[source_role, 0].astype(F32)
        for source in range(1, 8):
            own = own + d_into[source_role, source].astype(F32)
        return own.astype(BF16)

    teacher_rows = summed(0)
    error = summed(1).astype(F32) - teacher_rows.astype(F32)
    err[role, mp] = error.astype(BF16)

    def err_copy(apart):
        peer = lax.rem(mp + apart, 8)
        return remote(
            err.at[role, mp], err.at[role, mp], i_s.at[apart - 1], i_r.at[role, apart - 1], (1, dp, peer)
        )

    def err_arrival(source_role, apart):
        source = lax.rem(mp - apart + 8, 8)
        got = err.at[source_role, source]
        return remote(got, got, i_s.at[apart - 1], i_r.at[source_role, apart - 1], (source_role, dp, source))

    def err_partner():
        return remote(err.at[0, mp], err.at[0, mp], one_s.at[1], one_r.at[1], place.partner)

    for apart in (4, 3, 5, 2, 6, 1, 7):
        err_copy(apart).start()

    @pl.when(teacher)
    def _():
        err_partner().start()

    target_out[...] = teacher_rows

    def target_copy():
        return remote(target_out, target, one_s.at[2], one_r.at[2], place.across)

    @pl.when(z != mp)
    def _():
        target_copy().start()

    @pl.when(z == mp)
    def _():
        target[...] = target_out[...]

    row = lax.broadcasted_iota(jnp.int32, (8, 128), 0)
    teacher_float = teacher_rows.astype(F32)
    target_square = jnp.sum(teacher_float * teacher_float)
    error_square = jnp.sum(error * error)
    norm = Total(place, m1, z1, x1, x1_got, r1, r1_got, m1_s, m1_r, z1_s, z1_r, o1_s, o1_r)
    norm.start(jnp.where(row == 0, target_square, jnp.where(row == 1, error_square, 0.0)))
    e_sum.step(3)

    k_sum = RingSum(place, part.at[0], k_out, k_into, k_s, k_r, [()], lambda tag: 0)
    ks_sum = PairRingSum(place, s_part.at[1, 0], ks_out, ks_into, ks_s, ks_r, [()], lambda tag: 1)
    ks_sum.pair(s_part.at[0, 0], ksx_out, ksx_into, ksx_s, ksx_r)

    def err_share():
        return remote(err, err_out, share_s.at[2], share_r.at[2], place.partner)

    def err_store():
        return pltpu.make_async_copy(err, err_out, store_sem.at[3])

    def parts_of(whole, split, out):
        yield whole, out.at[:, :, :WHOLE]
        for b in halves:
            yield split.at[:, b], out.at[:, :, WHOLE + b * SPLIT : WHOLE + (b + 1) * SPLIT]

    def hid_shares():
        return [
            remote(here, there, share_s.at[5 + i], share_r.at[5 + i], place.partner)
            for i, (here, there) in enumerate(parts_of(hid, s_hid, hid_out))
        ]

    def hid_stores():
        return [
            pltpu.make_async_copy(here, there, store_sem.at[7 + i])
            for i, (here, there) in enumerate(parts_of(hid, s_hid, hid_out))
        ]

    def cot_dot(start, size):
        return lax.dot_general(
            jnp.concatenate([err[b].reshape(Z * ROWS, QUARTER) for b in halves], axis=1),
            down[pl.ds(start, size)],
            (((1,), (1,)), ((), ())),
            preferred_element_type=F32,
        ).reshape(Z, ROWS, size)

    @pl.when(student)
    def _():
        for apart in (1, 7, 2, 6, 3, 5, 4):
            for source_role in (0, 1):
                err_arrival(source_role, apart).wait_recv()
        err_partner().wait_recv()
        s_part[0, 0] = cot_dot(pl.multiple_of(WHOLE + x_of[0] * SPLIT, 128), SPLIT)
        ks_sum.exchange((4, 3, 5, 2, 6, 1, 7, 0))
        part[0] = cot_dot(0, WHOLE)
        k_sum.begin(())
        s_part[1, 0] = cot_dot(pl.multiple_of(WHOLE + x_of[1] * SPLIT, 128), SPLIT)
        err_share().start()
        err_store().start()
        for copy in hid_shares() + hid_stores():
            copy.start()

    norm.over_x()
    e_sum.step(4)
    norm.over_z()

    @pl.when(student)
    def _():
        k_sum.step(2)
        ks_sum.begin(())

    def ex_copy():
        return remote(ex_out, ex_into, one_s.at[3], one_r.at[3], place.x_other)

    ex_out[...] = e_sum.result((0,)).astype(BF16)
    ex_copy().start()
    linear_rows = e_sum.result((1,))
    norm.over_role()

    @pl.when(student)
    def _():
        k_sum.step(3)
        ks_sum.step(2)

    ex_copy().wait_recv()

    @pl.when(z != mp)
    def _():
        target_copy().wait_recv()

    linear_error = linear_rows + ex_into[...].astype(F32) - target[...].astype(F32)
    lin_err[z, x] = linear_error.astype(BF16)
    j_all = RingGather(place, lin_err, j_s, j_r, jx_s.at[0], jx_r.at[0])
    j_all.begin()
    loss = Total(place, m2, z2, x2, x2_got, r2, r2_got, m2_s, m2_r, z2_s, z2_r, o2_s, o2_r)
    loss.start(jnp.where(row == 2, jnp.sum(linear_error * linear_error), 0.0))

    @pl.when(student)
    def _():
        k_sum.step(4)
        ks_sum.step(3)

    stat[...] = norm.result()
    j_all.begin_other()
    loss.over_x()

    def kx_copy():
        return remote(kx_out, kx_into, bx_s.at[2], bx_r.at[2], place.x_other)

    def gate_copy(i):
        return remote(*((s_gate_out, s_cot.at[z, x]), (gate_out, cot.at[z]))[i], g_s.at[i], g_r.at[i], place.partner)

    l_all = Gather(place, cot, s_cot, l_s, l_r, ls_s, ls_r, lx_s, lx_r)

    def gate_next(way, i):
        ends = ((s_gate_out, s_cot.at[z, x]), (gate_out, cot.at[z]))[i]
        return remote(*ends, gn_s.at[way, i], (ls_r, l_r)[i].at[way, 0], place.z_next_cross[way])

    def cotangents(total, inputs):
        factor = (16.0 * MODEL) / stat[0:1, 0:1]
        hidden_cot = total * factor
        gate_pre, up_pre = inputs[0], inputs[1]
        sig = jax.nn.sigmoid(gate_pre)
        gate_cot = hidden_cot * up_pre * sig * (1.0 + gate_pre * (1.0 - sig))
        return gate_cot.astype(BF16), (hidden_cot * gate_pre * sig).astype(BF16)

    @pl.when(student)
    def _():
        kx_out[...] = k_sum.result(()).astype(BF16)
        kx_copy().start()
        ks_sum.step(4)
        s_gate_out[...], s_cot[z, x] = cotangents(ks_sum.result(()), s_pre)
        for way in (0, 1):
            gate_next(way, 0).start()
        gate_copy(0).start()
        l_all.begin_split()
        kx_copy().wait_recv()
        gate_out[...], cot[z] = cotangents(kx_out[...].astype(F32) + kx_into[...].astype(F32), pre)
        for way in (0, 1):
            gate_next(way, 1).start()
        l_all.begin_whole()
        gate_copy(1).start()

    j_all.step(1)

    @pl.when(teacher)
    def _():
        gate_copy(0).wait_recv()
        l_all.x_copy(0, 0).start()

    tokens.drain()
    for apart in range(1, 8):
        hand(apart).wait_send()
        for b in halves:
            d_copy(b, apart).wait_send()
    b_sum.drain()
    s_sum.drain()
    for g in (0, 1):
        bx_copy(g).wait_send()
    loss.over_z()
    l_all.step(1)
    j_all.step(2)
    c_all.drain()
    e_sum.drain()
    l_all.step(2)
    j_all.step(3)
    loss.over_role()
    d_partner().wait_send()
    for apart in range(1, 8):
        err_copy(apart).wait_send()
    ex_copy().wait_send()
    norm.drain()
    l_all.step(3)
    stat[...] = stat[...] + loss.result()
    stores.append(pltpu.make_async_copy(stat, stat_out, store_sem.at[4]))
    stores[-1].start()
    j_all.last()

    def lin_columns(b):
        start = pl.multiple_of(b * 2 * QUARTER + role * QUARTER, QUARTER)
        return lin_out.at[:, :, pl.ds(start, QUARTER)]

    def lin_share(b):
        return remote(lin_err.at[:, b], lin_columns(b), share_s.at[3 + b], share_r.at[3 + b], place.partner)

    def lin_arrival(b):
        start = pl.multiple_of(b * 2 * QUARTER + (1 - role) * QUARTER, QUARTER)
        got = lin_out.at[:, :, pl.ds(start, QUARTER)]
        return remote(lin_err.at[:, b], got, share_s.at[3 + b], share_r.at[3 + b], place.partner)

    for b in halves:
        lin_share(b).start()
        stores.append(pltpu.make_async_copy(lin_err.at[:, b], lin_columns(b), store_sem.at[5 + b]))
        stores[-1].start()

    @pl.when(teacher)
    def _():
        gate_copy(1).wait_recv()

    l_all.last_split()
    l_all.last_whole()
    l_all.wait_pair()
    for i, (here, there) in enumerate(parts_of(cot, s_cot, cot_out)):
        stores.append(pltpu.make_async_copy(here, there, store_sem.at[10 + i]))
        stores[-1].start()

    loss.drain()
    j_all.drain()
    for b in halves:
        lin_share(b).wait_send()

    @pl.when(z != mp)
    def _():
        target_copy().wait_send()

    @pl.when(student)
    def _():
        k_sum.drain()
        ks_sum.drain()
        l_all.drain()
        err_share().wait_send()
        err_store().wait()
        kx_copy().wait_send()
        for i in (0, 1):
            gate_copy(i).wait_send()
            for way in (0, 1):
                gate_next(way, i).wait_send()
        for copy in hid_shares():
            copy.wait_send()
        for copy in hid_stores():
            copy.wait()

    @pl.when(teacher)
    def _():
        l_all.drain(2)
        err_partner().wait_send()
        err_share().wait_recv()
        for copy in hid_shares():
            copy.wait_recv()

    for b in halves:
        lin_arrival(b).wait_recv()
    for store in stores:
        store.wait()


def exchange(tokens, w, down, linear):
    def vmem(*shape, dtype=BF16):
        return pltpu.VMEM(shape, dtype)

    def sems(*shape):
        return pltpu.SemaphoreType.DMA(shape)

    def array(*shape, dtype=BF16):
        return jax.ShapeDtypeStruct(shape, dtype)

    def total_tiles():
        return [vmem(8, 8, 128, dtype=F32)] * 2 + [vmem(8, 128, dtype=F32)] * 4

    anywhere = pl.BlockSpec(memory_space=pl.ANY)
    return pl.pallas_call(
        exchange_kernel,
        out_shape=[
            array(2, Z, ROWS, QUARTER),
            array(Z, ROWS, UNITS),
            array(Z, ROWS, UNITS),
            array(2, Z, ROWS, QUARTER),
            array(Z, ROWS, LIN),
            array(8, 128, dtype=F32),
        ],
        in_specs=[anywhere] * 4,
        out_specs=[anywhere] * 6,
        scratch_shapes=[
            vmem(2, Z, ROWS, QUARTER), vmem(WIDTH, 2 * UNITS), vmem(UNITS, WIDTH), vmem(2, WIDTH, QUARTER),
            vmem(2, Z, ROWS, WHOLE, dtype=F32), vmem(2, 4, 2, ROWS, WHOLE), vmem(2, 4, 2, ROWS, WHOLE),
            vmem(2, ROWS, WHOLE), vmem(2, ROWS, WHOLE), vmem(2, ROWS, WHOLE, dtype=F32), vmem(Z, ROWS, WHOLE),
            vmem(2, 2, Z, ROWS, SPLIT, dtype=F32), vmem(2, 4, 2, ROWS, SPLIT), vmem(2, 4, 2, ROWS, SPLIT),
            vmem(Z, 2, ROWS, SPLIT), vmem(Z, 2, ROWS, SPLIT), vmem(2, ROWS, SPLIT, dtype=F32), vmem(Z, 2, ROWS, SPLIT),
            vmem(Z * ROWS, WIDTH, dtype=F32), vmem(2, 8, ROWS, QUARTER), vmem(2, 8, ROWS, QUARTER),
            vmem(2, 8, ROWS, QUARTER), vmem(ROWS, QUARTER), vmem(ROWS, QUARTER),
            vmem(2, Z, ROWS, QUARTER, dtype=F32), vmem(2, 4, 2, ROWS, QUARTER), vmem(2, 4, 2, ROWS, QUARTER),
            vmem(ROWS, QUARTER), vmem(ROWS, QUARTER), vmem(Z, 2, ROWS, QUARTER),
            vmem(2, 4, ROWS, WHOLE), vmem(2, 4, ROWS, WHOLE), vmem(ROWS, WHOLE), vmem(ROWS, WHOLE),
            vmem(ROWS, WHOLE), vmem(Z, ROWS, WHOLE),
            vmem(2, 4, ROWS, SPLIT), vmem(2, 4, ROWS, SPLIT), vmem(Z, ROWS, SPLIT), vmem(Z, ROWS, SPLIT),
            vmem(ROWS, SPLIT), vmem(Z, 2, ROWS, SPLIT),
            *total_tiles(), *total_tiles(), vmem(8, 128, dtype=F32),
            sems(6), sems(13),
            sems(7), sems(7), sems(7), sems(7), sems(2, 4, 2), sems(2, 4, 2), sems(3), sems(3),
            sems(2, 4, 2), sems(2, 4, 2), sems(8), sems(8),
            sems(2, 4), sems(2, 4), sems(2, 4), sems(2, 4), sems(8), sems(8),
            sems(2, 7), sems(2, 7), sems(4), sems(4), sems(7), sems(2, 7), sems(2, 4, 2), sems(2, 4, 2),
            sems(2, 4), sems(2, 4), sems(2, 4), sems(2, 4), sems(8), sems(8),
            sems(2, 4, 2), sems(2, 4, 2), sems(1), sems(1),
            sems(2, 4), sems(2, 4), sems(2, 4), sems(2, 4), sems(8), sems(8), sems(2), sems(2), sems(2, 2),
            sems(7), sems(7), sems(7), sems(7), sems(2), sems(2),
            sems(7), sems(7), sems(7), sems(7), sems(2), sems(2),
            sems(8), sems(8),
        ],
        compiler_params=pltpu.CompilerParams(
            collective_id=0, has_side_effects=True, vmem_limit_bytes=34 * 1024 * 1024
        ),
        name="exchange",
    )(tokens, w, down, linear)


def contract_rows(left, right):
    return lax.dot_general(left, right, (((0,), (0,)), ((), ())), preferred_element_type=F32)


BLOCK = 256


def gradients_kernel(tok, cot, hid, err, lin_err, stat, unit_out, down_out, linear_out, losses, turned, unit, down, linear, sem):
    factor = (16.0 * MODEL) / stat[0:1, 0:1]
    share = stat[...] / stat[0:1, 0:1]
    losses[0] = share[1, 0]
    losses[1] = share[2, 0]
    for b in (0, 1):
        turned[b * QUARTER : (b + 1) * QUARTER] = tok[b].T
    copies = []

    def send(here, there):
        copies.append(pltpu.make_async_copy(here, there, sem.at[len(copies)]))
        copies[-1].start()

    for i in range(UNITS // BLOCK):
        part = slice(i * BLOCK, (i + 1) * BLOCK)
        unit[:, part] = jnp.dot(turned[...], cot[:, part], preferred_element_type=F32).astype(BF16)
        send(unit.at[:, part], unit_out.at[:, part])
        for b in (0, 1):
            down[part, b * QUARTER : (b + 1) * QUARTER] = (factor * contract_rows(hid[:, part], err[b])).astype(BF16)
        send(down.at[part], down_out.at[part])
        if i < LIN // BLOCK:
            product = jnp.dot(turned[...], lin_err[:, part], preferred_element_type=F32)
            linear[:, part] = (factor * product).astype(BF16)
            send(linear.at[:, part], linear_out.at[:, part])
    for copy in copies:
        copy.wait()


def gradients(tok, cot, hid, err, lin_err, stat):
    shapes = [(WIDTH, UNITS), (UNITS, WIDTH), (WIDTH, LIN)]
    return pl.pallas_call(
        gradients_kernel,
        out_shape=[jax.ShapeDtypeStruct(shape, BF16) for shape in shapes] + [jax.ShapeDtypeStruct((2,), F32)],
        in_specs=[pl.BlockSpec(memory_space=pltpu.VMEM)] * 6,
        out_specs=[pl.BlockSpec(memory_space=pl.ANY)] * 3 + [pl.BlockSpec(memory_space=pltpu.SMEM)],
        scratch_shapes=[
            pltpu.VMEM((WIDTH, Z * ROWS), BF16),
            *[pltpu.VMEM(shape, BF16) for shape in shapes],
            pltpu.SemaphoreType.DMA((2 * (UNITS // BLOCK) + LIN // BLOCK,)),
        ],
        compiler_params=pltpu.CompilerParams(vmem_limit_bytes=24 * 1024 * 1024),
        name="gradients",
    )(tok, cot, hid, err, lin_err, stat)


def body(tokens, gate_up, down, linear):
    w = gate_up.reshape(WIDTH, 2 * UNITS)
    tok, cot, hid, err, lin_err, stat = exchange(tokens, w, down[0], linear)
    rows = Z * ROWS
    unit_grad, down_grad, linear_grad, losses = gradients(
        tok.reshape(2, rows, QUARTER),
        cot.reshape(rows, UNITS),
        hid.reshape(rows, UNITS),
        err.reshape(2, rows, QUARTER),
        lin_err.reshape(rows, LIN),
        stat,
    )
    return (unit_grad[None], down_grad, linear_grad, losses)


def solution(mesh):
    return jax.shard_map(
        body,
        mesh=mesh,
        in_specs=(P("mp", "dp"), P("role", "dp", None, "mp"), P("role", "mp", "dp"), P("dp", "mp")),
        out_specs=(P("role", "dp", "mp"), P("mp", "dp"), P("dp", "mp"), P()),
        check_vma=False,
    )
```

```python
import jax
import jax.numpy as jnp
from jax import lax
from jax.experimental import pallas as pl
from jax.experimental.pallas import tpu as pltpu
from jax.sharding import PartitionSpec as P

MESH = pl.DeviceIdType.MESH
BF16, F32 = jnp.bfloat16, jnp.float32
MODEL = 8192
Z = 8
ROWS = 48
WIDTH = 512
UNITS = 1792
WHOLE = 768
SPLIT = 512
LIN = 1024
QUARTER = LIN // 4


def remote(src, dst, send, recv, device):
    return pltpu.make_async_remote_copy(
        src_ref=src, dst_ref=dst, send_sem=send, recv_sem=recv, device_id=device, device_id_type=MESH
    )


class RingSum:
    def __init__(self, place, part, out, into, send, recv, tags, long_way):
        self.place, self.part, self.out, self.into = place, part, out, into
        self.send, self.recv, self.tags, self.long_way = send, recv, tags, long_way

    def copy(self, way, step, tag):
        at = (way, step - 1) + tag
        return remote(
            self.out.at[at], self.into.at[at], self.send.at[at], self.recv.at[at], self.place.z_next[way]
        )

    def push(self, way, step, tag, first):
        sign = 1 - 2 * way
        total = self.local(tag, sign * (5 - step))
        if not first:
            self.copy(way, step - 1, tag).wait_recv()
            total = total + self.into[(way, step - 2) + tag].astype(F32)
        self.out[(way, step - 1) + tag] = total.astype(BF16)
        self.copy(way, step, tag).start()

    def local(self, tag, offset):
        return self.part[tag + (lax.rem(self.place.z + offset + Z, Z),)]

    def begin(self, tag, both=True):
        far = self.long_way(tag)
        self.push(far, 1, tag, True)
        if both:
            self.push(1 - far, 2, tag, True)

    def step(self, step, both=False):
        for tag in self.tags:
            for way in (0, 1):
                if step > 2 or way == self.long_way(tag):
                    self.push(way, step, tag, False)
                elif both:
                    self.push(way, step, tag, True)

    def result(self, tag):
        total = self.local(tag, 0)
        for way in (0, 1):
            self.copy(way, 4, tag).wait_recv()
            total = total + self.into[(way, 3) + tag].astype(F32)
        return total

    def drain(self):
        for tag in self.tags:
            for way in (0, 1):
                for step in range(1 if way == self.long_way(tag) else 2, 5):
                    self.copy(way, step, tag).wait_send()


class RingGather:
    def __init__(self, place, buf, send, recv, x_send, x_recv):
        self.place, self.buf, self.send, self.recv = place, buf, send, recv
        self.x_send, self.x_recv = x_send, x_recv

    def copy(self, way, step, mine, arriving=False):
        place = self.place
        sign = 1 - 2 * way
        block = lax.rem(place.z - sign * (step if arriving else step - 1) + Z, Z)
        x = place.x if mine else 1 - place.x
        part = self.buf.at[block, x]
        at = (way, step - 1, mine)
        return remote(part, part, self.send.at[at], self.recv.at[at], place.z_next[way])

    def x_copy(self, arriving=False):
        place = self.place
        part = self.buf.at[place.z, 1 - place.x if arriving else place.x]
        return remote(part, part, self.x_send, self.x_recv, place.x_other)

    def begin(self):
        self.copy(0, 1, 1).start()
        self.copy(1, 1, 1).start()
        self.x_copy().start()

    def begin_other(self):
        self.x_copy(True).wait_recv()
        self.copy(0, 1, 0).start()
        self.copy(1, 1, 0).start()

    def step(self, step):
        for mine in (1, 0):
            for way in (0, 1):
                self.copy(way, step, mine, True).wait_recv()
                if step < 3 or way == 1 - mine:
                    self.copy(way, step + 1, mine).start()

    def last(self):
        for mine in (1, 0):
            self.copy(1 - mine, 4, mine, True).wait_recv()

    def drain(self):
        self.x_copy().wait_send()
        for mine in (1, 0):
            for way in (0, 1):
                for step in range(1, 5 if way == 1 - mine else 4):
                    self.copy(way, step, mine).wait_send()


class PairRingSum(RingSum):
    def pair(self, other, x_out, x_into, x_send, x_recv):
        self.other, self.x_out, self.x_into, self.x_send, self.x_recv = other, x_out, x_into, x_send, x_recv
        self.got = set()

    def block(self, offset):
        return lax.rem(self.place.z + offset, Z)

    def x_copy(self, offset):
        block = self.block(offset)
        return remote(
            self.x_out.at[block], self.x_into.at[block], self.x_send.at[offset], self.x_recv.at[offset], self.place.x_other
        )

    def exchange(self, offsets):
        for offset in offsets:
            block = self.block(offset)
            for tag in self.tags:
                self.x_out[(block,) + tag] = self.other[tag + (block,)].astype(BF16)
            self.x_copy(offset).start()

    def local(self, tag, offset):
        offset = offset % Z
        if offset not in self.got:
            self.got.add(offset)
            self.x_copy(offset).wait_recv()
        block = self.block(offset)
        return self.part[tag + (block,)] + self.x_into[(block,) + tag].astype(F32)

    def drain(self):
        super().drain()
        for offset in range(Z):
            self.x_copy(offset).wait_send()


class Gather:
    def __init__(self, place, whole, split, w_send, w_recv, s_send, s_recv, x_send, x_recv):
        self.place, self.whole, self.split = place, whole, split
        self.w_send, self.w_recv, self.s_send, self.s_recv = w_send, w_recv, s_send, s_recv
        self.x_send, self.x_recv = x_send, x_recv

    def block(self, way, steps):
        return lax.rem(self.place.z - (1 - 2 * way) * steps + Z, Z)

    def w_copy(self, way, step, arriving=False, source=None):
        part = self.whole.at[self.block(way, step if arriving else step - 1)]
        if step == 4:
            part = part.at[:, way * WHOLE // 2 : (way + 1) * WHOLE // 2]
        at = (way, step - 1)
        return remote(part if source is None else source, part, self.w_send.at[at], self.w_recv.at[at], self.place.z_next[way])

    def s_copy(self, way, step, arriving=False, source=None):
        part = self.split.at[self.block(way, step if arriving else step - 1), self.place.x]
        at = (way, step - 1)
        return remote(part if source is None else source, part, self.s_send.at[at], self.s_recv.at[at], self.place.z_next[way])

    def x_copy(self, way, steps, arriving=False, source=None):
        part = self.split.at[self.block(way, steps), 1 - self.place.x if arriving else self.place.x]
        at = steps + 3 * way if steps else 0
        return remote(
            part if source is None else source, part, self.x_send.at[at], self.x_recv.at[at], self.place.x_other
        )

    def begin_split(self, source=None):
        for way in (0, 1):
            self.s_copy(way, 1, source=source).start()
        self.x_copy(0, 0, source=source).start()

    def begin_whole(self, source=None):
        for way in (0, 1):
            self.w_copy(way, 1, source=source).start()

    def step(self, step):
        for way in (0, 1):
            self.s_copy(way, step, True).wait_recv()
            if step < 3 or way == 1:
                self.s_copy(way, step + 1).start()
            self.x_copy(way, step).start()
        for way in (0, 1):
            self.w_copy(way, step, True).wait_recv()
            self.w_copy(way, step + 1).start()

    def last_split(self):
        self.s_copy(1, 4, True).wait_recv()
        self.x_copy(1, 4).start()

    def last_whole(self):
        for way in (0, 1):
            self.w_copy(way, 4, True).wait_recv()

    def crossings(self):
        return [(0, 0)] + [(way, steps) for steps in (1, 2, 3) for way in (0, 1)] + [(1, 4)]

    def wait_pair(self):
        for way, steps in self.crossings():
            self.x_copy(way, steps, True).wait_recv()

    def drain(self, first=1):
        for way in (0, 1):
            for step in range(first, 5):
                self.w_copy(way, step).wait_send()
                if step < 4 or way == 1:
                    self.s_copy(way, step).wait_send()
        for way, steps in self.crossings():
            self.x_copy(way, steps).wait_send()


class Direct:
    def __init__(self, me, device_of, out, into, send, recv):
        self.me, self.device_of, self.out, self.into, self.send, self.recv = me, device_of, out, into, send, recv

    def copy(self, apart):
        peer = lax.rem(self.me + apart, 8)
        return remote(
            self.out(peer), self.into(self.me), self.send.at[apart - 1], self.recv.at[apart - 1], self.device_of(peer)
        )

    def start(self):
        for apart in (4, 3, 5, 2, 6, 1, 7):
            self.copy(apart).start()

    def wait_one(self, apart):
        source = lax.rem(self.me - apart + 8, 8)
        part = self.into(source)
        remote(part, part, self.send.at[apart - 1], self.recv.at[apart - 1], self.device_of(source)).wait_recv()

    def wait(self):
        for apart in (1, 7, 2, 6, 3, 5, 4):
            self.wait_one(apart)

    def drain(self):
        for apart in range(1, 8):
            self.copy(apart).wait_send()


class Total:
    def __init__(self, place, m, zs, x, x_got, r, r_got, m_s, m_r, z_s, z_r, one_s, one_r):
        self.place, self.m, self.zs, self.x, self.x_got, self.r, self.r_got = place, m, zs, x, x_got, r, r_got
        self.m_all = Direct(place.mp, place.of_mp, lambda peer: m.at[place.mp], lambda source: m.at[source], m_s, m_r)
        self.z_all = Direct(place.z, place.of_z, lambda peer: zs.at[place.z], lambda source: zs.at[source], z_s, z_r)
        self.one_s, self.one_r = one_s, one_r

    def x_copy(self):
        return remote(self.x, self.x_got, self.one_s.at[0], self.one_r.at[0], self.place.x_other)

    def r_copy(self):
        return remote(self.r, self.r_got, self.one_s.at[1], self.one_r.at[1], self.place.partner)

    def in_order(self, slots):
        total = slots[0]
        for source in range(1, 8):
            total = total + slots[source]
        return total

    def start(self, tile):
        self.m[self.place.mp] = tile
        self.m_all.start()

    def over_x(self):
        self.m_all.wait()
        self.x[...] = self.in_order(self.m)
        self.x_copy().start()

    def over_z(self):
        self.x_copy().wait_recv()
        self.zs[self.place.z] = self.x[...] + self.x_got[...]
        self.z_all.start()

    def over_role(self):
        self.z_all.wait()
        self.r[...] = self.in_order(self.zs)
        self.r_copy().start()

    def result(self):
        self.r_copy().wait_recv()
        return self.r[...] + self.r_got[...]

    def drain(self):
        self.m_all.drain()
        self.x_copy().wait_send()
        self.z_all.drain()
        self.r_copy().wait_send()


class Place:
    def __init__(self):
        self.role, self.mp, self.dp = lax.axis_index("role"), lax.axis_index("mp"), lax.axis_index("dp")
        dp = self.dp
        self.z, self.x = dp // 2, lax.rem(dp, 2)
        role, mp, z, x = self.role, self.mp, self.z, self.x
        up, down = lax.rem(z + 1, Z) * 2 + x, lax.rem(z + Z - 1, Z) * 2 + x
        self.z_next = ((role, up, mp), (role, down, mp))
        self.z_next_cross = ((1 - role, up, mp), (1 - role, down, mp))
        self.x_other = (role, z * 2 + 1 - x, mp)
        self.partner = (1 - role, dp, mp)
        self.across = (role, mp * 2 + x, z)
        self.of_z = lambda peer: (role, peer * 2 + x, mp)
        self.of_mp = lambda peer: (role, dp, peer)


def exchange_kernel(
    tok_in, w_in, down_in, lin_in,
    tok_out, cot, s_cot, hid_out, err_out, lin_out, stat_out,
    tok, w, down, lin, down_turned,
    part, b_out, b_into, bx_out, bx_into, pre, hid,
    s_part, s_out, s_into, sx_out, sx_into, s_pre, s_hid,
    d_part, d_out, d_into, err, target_out, target,
    lin_part, e_out, e_into, ex_out, ex_into, lin_err,
    k_out, k_into, kx_out, kx_into, gate_out, up_out,
    ks_out, ks_into, ksx_out, ksx_into, s_gate_out, s_up_out,
    m1, z1, x1, x1_got, r1, r1_got, stat,
    load_sem, store_sem,
    tok_s, tok_r, hand_s, hand_r, b_s, b_r, bx_s, bx_r, s_s, s_r, sx_s, sx_r,
    c_s, c_r, cs_s, cs_r, cx_s, cx_r,
    d_s, d_r, one_s, one_r, i_s, i_r, e_s, e_r, k_s, k_r, ks_s, ks_r, ksx_s, ksx_r,
    j_s, j_r, jx_s, jx_r, l_s, l_r, ls_s, ls_r, lx_s, lx_r, g_s, g_r, gn_s,
    m1_s, m1_r, z1_s, z1_r, o1_s, o1_r,
    share_s, share_r,
):
    place = Place()
    role, mp, dp, z, x = place.role, place.mp, place.dp, place.z, place.x
    student, teacher = role == 1, role == 0
    x_of = (1 - x, x)
    halves = (0, 1)

    loads = [
        pltpu.make_async_copy(tok_in.at[:, b * QUARTER : (b + 1) * QUARTER], tok.at[b, mp], load_sem.at[b])
        for b in halves
    ]
    loads += [
        pltpu.make_async_copy(w_in, w, load_sem.at[2]),
        pltpu.make_async_copy(down_in, down, load_sem.at[3]),
    ]
    loads += [
        pltpu.make_async_copy(
            lin_in.at[:, pl.ds(pl.multiple_of(b * 2 * QUARTER + role * QUARTER, QUARTER), QUARTER)],
            lin.at[b],
            load_sem.at[4 + b],
        )
        for b in halves
    ]
    for load in loads:
        load.start()

    barrier = pltpu.get_barrier_semaphore()

    def greet(device):
        pl.semaphore_signal(barrier, inc=1, device_id=device, device_id_type=MESH)

    for apart in range(1, 8):
        greet(place.of_mp(lax.rem(mp + apart, 8)))
        greet((1 - role, dp, lax.rem(mp + apart, 8)))
        greet(place.of_z(lax.rem(z + apart, 8)))
    greet(place.x_other)
    greet(place.partner)
    for way in (0, 1):
        greet(place.z_next_cross[way])

    @pl.when(z != mp)
    def _():
        greet(place.across)
        pl.semaphore_wait(barrier, 26)

    @pl.when(z == mp)
    def _():
        pl.semaphore_wait(barrier, 25)

    for load in loads[:2]:
        load.wait()
    tokens = Direct(mp, place.of_mp, lambda peer: tok.at[role, mp], lambda source: tok.at[role, source], tok_s, tok_r)
    tokens.start()

    def hand(apart, arriving=False):
        source = lax.rem(mp - apart + 8, 8)
        part_of = tok.at[1 - role if arriving else role, source]
        return remote(part_of, part_of, hand_s.at[apart - 1], hand_r.at[apart - 1], place.partner)

    for apart in (1, 7, 2, 6, 3, 5, 4):
        tokens.wait_one(apart)
        hand(apart).start()
    loads[2].wait()
    for apart in (1, 7, 2, 6, 3, 5, 4):
        hand(apart, True).wait_recv()
    stores = [pltpu.make_async_copy(tok, tok_out, store_sem.at[0])]
    stores[0].start()

    def all_tokens():
        return jnp.concatenate([tok[b].reshape(Z * ROWS, QUARTER) for b in halves], axis=1)

    tags = [(0,), (1,)]
    b_sum = RingSum(place, part, b_out, b_into, b_s, b_r, tags, lambda tag: tag[0])
    s_sum = PairRingSum(place, s_part.at[1], s_out, s_into, s_s, s_r, tags, lambda tag: tag[0])
    s_sum.pair(s_part.at[0], sx_out, sx_into, sx_s, sx_r)

    def split_dot(q):
        for g in (0, 1):
            column = pl.multiple_of(g * UNITS + WHOLE + x_of[q] * SPLIT, 128)
            s_part[q, g] = jnp.dot(
                all_tokens(), w[:, pl.ds(column, SPLIT)], preferred_element_type=F32
            ).reshape(Z, ROWS, SPLIT)

    split_dot(0)
    s_sum.exchange((4,))
    for g in (0, 1):
        part[g] = jnp.dot(
            all_tokens(), w[:, g * UNITS : g * UNITS + WHOLE], preferred_element_type=F32
        ).reshape(Z, ROWS, WHOLE)
        b_sum.begin((g,))
        if g == 0:
            s_sum.exchange((3, 5))
    split_dot(1)
    for tag in tags:
        s_sum.begin(tag, False)
    b_sum.step(2)
    s_sum.exchange((2, 6))
    for load in loads[3:]:
        load.wait()
    for q in (0, 1):
        lin_part[q] = jnp.dot(all_tokens(), lin[x_of[q]], preferred_element_type=F32).reshape(Z, ROWS, QUARTER)
    s_sum.step(2, True)
    b_sum.step(3)
    s_sum.exchange((1, 7, 0))
    for c in range(UNITS // QUARTER):
        down_turned[:, c * QUARTER : (c + 1) * QUARTER] = down[c * QUARTER : (c + 1) * QUARTER].T
    s_sum.step(3)
    b_sum.step(4)
    s_sum.step(4)

    def bx_copy(g):
        return remote(bx_out.at[g], bx_into.at[g], bx_s.at[g], bx_r.at[g], place.x_other)

    for g in (0, 1):
        bx_out[g] = b_sum.result((g,)).astype(BF16)
        bx_copy(g).start()

    def hidden(inputs):
        return (inputs[0] * jax.nn.sigmoid(inputs[0]) * inputs[1]).astype(BF16)

    c_all = Gather(place, hid, s_hid, c_s, c_r, cs_s, cs_r, cx_s, cx_r)
    for g in (0, 1):
        s_pre[g] = s_sum.result((g,))
    s_hid[z, x] = hidden(s_pre)
    c_all.begin_split()
    for g in (0, 1):
        bx_copy(g).wait_recv()
        pre[g] = bx_out[g].astype(F32) + bx_into[g].astype(F32)
    hid[z] = hidden(pre)
    c_all.begin_whole()
    e_sum = RingSum(place, lin_part, e_out, e_into, e_s, e_r, [(0,), (1,)], lambda tag: tag[0])
    for tag in e_sum.tags:
        e_sum.begin(tag)
    for step in (1, 2, 3):
        c_all.step(step)
        e_sum.step(step + 1)

    c_all.last_split()
    c_all.last_whole()
    d_part[...] = jnp.dot(hid[...].reshape(Z * ROWS, WHOLE), down[:WHOLE], preferred_element_type=F32)
    c_all.wait_pair()

    def d_copy(b, apart):
        peer = lax.rem(mp + apart, 8)
        return remote(
            d_out.at[b, peer], d_into.at[role, mp], d_s.at[b, apart - 1], d_r.at[role, apart - 1], (b, dp, peer)
        )

    def d_arrival(source_role, apart):
        source = lax.rem(mp - apart + 8, 8)
        got = d_into.at[source_role, source]
        return remote(got, got, d_s.at[0, apart - 1], d_r.at[source_role, apart - 1], (source_role, dp, source))

    def d_partner(arriving=False):
        return remote(
            d_out.at[1 - role, mp],
            d_into.at[1 - role if arriving else role, mp],
            one_s.at[0],
            one_r.at[0],
            place.partner,
        )

    for b in halves:
        columns = slice(b * QUARTER, (b + 1) * QUARTER)
        total = d_part[:, columns] + jnp.dot(
            jnp.concatenate([s_hid[:, c].reshape(Z * ROWS, SPLIT) for c in halves], axis=1),
            down[WHOLE:, columns],
            preferred_element_type=F32,
        )
        d_out[b] = total.reshape(Z, ROWS, QUARTER).astype(BF16)
        for apart in (4, 3, 5, 2, 6, 1, 7):
            d_copy(b, apart).start()
    d_partner().start()
    d_into[role, mp] = d_out[role, mp]

    def ex_copy():
        return remote(ex_out, ex_into, one_s.at[3], one_r.at[3], place.x_other)

    ex_out[...] = e_sum.result((0,)).astype(BF16)
    ex_copy().start()
    linear_rows = e_sum.result((1,))
    tokens.drain()
    b_sum.drain()
    s_sum.drain()
    for apart in range(1, 8):
        hand(apart).wait_send()
    for g in (0, 1):
        bx_copy(g).wait_send()
    for apart in (1, 7, 2, 6, 3, 5, 4):
        for source_role in (0, 1):
            d_arrival(source_role, apart).wait_recv()
    d_partner(True).wait_recv()

    def summed(source_role):
        own = d_into[source_role, 0].astype(F32)
        for source in range(1, 8):
            own = own + d_into[source_role, source].astype(F32)
        return own.astype(BF16)

    teacher_rows = summed(0)
    error = summed(1).astype(F32) - teacher_rows.astype(F32)
    err[role, mp] = error.astype(BF16)

    def err_copy(apart):
        peer = lax.rem(mp + apart, 8)
        return remote(
            err.at[role, mp], err.at[role, mp], i_s.at[apart - 1], i_r.at[role, apart - 1], (1, dp, peer)
        )

    def err_arrival(source_role, apart):
        source = lax.rem(mp - apart + 8, 8)
        got = err.at[source_role, source]
        return remote(got, got, i_s.at[apart - 1], i_r.at[source_role, apart - 1], (source_role, dp, source))

    def err_partner():
        return remote(err.at[0, mp], err.at[0, mp], one_s.at[1], one_r.at[1], place.partner)

    for apart in (4, 3, 5, 2, 6, 1, 7):
        err_copy(apart).start()

    @pl.when(teacher)
    def _():
        err_partner().start()

    target_out[...] = teacher_rows

    def target_copy():
        return remote(target_out, target, one_s.at[2], one_r.at[2], place.across)

    @pl.when(z != mp)
    def _():
        target_copy().start()

    @pl.when(z == mp)
    def _():
        target[...] = target_out[...]

    k_sum = RingSum(place, part.at[0], k_out, k_into, k_s, k_r, [()], lambda tag: 0)
    ks_sum = PairRingSum(place, s_part.at[1, 0], ks_out, ks_into, ks_s, ks_r, [()], lambda tag: 1)
    ks_sum.pair(s_part.at[0, 0], ksx_out, ksx_into, ksx_s, ksx_r)

    def err_share():
        return remote(err, err_out, share_s.at[2], share_r.at[2], place.partner)

    def err_store():
        return pltpu.make_async_copy(err, err_out, store_sem.at[3])

    def parts_of(whole, split, out):
        yield whole, out.at[:, :, :WHOLE]
        for b in halves:
            yield split.at[:, b], out.at[:, :, WHOLE + b * SPLIT : WHOLE + (b + 1) * SPLIT]

    def hid_shares():
        return [
            remote(here, there, share_s.at[5 + i], share_r.at[5 + i], place.partner)
            for i, (here, there) in enumerate(parts_of(hid, s_hid, hid_out))
        ]

    def hid_stores():
        return [
            pltpu.make_async_copy(here, there, store_sem.at[7 + i])
            for i, (here, there) in enumerate(parts_of(hid, s_hid, hid_out))
        ]

    def cot_dot(start, size):
        all_err = jnp.concatenate([err[b].reshape(Z * ROWS, QUARTER) for b in halves], axis=1)
        return jnp.dot(all_err, down_turned[:, pl.ds(start, size)], preferred_element_type=F32).reshape(Z, ROWS, size)

    @pl.when(student)
    def _():
        for apart in (1, 7, 2, 6, 3, 5, 4):
            for source_role in (0, 1):
                err_arrival(source_role, apart).wait_recv()
        err_partner().wait_recv()
        s_part[0, 0] = cot_dot(pl.multiple_of(WHOLE + x_of[0] * SPLIT, 128), SPLIT)
        ks_sum.exchange((4,))
        part[0] = cot_dot(0, WHOLE)
        k_sum.begin(())
        ks_sum.exchange((3, 5))
        s_part[1, 0] = cot_dot(pl.multiple_of(WHOLE + x_of[1] * SPLIT, 128), SPLIT)
        ks_sum.exchange((2, 6, 1, 7, 0))
        err_share().start()
        err_store().start()
        for copy in hid_shares() + hid_stores():
            copy.start()

    ex_copy().wait_recv()

    @pl.when(z != mp)
    def _():
        target_copy().wait_recv()

    linear_error = linear_rows + ex_into[...].astype(F32) - target[...].astype(F32)
    lin_err[z, x] = linear_error.astype(BF16)
    j_all = RingGather(place, lin_err, j_s, j_r, jx_s.at[0], jx_r.at[0])
    j_all.begin()
    row = lax.broadcasted_iota(jnp.int32, (8, 128), 0)
    teacher_float = teacher_rows.astype(F32)
    norm = Total(place, m1, z1, x1, x1_got, r1, r1_got, m1_s, m1_r, z1_s, z1_r, o1_s, o1_r)
    target_square = jnp.sum(teacher_float * teacher_float)
    error_square = jnp.sum(error * error)
    linear_square = jnp.sum(linear_error * linear_error)
    norm.start(jnp.where(row == 0, target_square, jnp.where(row == 1, error_square, linear_square)))

    @pl.when(student)
    def _():
        ks_sum.begin((), False)
        k_sum.step(2)

    j_all.begin_other()
    norm.over_x()

    @pl.when(student)
    def _():
        ks_sum.step(2, True)
        k_sum.step(3)

    norm.over_z()
    j_all.step(1)

    @pl.when(student)
    def _():
        ks_sum.step(3)
        k_sum.step(4)
        ks_sum.step(4)

    norm.over_role()
    j_all.step(2)
    stat[...] = norm.result()
    stores.append(pltpu.make_async_copy(stat, stat_out, store_sem.at[4]))
    stores[-1].start()

    def kx_copy():
        return remote(kx_out, kx_into, bx_s.at[2], bx_r.at[2], place.x_other)

    def gate_copy(i):
        return remote(*((s_gate_out, s_cot.at[z, x]), (gate_out, cot.at[z]))[i], g_s.at[i], g_r.at[i], place.partner)

    def up_store(i):
        here, there = ((s_up_out, s_cot.at[z, x]), (up_out, cot.at[z]))[i]
        return pltpu.make_async_copy(here, there, store_sem.at[10 + i])

    l_all = Gather(place, cot, s_cot, l_s, l_r, ls_s, ls_r, lx_s, lx_r)

    def gate_next(way, i):
        ends = ((s_gate_out, s_cot.at[z, x]), (gate_out, cot.at[z]))[i]
        return remote(*ends, gn_s.at[way, i], (ls_r, l_r)[i].at[way, 0], place.z_next_cross[way])

    def cotangents(total, inputs):
        factor = (16.0 * MODEL) / stat[0:1, 0:1]
        hidden_cot = total * factor
        gate_pre, up_pre = inputs[0], inputs[1]
        sig = jax.nn.sigmoid(gate_pre)
        gate_cot = hidden_cot * up_pre * sig * (1.0 + gate_pre * (1.0 - sig))
        return gate_cot.astype(BF16), (hidden_cot * gate_pre * sig).astype(BF16)

    @pl.when(student)
    def _():
        kx_out[...] = k_sum.result(()).astype(BF16)
        kx_copy().start()
        s_gate_out[...], s_up_out[...] = cotangents(ks_sum.result(()), s_pre)
        for way in (0, 1):
            gate_next(way, 0).start()
        gate_copy(0).start()
        l_all.begin_split(s_up_out)
        up_store(0).start()
        kx_copy().wait_recv()
        gate_out[...], up_out[...] = cotangents(kx_out[...].astype(F32) + kx_into[...].astype(F32), pre)
        for way in (0, 1):
            gate_next(way, 1).start()
        l_all.begin_whole(up_out)
        up_store(1).start()
        gate_copy(1).start()

    @pl.when(teacher)
    def _():
        gate_copy(0).wait_recv()
        l_all.x_copy(0, 0).start()

    for apart in range(1, 8):
        err_copy(apart).wait_send()
        for b in halves:
            d_copy(b, apart).wait_send()
    d_partner().wait_send()
    j_all.step(3)
    l_all.step(1)
    j_all.last()

    def lin_columns(b):
        start = pl.multiple_of(b * 2 * QUARTER + role * QUARTER, QUARTER)
        return lin_out.at[:, :, pl.ds(start, QUARTER)]

    def lin_share(b):
        return remote(lin_err.at[:, b], lin_columns(b), share_s.at[3 + b], share_r.at[3 + b], place.partner)

    def lin_arrival(b):
        start = pl.multiple_of(b * 2 * QUARTER + (1 - role) * QUARTER, QUARTER)
        got = lin_out.at[:, :, pl.ds(start, QUARTER)]
        return remote(lin_err.at[:, b], got, share_s.at[3 + b], share_r.at[3 + b], place.partner)

    for b in halves:
        lin_share(b).start()
        stores.append(pltpu.make_async_copy(lin_err.at[:, b], lin_columns(b), store_sem.at[5 + b]))
        stores[-1].start()

    c_all.drain()
    e_sum.drain()
    l_all.step(2)
    ex_copy().wait_send()
    norm.drain()
    j_all.drain()
    l_all.step(3)

    @pl.when(teacher)
    def _():
        gate_copy(1).wait_recv()

    l_all.last_split()
    l_all.last_whole()
    l_all.wait_pair()

    for b in halves:
        lin_share(b).wait_send()

    @pl.when(z != mp)
    def _():
        target_copy().wait_send()

    @pl.when(student)
    def _():
        k_sum.drain()
        ks_sum.drain()
        l_all.drain()
        err_share().wait_send()
        err_store().wait()
        kx_copy().wait_send()
        for i in (0, 1):
            up_store(i).wait()
            gate_copy(i).wait_send()
            for way in (0, 1):
                gate_next(way, i).wait_send()
        for copy in hid_shares():
            copy.wait_send()
        for copy in hid_stores():
            copy.wait()

    @pl.when(teacher)
    def _():
        l_all.drain(2)
        err_partner().wait_send()
        err_share().wait_recv()
        for copy in hid_shares():
            copy.wait_recv()

    for b in halves:
        lin_arrival(b).wait_recv()
    for store in stores:
        store.wait()


def exchange(tokens, w, down, linear):
    def vmem(*shape, dtype=BF16):
        return pltpu.VMEM(shape, dtype)

    def sems(*shape):
        return pltpu.SemaphoreType.DMA(shape)

    def array(*shape, dtype=BF16):
        return jax.ShapeDtypeStruct(shape, dtype)

    def total_tiles():
        return [vmem(8, 8, 128, dtype=F32)] * 2 + [vmem(8, 128, dtype=F32)] * 4

    anywhere = pl.BlockSpec(memory_space=pl.ANY)
    return pl.pallas_call(
        exchange_kernel,
        out_shape=[
            array(2, Z, ROWS, QUARTER),
            array(Z, ROWS, WHOLE),
            array(Z, 2, ROWS, SPLIT),
            array(Z, ROWS, UNITS),
            array(2, Z, ROWS, QUARTER),
            array(Z, ROWS, LIN),
            array(8, 128, dtype=F32),
        ],
        in_specs=[anywhere] * 4,
        out_specs=[anywhere] * 7,
        scratch_shapes=[
            vmem(2, Z, ROWS, QUARTER), vmem(WIDTH, 2 * UNITS), vmem(UNITS, WIDTH), vmem(2, WIDTH, QUARTER), vmem(WIDTH, UNITS),
            vmem(2, Z, ROWS, WHOLE, dtype=F32), vmem(2, 4, 2, ROWS, WHOLE), vmem(2, 4, 2, ROWS, WHOLE),
            vmem(2, ROWS, WHOLE), vmem(2, ROWS, WHOLE), vmem(2, ROWS, WHOLE, dtype=F32), vmem(Z, ROWS, WHOLE),
            vmem(2, 2, Z, ROWS, SPLIT, dtype=F32), vmem(2, 4, 2, ROWS, SPLIT), vmem(2, 4, 2, ROWS, SPLIT),
            vmem(Z, 2, ROWS, SPLIT), vmem(Z, 2, ROWS, SPLIT), vmem(2, ROWS, SPLIT, dtype=F32), vmem(Z, 2, ROWS, SPLIT),
            vmem(Z * ROWS, WIDTH, dtype=F32), vmem(2, 8, ROWS, QUARTER), vmem(2, 8, ROWS, QUARTER),
            vmem(2, 8, ROWS, QUARTER), vmem(ROWS, QUARTER), vmem(ROWS, QUARTER),
            vmem(2, Z, ROWS, QUARTER, dtype=F32), vmem(2, 4, 2, ROWS, QUARTER), vmem(2, 4, 2, ROWS, QUARTER),
            vmem(ROWS, QUARTER), vmem(ROWS, QUARTER), vmem(Z, 2, ROWS, QUARTER),
            vmem(2, 4, ROWS, WHOLE), vmem(2, 4, ROWS, WHOLE), vmem(ROWS, WHOLE), vmem(ROWS, WHOLE),
            vmem(ROWS, WHOLE), vmem(ROWS, WHOLE),
            vmem(2, 4, ROWS, SPLIT), vmem(2, 4, ROWS, SPLIT), vmem(Z, ROWS, SPLIT), vmem(Z, ROWS, SPLIT),
            vmem(ROWS, SPLIT), vmem(ROWS, SPLIT),
            *total_tiles(), vmem(8, 128, dtype=F32),
            sems(6), sems(13),
            sems(7), sems(7), sems(7), sems(7), sems(2, 4, 2), sems(2, 4, 2), sems(3), sems(3),
            sems(2, 4, 2), sems(2, 4, 2), sems(8), sems(8),
            sems(2, 4), sems(2, 4), sems(2, 4), sems(2, 4), sems(8), sems(8),
            sems(2, 7), sems(2, 7), sems(4), sems(4), sems(7), sems(2, 7), sems(2, 4, 2), sems(2, 4, 2),
            sems(2, 4), sems(2, 4), sems(2, 4), sems(2, 4), sems(8), sems(8),
            sems(2, 4, 2), sems(2, 4, 2), sems(1), sems(1),
            sems(2, 4), sems(2, 4), sems(2, 4), sems(2, 4), sems(8), sems(8), sems(2), sems(2), sems(2, 2),
            sems(7), sems(7), sems(7), sems(7), sems(2), sems(2),
            sems(8), sems(8),
        ],
        compiler_params=pltpu.CompilerParams(
            collective_id=0, has_side_effects=True, vmem_limit_bytes=36 * 1024 * 1024
        ),
        name="exchange",
    )(tokens, w, down, linear)


def contract_rows(left, right):
    return lax.dot_general(left, right, (((0,), (0,)), ((), ())), preferred_element_type=F32)


BLOCK = 256


def gradients_kernel(
    tok, cot, s_cot, hid, err, lin_err, stat, unit_out, down_out, linear_out, losses, turned, unit, down, linear, sem
):
    factor = (16.0 * MODEL) / stat[0:1, 0:1]
    share = stat[...] / stat[0:1, 0:1]
    losses[0] = share[1, 0]
    losses[1] = share[2, 0]
    for b in (0, 1):
        turned[b * QUARTER : (b + 1) * QUARTER] = tok[b].T
    copies = []

    def send(here, there):
        copies.append(pltpu.make_async_copy(here, there, sem.at[len(copies)]))
        copies[-1].start()

    for i in range(UNITS // BLOCK):
        part = slice(i * BLOCK, (i + 1) * BLOCK)
        split, column = divmod(i * BLOCK - WHOLE, SPLIT)
        if split < 0:
            columns = cot[:, part]
        else:
            columns = s_cot[:, split, :, column : column + BLOCK].reshape(Z * ROWS, BLOCK)
        unit[:, part] = jnp.dot(turned[...], columns, preferred_element_type=F32).astype(BF16)
        send(unit.at[:, part], unit_out.at[:, part])
        for b in (0, 1):
            down[part, b * QUARTER : (b + 1) * QUARTER] = (factor * contract_rows(hid[:, part], err[b])).astype(BF16)
        send(down.at[part], down_out.at[part])
        if i < LIN // BLOCK:
            product = jnp.dot(turned[...], lin_err[:, part], preferred_element_type=F32)
            linear[:, part] = (factor * product).astype(BF16)
            send(linear.at[:, part], linear_out.at[:, part])
    for copy in copies:
        copy.wait()


def gradients(tok, cot, s_cot, hid, err, lin_err, stat):
    shapes = [(WIDTH, UNITS), (UNITS, WIDTH), (WIDTH, LIN)]
    return pl.pallas_call(
        gradients_kernel,
        out_shape=[jax.ShapeDtypeStruct(shape, BF16) for shape in shapes] + [jax.ShapeDtypeStruct((2,), F32)],
        in_specs=[pl.BlockSpec(memory_space=pltpu.VMEM)] * 7,
        out_specs=[pl.BlockSpec(memory_space=pl.ANY)] * 3 + [pl.BlockSpec(memory_space=pltpu.SMEM)],
        scratch_shapes=[
            pltpu.VMEM((WIDTH, Z * ROWS), BF16),
            *[pltpu.VMEM(shape, BF16) for shape in shapes],
            pltpu.SemaphoreType.DMA((2 * (UNITS // BLOCK) + LIN // BLOCK,)),
        ],
        compiler_params=pltpu.CompilerParams(vmem_limit_bytes=24 * 1024 * 1024),
        name="gradients",
    )(tok, cot, s_cot, hid, err, lin_err, stat)


def body(tokens, gate_up, down, linear):
    w = gate_up.reshape(WIDTH, 2 * UNITS)
    tok, cot, s_cot, hid, err, lin_err, stat = exchange(tokens, w, down[0], linear)
    rows = Z * ROWS
    unit_grad, down_grad, linear_grad, losses = gradients(
        tok.reshape(2, rows, QUARTER),
        cot.reshape(rows, WHOLE),
        s_cot,
        hid.reshape(rows, UNITS),
        err.reshape(2, rows, QUARTER),
        lin_err.reshape(rows, LIN),
        stat,
    )
    return (unit_grad[None], down_grad, linear_grad, losses)


def solution(mesh):
    return jax.shard_map(
        body,
        mesh=mesh,
        in_specs=(P("mp", "dp"), P("role", "dp", None, "mp"), P("role", "mp", "dp"), P("dp", "mp")),
        out_specs=(P("role", "dp", "mp"), P("mp", "dp"), P("dp", "mp"), P()),
        check_vma=False,
    )
```

```python
import jax
import jax.numpy as jnp
from jax import lax
from jax.experimental import pallas as pl
from jax.experimental.pallas import tpu as pltpu
from jax.sharding import PartitionSpec as P

MESH = pl.DeviceIdType.MESH
BF16, F32 = jnp.bfloat16, jnp.float32
MODEL = 8192
Z = 8
ROWS = 48
WIDTH = 512
UNITS = 1792
WHOLE = 768
SPLIT = 512
LIN = 1024
QUARTER = LIN // 4


def remote(src, dst, send, recv, device):
    return pltpu.make_async_remote_copy(
        src_ref=src, dst_ref=dst, send_sem=send, recv_sem=recv, device_id=device, device_id_type=MESH
    )


class RingSum:
    def __init__(self, place, part, out, into, send, recv, tags, long_way):
        self.place, self.part, self.out, self.into = place, part, out, into
        self.send, self.recv, self.tags, self.long_way = send, recv, tags, long_way

    def copy(self, way, step, tag):
        at = (way, step - 1) + tag
        return remote(
            self.out.at[at], self.into.at[at], self.send.at[at], self.recv.at[at], self.place.z_next[way]
        )

    def push(self, way, step, tag, first):
        sign = 1 - 2 * way
        total = self.local(tag, sign * (5 - step))
        if not first:
            self.copy(way, step - 1, tag).wait_recv()
            total = total + self.into[(way, step - 2) + tag].astype(F32)
        self.out[(way, step - 1) + tag] = total.astype(BF16)
        self.copy(way, step, tag).start()

    def local(self, tag, offset):
        return self.part[tag + (lax.rem(self.place.z + offset + Z, Z),)]

    def begin(self, tag, both=True):
        far = self.long_way(tag)
        self.push(far, 1, tag, True)
        if both:
            self.push(1 - far, 2, tag, True)

    def step(self, step, both=False):
        for tag in self.tags:
            for way in (0, 1):
                if step > 2 or way == self.long_way(tag):
                    self.push(way, step, tag, False)
                elif both:
                    self.push(way, step, tag, True)

    def result(self, tag):
        total = self.local(tag, 0)
        for way in (0, 1):
            self.copy(way, 4, tag).wait_recv()
            total = total + self.into[(way, 3) + tag].astype(F32)
        return total

    def drain(self):
        for tag in self.tags:
            for way in (0, 1):
                for step in range(1 if way == self.long_way(tag) else 2, 5):
                    self.copy(way, step, tag).wait_send()


class RingGather:
    def __init__(self, place, buf, send, recv, x_send, x_recv):
        self.place, self.buf, self.send, self.recv = place, buf, send, recv
        self.x_send, self.x_recv = x_send, x_recv

    def copy(self, way, step, mine, arriving=False):
        place = self.place
        sign = 1 - 2 * way
        block = lax.rem(place.z - sign * (step if arriving else step - 1) + Z, Z)
        x = place.x if mine else 1 - place.x
        part = self.buf.at[block, x]
        at = (way, step - 1, mine)
        return remote(part, part, self.send.at[at], self.recv.at[at], place.z_next[way])

    def x_copy(self, arriving=False):
        place = self.place
        part = self.buf.at[place.z, 1 - place.x if arriving else place.x]
        return remote(part, part, self.x_send, self.x_recv, place.x_other)

    def begin(self):
        self.copy(0, 1, 1).start()
        self.copy(1, 1, 1).start()
        self.x_copy().start()

    def begin_other(self):
        self.x_copy(True).wait_recv()
        self.copy(0, 1, 0).start()
        self.copy(1, 1, 0).start()

    def step(self, step):
        for mine in (1, 0):
            for way in (0, 1):
                self.copy(way, step, mine, True).wait_recv()
                if step < 3 or way == 1 - mine:
                    self.copy(way, step + 1, mine).start()

    def last(self):
        for mine in (1, 0):
            self.copy(1 - mine, 4, mine, True).wait_recv()

    def drain(self):
        self.x_copy().wait_send()
        for mine in (1, 0):
            for way in (0, 1):
                for step in range(1, 5 if way == 1 - mine else 4):
                    self.copy(way, step, mine).wait_send()


class PairRingSum(RingSum):
    def pair(self, other, x_out, x_into, x_send, x_recv):
        self.other, self.x_out, self.x_into, self.x_send, self.x_recv = other, x_out, x_into, x_send, x_recv
        self.got = set()

    def block(self, offset):
        return lax.rem(self.place.z + offset, Z)

    def x_copy(self, offset):
        block = self.block(offset)
        return remote(
            self.x_out.at[block], self.x_into.at[block], self.x_send.at[offset], self.x_recv.at[offset], self.place.x_other
        )

    def exchange(self, offsets):
        for offset in offsets:
            block = self.block(offset)
            for tag in self.tags:
                self.x_out[(block,) + tag] = self.other[tag + (block,)].astype(BF16)
            self.x_copy(offset).start()

    def local(self, tag, offset):
        offset = offset % Z
        if offset not in self.got:
            self.got.add(offset)
            self.x_copy(offset).wait_recv()
        block = self.block(offset)
        return self.part[tag + (block,)] + self.x_into[(block,) + tag].astype(F32)

    def drain(self):
        super().drain()
        for offset in range(Z):
            self.x_copy(offset).wait_send()


class Gather:
    def __init__(self, place, whole, split, w_send, w_recv, s_send, s_recv, x_send, x_recv):
        self.place, self.whole, self.split = place, whole, split
        self.w_send, self.w_recv, self.s_send, self.s_recv = w_send, w_recv, s_send, s_recv
        self.x_send, self.x_recv = x_send, x_recv

    def block(self, way, steps):
        return lax.rem(self.place.z - (1 - 2 * way) * steps + Z, Z)

    def w_copy(self, way, step, arriving=False, source=None):
        part = self.whole.at[self.block(way, step if arriving else step - 1)]
        if step == 4:
            part = part.at[:, way * WHOLE // 2 : (way + 1) * WHOLE // 2]
        at = (way, step - 1)
        return remote(part if source is None else source, part, self.w_send.at[at], self.w_recv.at[at], self.place.z_next[way])

    def s_copy(self, way, step, arriving=False, source=None):
        part = self.split.at[self.block(way, step if arriving else step - 1), self.place.x]
        at = (way, step - 1)
        return remote(part if source is None else source, part, self.s_send.at[at], self.s_recv.at[at], self.place.z_next[way])

    def x_copy(self, way, steps, arriving=False, source=None):
        part = self.split.at[self.block(way, steps), 1 - self.place.x if arriving else self.place.x]
        at = steps + 3 * way if steps else 0
        return remote(
            part if source is None else source, part, self.x_send.at[at], self.x_recv.at[at], self.place.x_other
        )

    def begin_split(self, source=None):
        for way in (0, 1):
            self.s_copy(way, 1, source=source).start()
        self.x_copy(0, 0, source=source).start()

    def begin_whole(self, source=None):
        for way in (0, 1):
            self.w_copy(way, 1, source=source).start()

    def step(self, step):
        for way in (0, 1):
            self.s_copy(way, step, True).wait_recv()
            if step < 3 or way == 1:
                self.s_copy(way, step + 1).start()
            self.x_copy(way, step).start()
        for way in (0, 1):
            self.w_copy(way, step, True).wait_recv()
            self.w_copy(way, step + 1).start()

    def last_split(self):
        self.s_copy(1, 4, True).wait_recv()
        self.x_copy(1, 4).start()

    def last_whole(self):
        for way in (0, 1):
            self.w_copy(way, 4, True).wait_recv()

    def crossings(self):
        return [(0, 0)] + [(way, steps) for steps in (1, 2, 3) for way in (0, 1)] + [(1, 4)]

    def wait_pair(self):
        for way, steps in self.crossings():
            self.x_copy(way, steps, True).wait_recv()

    def drain(self, first=1):
        for way in (0, 1):
            for step in range(first, 5):
                self.w_copy(way, step).wait_send()
                if step < 4 or way == 1:
                    self.s_copy(way, step).wait_send()
        for way, steps in self.crossings():
            self.x_copy(way, steps).wait_send()


class Direct:
    def __init__(self, me, device_of, out, into, send, recv):
        self.me, self.device_of, self.out, self.into, self.send, self.recv = me, device_of, out, into, send, recv

    def copy(self, apart):
        peer = lax.rem(self.me + apart, 8)
        return remote(
            self.out(peer), self.into(self.me), self.send.at[apart - 1], self.recv.at[apart - 1], self.device_of(peer)
        )

    def start(self):
        for apart in (4, 3, 5, 2, 6, 1, 7):
            self.copy(apart).start()

    def wait_one(self, apart):
        source = lax.rem(self.me - apart + 8, 8)
        part = self.into(source)
        remote(part, part, self.send.at[apart - 1], self.recv.at[apart - 1], self.device_of(source)).wait_recv()

    def wait(self):
        for apart in (1, 7, 2, 6, 3, 5, 4):
            self.wait_one(apart)

    def drain(self):
        for apart in range(1, 8):
            self.copy(apart).wait_send()


class Total:
    def __init__(self, place, m, zs, x, x_got, r, r_got, m_s, m_r, z_s, z_r, one_s, one_r):
        self.place, self.m, self.zs, self.x, self.x_got, self.r, self.r_got = place, m, zs, x, x_got, r, r_got
        self.m_all = Direct(place.mp, place.of_mp, lambda peer: m.at[place.mp], lambda source: m.at[source], m_s, m_r)
        self.z_all = Direct(place.z, place.of_z, lambda peer: zs.at[place.z], lambda source: zs.at[source], z_s, z_r)
        self.one_s, self.one_r = one_s, one_r

    def x_copy(self):
        return remote(self.x, self.x_got, self.one_s.at[0], self.one_r.at[0], self.place.x_other)

    def r_copy(self):
        return remote(self.r, self.r_got, self.one_s.at[1], self.one_r.at[1], self.place.partner)

    def in_order(self, slots):
        total = slots[0]
        for source in range(1, 8):
            total = total + slots[source]
        return total

    def start(self, tile):
        self.m[self.place.mp] = tile
        self.m_all.start()

    def over_x(self):
        self.m_all.wait()
        self.x[...] = self.in_order(self.m)
        self.x_copy().start()

    def over_z(self):
        self.x_copy().wait_recv()
        self.zs[self.place.z] = self.x[...] + self.x_got[...]
        self.z_all.start()

    def over_role(self):
        self.z_all.wait()
        self.r[...] = self.in_order(self.zs)
        self.r_copy().start()

    def result(self):
        self.r_copy().wait_recv()
        return self.r[...] + self.r_got[...]

    def drain(self):
        self.m_all.drain()
        self.x_copy().wait_send()
        self.z_all.drain()
        self.r_copy().wait_send()


class Place:
    def __init__(self):
        self.role, self.mp, self.dp = lax.axis_index("role"), lax.axis_index("mp"), lax.axis_index("dp")
        dp = self.dp
        self.z, self.x = dp // 2, lax.rem(dp, 2)
        role, mp, z, x = self.role, self.mp, self.z, self.x
        up, down = lax.rem(z + 1, Z) * 2 + x, lax.rem(z + Z - 1, Z) * 2 + x
        self.z_next = ((role, up, mp), (role, down, mp))
        self.z_next_cross = ((1 - role, up, mp), (1 - role, down, mp))
        self.x_other = (role, z * 2 + 1 - x, mp)
        self.partner = (1 - role, dp, mp)
        self.across = (role, mp * 2 + x, z)
        self.of_z = lambda peer: (role, peer * 2 + x, mp)
        self.of_mp = lambda peer: (role, dp, peer)


def exchange_kernel(
    tok_in, w_in, down_in, lin_in,
    tok_out, cot, s_cot, down_out, linear_out, stat_out,
    tok, w, down, lin, down_turned, hid_out, err_out, lin_out, down_grad, linear_grad,
    part, b_out, b_into, bx_out, bx_into, pre, hid,
    s_part, s_out, s_into, sx_out, sx_into, s_pre, s_hid,
    d_part, d_out, d_into, err, target_out, target,
    lin_part, e_out, e_into, ex_out, ex_into, lin_err,
    k_out, k_into, kx_out, kx_into, gate_out, up_out,
    ks_out, ks_into, ksx_out, ksx_into, s_gate_out, s_up_out,
    m1, z1, x1, x1_got, r1, r1_got, stat,
    load_sem, store_sem,
    tok_s, tok_r, hand_s, hand_r, b_s, b_r, bx_s, bx_r, s_s, s_r, sx_s, sx_r,
    c_s, c_r, cs_s, cs_r, cx_s, cx_r,
    d_s, d_r, one_s, one_r, i_s, i_r, e_s, e_r, k_s, k_r, ks_s, ks_r, ksx_s, ksx_r,
    j_s, j_r, jx_s, jx_r, l_s, l_r, ls_s, ls_r, lx_s, lx_r, g_s, g_r, gn_s,
    m1_s, m1_r, z1_s, z1_r, o1_s, o1_r,
    share_s, share_r,
):
    place = Place()
    role, mp, dp, z, x = place.role, place.mp, place.dp, place.z, place.x
    student, teacher = role == 1, role == 0
    x_of = (1 - x, x)
    halves = (0, 1)

    loads = [
        pltpu.make_async_copy(tok_in.at[:, b * QUARTER : (b + 1) * QUARTER], tok.at[b, mp], load_sem.at[b])
        for b in halves
    ]
    loads += [
        pltpu.make_async_copy(w_in, w, load_sem.at[2]),
        pltpu.make_async_copy(down_in, down, load_sem.at[3]),
    ]
    loads += [
        pltpu.make_async_copy(
            lin_in.at[:, pl.ds(pl.multiple_of(b * 2 * QUARTER + role * QUARTER, QUARTER), QUARTER)],
            lin.at[b],
            load_sem.at[4 + b],
        )
        for b in halves
    ]
    for load in loads:
        load.start()

    barrier = pltpu.get_barrier_semaphore()

    def greet(device):
        pl.semaphore_signal(barrier, inc=1, device_id=device, device_id_type=MESH)

    for apart in range(1, 8):
        greet(place.of_mp(lax.rem(mp + apart, 8)))
        greet((1 - role, dp, lax.rem(mp + apart, 8)))
        greet(place.of_z(lax.rem(z + apart, 8)))
    greet(place.x_other)
    greet(place.partner)
    for way in (0, 1):
        greet(place.z_next_cross[way])

    @pl.when(z != mp)
    def _():
        greet(place.across)
        pl.semaphore_wait(barrier, 26)

    @pl.when(z == mp)
    def _():
        pl.semaphore_wait(barrier, 25)

    for load in loads[:2]:
        load.wait()
    tokens = Direct(mp, place.of_mp, lambda peer: tok.at[role, mp], lambda source: tok.at[role, source], tok_s, tok_r)
    tokens.start()

    def hand(apart, arriving=False):
        source = lax.rem(mp - apart + 8, 8)
        part_of = tok.at[1 - role if arriving else role, source]
        return remote(part_of, part_of, hand_s.at[apart - 1], hand_r.at[apart - 1], place.partner)

    for apart in (1, 7, 2, 6, 3, 5, 4):
        tokens.wait_one(apart)
        hand(apart).start()
    loads[2].wait()
    for apart in (1, 7, 2, 6, 3, 5, 4):
        hand(apart, True).wait_recv()
    stores = [pltpu.make_async_copy(tok, tok_out, store_sem.at[0])]
    stores[0].start()

    def all_tokens():
        return jnp.concatenate([tok[b].reshape(Z * ROWS, QUARTER) for b in halves], axis=1)

    tags = [(0,), (1,)]
    b_sum = RingSum(place, part, b_out, b_into, b_s, b_r, tags, lambda tag: tag[0])
    s_sum = PairRingSum(place, s_part.at[1], s_out, s_into, s_s, s_r, tags, lambda tag: tag[0])
    s_sum.pair(s_part.at[0], sx_out, sx_into, sx_s, sx_r)

    def split_dot(q):
        for g in (0, 1):
            column = pl.multiple_of(g * UNITS + WHOLE + x_of[q] * SPLIT, 128)
            s_part[q, g] = jnp.dot(
                all_tokens(), w[:, pl.ds(column, SPLIT)], preferred_element_type=F32
            ).reshape(Z, ROWS, SPLIT)

    split_dot(0)
    s_sum.exchange((4,))
    for g in (0, 1):
        part[g] = jnp.dot(
            all_tokens(), w[:, g * UNITS : g * UNITS + WHOLE], preferred_element_type=F32
        ).reshape(Z, ROWS, WHOLE)
        b_sum.begin((g,))
        if g == 0:
            s_sum.exchange((3, 5))
    split_dot(1)
    for tag in tags:
        s_sum.begin(tag, False)
    b_sum.step(2)
    s_sum.exchange((2, 6))
    for load in loads[3:]:
        load.wait()
    for q in (0, 1):
        lin_part[q] = jnp.dot(all_tokens(), lin[x_of[q]], preferred_element_type=F32).reshape(Z, ROWS, QUARTER)
    s_sum.step(2, True)
    b_sum.step(3)
    s_sum.exchange((1, 7, 0))
    for c in range(UNITS // QUARTER):
        down_turned[:, c * QUARTER : (c + 1) * QUARTER] = down[c * QUARTER : (c + 1) * QUARTER].T
    s_sum.step(3)
    b_sum.step(4)
    s_sum.step(4)

    def bx_copy(g):
        return remote(bx_out.at[g], bx_into.at[g], bx_s.at[g], bx_r.at[g], place.x_other)

    for g in (0, 1):
        bx_out[g] = b_sum.result((g,)).astype(BF16)
        bx_copy(g).start()

    def hidden(inputs):
        return (inputs[0] * jax.nn.sigmoid(inputs[0]) * inputs[1]).astype(BF16)

    c_all = Gather(place, hid, s_hid, c_s, c_r, cs_s, cs_r, cx_s, cx_r)
    for g in (0, 1):
        s_pre[g] = s_sum.result((g,))
    s_hid[z, x] = hidden(s_pre)
    c_all.begin_split()
    for g in (0, 1):
        bx_copy(g).wait_recv()
        pre[g] = bx_out[g].astype(F32) + bx_into[g].astype(F32)
    hid[z] = hidden(pre)
    c_all.begin_whole()
    e_sum = RingSum(place, lin_part, e_out, e_into, e_s, e_r, [(0,), (1,)], lambda tag: tag[0])
    for tag in e_sum.tags:
        e_sum.begin(tag)
    for step in (1, 2, 3):
        c_all.step(step)
        e_sum.step(step + 1)

    c_all.last_split()
    c_all.last_whole()
    d_part[...] = jnp.dot(hid[...].reshape(Z * ROWS, WHOLE), down[:WHOLE], preferred_element_type=F32)
    c_all.wait_pair()

    def d_copy(b, apart):
        peer = lax.rem(mp + apart, 8)
        return remote(
            d_out.at[b, peer], d_into.at[role, mp], d_s.at[b, apart - 1], d_r.at[role, apart - 1], (b, dp, peer)
        )

    def d_arrival(source_role, apart):
        source = lax.rem(mp - apart + 8, 8)
        got = d_into.at[source_role, source]
        return remote(got, got, d_s.at[0, apart - 1], d_r.at[source_role, apart - 1], (source_role, dp, source))

    def d_partner(arriving=False):
        return remote(
            d_out.at[1 - role, mp],
            d_into.at[1 - role if arriving else role, mp],
            one_s.at[0],
            one_r.at[0],
            place.partner,
        )

    for b in halves:
        columns = slice(b * QUARTER, (b + 1) * QUARTER)
        total = d_part[:, columns] + jnp.dot(
            jnp.concatenate([s_hid[:, c].reshape(Z * ROWS, SPLIT) for c in halves], axis=1),
            down[WHOLE:, columns],
            preferred_element_type=F32,
        )
        d_out[b] = total.reshape(Z, ROWS, QUARTER).astype(BF16)
        for apart in (4, 3, 5, 2, 6, 1, 7):
            d_copy(b, apart).start()
    d_partner().start()
    d_into[role, mp] = d_out[role, mp]

    def ex_copy():
        return remote(ex_out, ex_into, one_s.at[3], one_r.at[3], place.x_other)

    ex_out[...] = e_sum.result((0,)).astype(BF16)
    ex_copy().start()
    linear_rows = e_sum.result((1,))
    tokens.drain()
    b_sum.drain()
    s_sum.drain()
    for apart in range(1, 8):
        hand(apart).wait_send()
    for g in (0, 1):
        bx_copy(g).wait_send()
    for apart in (1, 7, 2, 6, 3, 5, 4):
        for source_role in (0, 1):
            d_arrival(source_role, apart).wait_recv()
    d_partner(True).wait_recv()

    def summed(source_role):
        own = d_into[source_role, 0].astype(F32)
        for source in range(1, 8):
            own = own + d_into[source_role, source].astype(F32)
        return own.astype(BF16)

    teacher_rows = summed(0)
    error = summed(1).astype(F32) - teacher_rows.astype(F32)
    err[role, mp] = error.astype(BF16)

    def err_copy(apart):
        peer = lax.rem(mp + apart, 8)
        return remote(
            err.at[role, mp], err.at[role, mp], i_s.at[apart - 1], i_r.at[role, apart - 1], (1, dp, peer)
        )

    def err_arrival(source_role, apart):
        source = lax.rem(mp - apart + 8, 8)
        got = err.at[source_role, source]
        return remote(got, got, i_s.at[apart - 1], i_r.at[source_role, apart - 1], (source_role, dp, source))

    def err_partner():
        return remote(err.at[0, mp], err.at[0, mp], one_s.at[1], one_r.at[1], place.partner)

    for apart in (4, 3, 5, 2, 6, 1, 7):
        err_copy(apart).start()

    @pl.when(teacher)
    def _():
        err_partner().start()

    target_out[...] = teacher_rows

    def target_copy():
        return remote(target_out, target, one_s.at[2], one_r.at[2], place.across)

    @pl.when(z != mp)
    def _():
        target_copy().start()

    @pl.when(z == mp)
    def _():
        target[...] = target_out[...]

    k_sum = RingSum(place, part.at[0], k_out, k_into, k_s, k_r, [()], lambda tag: 0)
    ks_sum = PairRingSum(place, s_part.at[1, 0], ks_out, ks_into, ks_s, ks_r, [()], lambda tag: 1)
    ks_sum.pair(s_part.at[0, 0], ksx_out, ksx_into, ksx_s, ksx_r)

    def err_share():
        return remote(err, err_out, share_s.at[2], share_r.at[2], place.partner)

    def err_store():
        return pltpu.make_async_copy(err, err_out, store_sem.at[3])

    def parts_of(whole, split, out):
        yield whole, out.at[:, :, :WHOLE]
        for b in halves:
            yield split.at[:, b], out.at[:, :, WHOLE + b * SPLIT : WHOLE + (b + 1) * SPLIT]

    def hid_shares():
        return [
            remote(here, there, share_s.at[5 + i], share_r.at[5 + i], place.partner)
            for i, (here, there) in enumerate(parts_of(hid, s_hid, hid_out))
        ]

    def hid_stores():
        return [
            pltpu.make_async_copy(here, there, store_sem.at[7 + i])
            for i, (here, there) in enumerate(parts_of(hid, s_hid, hid_out))
        ]

    def cot_dot(start, size):
        all_err = jnp.concatenate([err[b].reshape(Z * ROWS, QUARTER) for b in halves], axis=1)
        return jnp.dot(all_err, down_turned[:, pl.ds(start, size)], preferred_element_type=F32).reshape(Z, ROWS, size)

    @pl.when(student)
    def _():
        for apart in (1, 7, 2, 6, 3, 5, 4):
            for source_role in (0, 1):
                err_arrival(source_role, apart).wait_recv()
        err_partner().wait_recv()
        s_part[0, 0] = cot_dot(pl.multiple_of(WHOLE + x_of[0] * SPLIT, 128), SPLIT)
        ks_sum.exchange((4,))
        part[0] = cot_dot(0, WHOLE)
        k_sum.begin(())
        ks_sum.exchange((3, 5))
        s_part[1, 0] = cot_dot(pl.multiple_of(WHOLE + x_of[1] * SPLIT, 128), SPLIT)
        ks_sum.exchange((2, 6, 1, 7, 0))

    ex_copy().wait_recv()

    @pl.when(z != mp)
    def _():
        target_copy().wait_recv()

    linear_error = linear_rows + ex_into[...].astype(F32) - target[...].astype(F32)
    lin_err[z, x] = linear_error.astype(BF16)
    j_all = RingGather(place, lin_err, j_s, j_r, jx_s.at[0], jx_r.at[0])
    j_all.begin()
    row = lax.broadcasted_iota(jnp.int32, (8, 128), 0)
    teacher_float = teacher_rows.astype(F32)
    norm = Total(place, m1, z1, x1, x1_got, r1, r1_got, m1_s, m1_r, z1_s, z1_r, o1_s, o1_r)
    target_square = jnp.sum(teacher_float * teacher_float)
    error_square = jnp.sum(error * error)
    linear_square = jnp.sum(linear_error * linear_error)
    norm.start(jnp.where(row == 0, target_square, jnp.where(row == 1, error_square, linear_square)))

    @pl.when(student)
    def _():
        ks_sum.begin((), False)
        k_sum.step(2)

    j_all.begin_other()
    norm.over_x()

    @pl.when(student)
    def _():
        ks_sum.step(2, True)
        k_sum.step(3)

    norm.over_z()
    j_all.step(1)

    @pl.when(student)
    def _():
        ks_sum.step(3)
        k_sum.step(4)
        ks_sum.step(4)
        err_share().start()
        err_store().start()
        for copy in hid_shares() + hid_stores():
            copy.start()

    norm.over_role()
    j_all.step(2)
    stat[...] = norm.result()
    stores.append(pltpu.make_async_copy(stat, stat_out, store_sem.at[4]))
    stores[-1].start()

    def kx_copy():
        return remote(kx_out, kx_into, bx_s.at[2], bx_r.at[2], place.x_other)

    def gate_copy(i):
        return remote(*((s_gate_out, s_cot.at[z, x]), (gate_out, cot.at[z]))[i], g_s.at[i], g_r.at[i], place.partner)

    def up_store(i):
        here, there = ((s_up_out, s_cot.at[z, x]), (up_out, cot.at[z]))[i]
        return pltpu.make_async_copy(here, there, store_sem.at[10 + i])

    l_all = Gather(place, cot, s_cot, l_s, l_r, ls_s, ls_r, lx_s, lx_r)

    def gate_next(way, i):
        ends = ((s_gate_out, s_cot.at[z, x]), (gate_out, cot.at[z]))[i]
        return remote(*ends, gn_s.at[way, i], (ls_r, l_r)[i].at[way, 0], place.z_next_cross[way])

    def cotangents(total, inputs):
        factor = (16.0 * MODEL) / stat[0:1, 0:1]
        hidden_cot = total * factor
        gate_pre, up_pre = inputs[0], inputs[1]
        sig = jax.nn.sigmoid(gate_pre)
        gate_cot = hidden_cot * up_pre * sig * (1.0 + gate_pre * (1.0 - sig))
        return gate_cot.astype(BF16), (hidden_cot * gate_pre * sig).astype(BF16)

    @pl.when(student)
    def _():
        kx_out[...] = k_sum.result(()).astype(BF16)
        kx_copy().start()
        s_gate_out[...], s_up_out[...] = cotangents(ks_sum.result(()), s_pre)
        for way in (0, 1):
            gate_next(way, 0).start()
        gate_copy(0).start()
        l_all.begin_split(s_up_out)
        up_store(0).start()
        kx_copy().wait_recv()
        gate_out[...], up_out[...] = cotangents(kx_out[...].astype(F32) + kx_into[...].astype(F32), pre)
        for way in (0, 1):
            gate_next(way, 1).start()
        l_all.begin_whole(up_out)
        up_store(1).start()
        gate_copy(1).start()

    @pl.when(teacher)
    def _():
        gate_copy(0).wait_recv()
        l_all.x_copy(0, 0).start()

    for apart in range(1, 8):
        err_copy(apart).wait_send()
        for b in halves:
            d_copy(b, apart).wait_send()
    d_partner().wait_send()
    j_all.step(3)
    l_all.step(1)
    j_all.last()

    def lin_columns(b):
        start = pl.multiple_of(b * 2 * QUARTER + role * QUARTER, QUARTER)
        return lin_out.at[:, :, pl.ds(start, QUARTER)]

    def lin_share(b):
        return remote(lin_err.at[:, b], lin_columns(b), share_s.at[3 + b], share_r.at[3 + b], place.partner)

    def lin_arrival(b):
        start = pl.multiple_of(b * 2 * QUARTER + (1 - role) * QUARTER, QUARTER)
        got = lin_out.at[:, :, pl.ds(start, QUARTER)]
        return remote(lin_err.at[:, b], got, share_s.at[3 + b], share_r.at[3 + b], place.partner)

    lin_stores = [pltpu.make_async_copy(lin_err.at[:, b], lin_columns(b), store_sem.at[5 + b]) for b in halves]
    for b in halves:
        lin_share(b).start()
        lin_stores[b].start()

    @pl.when(student)
    def _():
        err_store().wait()
        for copy in hid_stores():
            copy.wait()

    @pl.when(teacher)
    def _():
        err_share().wait_recv()
        for copy in hid_shares():
            copy.wait_recv()

    factor = (16.0 * MODEL) / stat[0:1, 0:1]

    def rows_of(ref, c):
        return ref[:, :, c * QUARTER : (c + 1) * QUARTER].reshape(Z * ROWS, QUARTER)

    def down_piece(c):
        for b in halves:
            product = contract_rows(rows_of(hid_out, c), err_out[b].reshape(Z * ROWS, QUARTER))
            down_grad[c * QUARTER : (c + 1) * QUARTER, b * QUARTER : (b + 1) * QUARTER] = (factor * product).astype(BF16)

    def linear_piece(c):
        for b in halves:
            product = contract_rows(tok[b].reshape(Z * ROWS, QUARTER), rows_of(lin_out, c))
            linear_grad[b * QUARTER : (b + 1) * QUARTER, c * QUARTER : (c + 1) * QUARTER] = (factor * product).astype(BF16)

    for c in range(4):
        down_piece(c)
    c_all.drain()
    e_sum.drain()
    l_all.step(2)
    for c in range(4, UNITS // QUARTER):
        down_piece(c)
    stores.append(pltpu.make_async_copy(down_grad, down_out, store_sem.at[12]))
    stores[-1].start()
    ex_copy().wait_send()
    norm.drain()
    j_all.drain()
    l_all.step(3)
    for b in halves:
        lin_arrival(b).wait_recv()
        lin_stores[b].wait()
    for c in range(LIN // QUARTER):
        linear_piece(c)
    stores.append(pltpu.make_async_copy(linear_grad, linear_out, store_sem.at[13]))
    stores[-1].start()

    @pl.when(teacher)
    def _():
        gate_copy(1).wait_recv()

    l_all.last_split()
    l_all.last_whole()
    l_all.wait_pair()

    for b in halves:
        lin_share(b).wait_send()

    @pl.when(z != mp)
    def _():
        target_copy().wait_send()

    @pl.when(student)
    def _():
        k_sum.drain()
        ks_sum.drain()
        l_all.drain()
        err_share().wait_send()
        kx_copy().wait_send()
        for i in (0, 1):
            up_store(i).wait()
            gate_copy(i).wait_send()
            for way in (0, 1):
                gate_next(way, i).wait_send()
        for copy in hid_shares():
            copy.wait_send()

    @pl.when(teacher)
    def _():
        l_all.drain(2)
        err_partner().wait_send()

    for store in stores:
        store.wait()


def exchange(tokens, w, down, linear):
    def vmem(*shape, dtype=BF16):
        return pltpu.VMEM(shape, dtype)

    def sems(*shape):
        return pltpu.SemaphoreType.DMA(shape)

    def array(*shape, dtype=BF16):
        return jax.ShapeDtypeStruct(shape, dtype)

    def total_tiles():
        return [vmem(8, 8, 128, dtype=F32)] * 2 + [vmem(8, 128, dtype=F32)] * 4

    anywhere = pl.BlockSpec(memory_space=pl.ANY)
    return pl.pallas_call(
        exchange_kernel,
        out_shape=[
            array(2, Z, ROWS, QUARTER),
            array(Z, ROWS, WHOLE),
            array(Z, 2, ROWS, SPLIT),
            array(UNITS, WIDTH),
            array(WIDTH, LIN),
            array(8, 128, dtype=F32),
        ],
        in_specs=[anywhere] * 4,
        out_specs=[anywhere] * 6,
        scratch_shapes=[
            vmem(2, Z, ROWS, QUARTER), vmem(WIDTH, 2 * UNITS), vmem(UNITS, WIDTH), vmem(2, WIDTH, QUARTER), vmem(WIDTH, UNITS),
            vmem(Z, ROWS, UNITS), vmem(2, Z, ROWS, QUARTER), vmem(Z, ROWS, LIN), vmem(UNITS, WIDTH), vmem(WIDTH, LIN),
            vmem(2, Z, ROWS, WHOLE, dtype=F32), vmem(2, 4, 2, ROWS, WHOLE), vmem(2, 4, 2, ROWS, WHOLE),
            vmem(2, ROWS, WHOLE), vmem(2, ROWS, WHOLE), vmem(2, ROWS, WHOLE, dtype=F32), vmem(Z, ROWS, WHOLE),
            vmem(2, 2, Z, ROWS, SPLIT, dtype=F32), vmem(2, 4, 2, ROWS, SPLIT), vmem(2, 4, 2, ROWS, SPLIT),
            vmem(Z, 2, ROWS, SPLIT), vmem(Z, 2, ROWS, SPLIT), vmem(2, ROWS, SPLIT, dtype=F32), vmem(Z, 2, ROWS, SPLIT),
            vmem(Z * ROWS, WIDTH, dtype=F32), vmem(2, 8, ROWS, QUARTER), vmem(2, 8, ROWS, QUARTER),
            vmem(2, 8, ROWS, QUARTER), vmem(ROWS, QUARTER), vmem(ROWS, QUARTER),
            vmem(2, Z, ROWS, QUARTER, dtype=F32), vmem(2, 4, 2, ROWS, QUARTER), vmem(2, 4, 2, ROWS, QUARTER),
            vmem(ROWS, QUARTER), vmem(ROWS, QUARTER), vmem(Z, 2, ROWS, QUARTER),
            vmem(2, 4, ROWS, WHOLE), vmem(2, 4, ROWS, WHOLE), vmem(ROWS, WHOLE), vmem(ROWS, WHOLE),
            vmem(ROWS, WHOLE), vmem(ROWS, WHOLE),
            vmem(2, 4, ROWS, SPLIT), vmem(2, 4, ROWS, SPLIT), vmem(Z, ROWS, SPLIT), vmem(Z, ROWS, SPLIT),
            vmem(ROWS, SPLIT), vmem(ROWS, SPLIT),
            *total_tiles(), vmem(8, 128, dtype=F32),
            sems(6), sems(14),
            sems(7), sems(7), sems(7), sems(7), sems(2, 4, 2), sems(2, 4, 2), sems(3), sems(3),
            sems(2, 4, 2), sems(2, 4, 2), sems(8), sems(8),
            sems(2, 4), sems(2, 4), sems(2, 4), sems(2, 4), sems(8), sems(8),
            sems(2, 7), sems(2, 7), sems(4), sems(4), sems(7), sems(2, 7), sems(2, 4, 2), sems(2, 4, 2),
            sems(2, 4), sems(2, 4), sems(2, 4), sems(2, 4), sems(8), sems(8),
            sems(2, 4, 2), sems(2, 4, 2), sems(1), sems(1),
            sems(2, 4), sems(2, 4), sems(2, 4), sems(2, 4), sems(8), sems(8), sems(2), sems(2), sems(2, 2),
            sems(7), sems(7), sems(7), sems(7), sems(2), sems(2),
            sems(8), sems(8),
        ],
        compiler_params=pltpu.CompilerParams(
            collective_id=0, has_side_effects=True, vmem_limit_bytes=42 * 1024 * 1024
        ),
        name="exchange",
    )(tokens, w, down, linear)


def contract_rows(left, right):
    return lax.dot_general(left, right, (((0,), (0,)), ((), ())), preferred_element_type=F32)


BLOCK = 256


def gradients_kernel(
    tok, cot, s_cot, stat, down, linear, unit_out, down_out, linear_out, losses, turned, unit, sem
):
    copies = []

    def send(here, there):
        copies.append(pltpu.make_async_copy(here, there, sem.at[len(copies)]))
        copies[-1].start()

    send(down, down_out)
    send(linear, linear_out)
    share = stat[...] / stat[0:1, 0:1]
    losses[0] = share[1, 0]
    losses[1] = share[2, 0]
    for b in (0, 1):
        turned[b * QUARTER : (b + 1) * QUARTER] = tok[b].T
    for i in range(UNITS // BLOCK):
        part = slice(i * BLOCK, (i + 1) * BLOCK)
        split, column = divmod(i * BLOCK - WHOLE, SPLIT)
        if split < 0:
            columns = cot[:, part]
        else:
            columns = s_cot[:, split, :, column : column + BLOCK].reshape(Z * ROWS, BLOCK)
        unit[:, part] = jnp.dot(turned[...], columns, preferred_element_type=F32).astype(BF16)
        send(unit.at[:, part], unit_out.at[:, part])
    for copy in copies:
        copy.wait()


def gradients(tok, cot, s_cot, stat, down, linear):
    shapes = [(WIDTH, UNITS), (UNITS, WIDTH), (WIDTH, LIN)]
    whole = pl.BlockSpec(memory_space=pltpu.VMEM)
    anywhere = pl.BlockSpec(memory_space=pl.ANY)
    return pl.pallas_call(
        gradients_kernel,
        out_shape=[jax.ShapeDtypeStruct(shape, BF16) for shape in shapes] + [jax.ShapeDtypeStruct((2,), F32)],
        in_specs=[whole] * 4 + [anywhere] * 2,
        out_specs=[anywhere] * 3 + [pl.BlockSpec(memory_space=pltpu.SMEM)],
        scratch_shapes=[
            pltpu.VMEM((WIDTH, Z * ROWS), BF16),
            pltpu.VMEM((WIDTH, UNITS), BF16),
            pltpu.SemaphoreType.DMA((2 + UNITS // BLOCK,)),
        ],
        compiler_params=pltpu.CompilerParams(vmem_limit_bytes=24 * 1024 * 1024),
        name="gradients",
    )(tok, cot, s_cot, stat, down, linear)


def body(tokens, gate_up, down, linear):
    w = gate_up.reshape(WIDTH, 2 * UNITS)
    tok, cot, s_cot, down_own, linear_own, stat = exchange(tokens, w, down[0], linear)
    rows = Z * ROWS
    unit_grad, down_grad, linear_grad, losses = gradients(
        tok.reshape(2, rows, QUARTER), cot.reshape(rows, WHOLE), s_cot, stat, down_own, linear_own
    )
    return (unit_grad[None], down_grad, linear_grad, losses)


def solution(mesh):
    return jax.shard_map(
        body,
        mesh=mesh,
        in_specs=(P("mp", "dp"), P("role", "dp", None, "mp"), P("role", "mp", "dp"), P("dp", "mp")),
        out_specs=(P("role", "dp", "mp"), P("mp", "dp"), P("dp", "mp"), P()),
        check_vma=False,
    )
```

```python
import jax
import jax.numpy as jnp
from jax import lax
from jax.experimental import pallas as pl
from jax.experimental.pallas import tpu as pltpu
from jax.sharding import PartitionSpec as P

MESH = pl.DeviceIdType.MESH
BF16, F32 = jnp.bfloat16, jnp.float32
MODEL = 8192
Z = 8
ROWS = 48
WIDTH = 512
UNITS = 1792
WHOLE = 768
SPLIT = 512
LIN = 1024
QUARTER = LIN // 4


def remote(src, dst, send, recv, device):
    return pltpu.make_async_remote_copy(
        src_ref=src, dst_ref=dst, send_sem=send, recv_sem=recv, device_id=device, device_id_type=MESH
    )


class RingSum:
    def __init__(self, place, part, out, into, send, recv, tags, long_way):
        self.place, self.part, self.out, self.into = place, part, out, into
        self.send, self.recv, self.tags, self.long_way = send, recv, tags, long_way

    def copy(self, way, step, tag):
        at = (way, step - 1) + tag
        return remote(
            self.out.at[at], self.into.at[at], self.send.at[at], self.recv.at[at], self.place.z_next[way]
        )

    def push(self, way, step, tag, first):
        sign = 1 - 2 * way
        total = self.local(tag, sign * (5 - step))
        if not first:
            self.copy(way, step - 1, tag).wait_recv()
            total = total + self.into[(way, step - 2) + tag].astype(F32)
        self.out[(way, step - 1) + tag] = total.astype(BF16)
        self.copy(way, step, tag).start()

    def local(self, tag, offset):
        return self.part[tag + (lax.rem(self.place.z + offset + Z, Z),)]

    def begin(self, tag, both=True):
        far = self.long_way(tag)
        self.push(far, 1, tag, True)
        if both:
            self.push(1 - far, 2, tag, True)

    def step(self, step, both=False):
        for tag in self.tags:
            for way in (0, 1):
                if step > 2 or way == self.long_way(tag):
                    self.push(way, step, tag, False)
                elif both:
                    self.push(way, step, tag, True)

    def result(self, tag):
        total = self.local(tag, 0)
        for way in (0, 1):
            self.copy(way, 4, tag).wait_recv()
            total = total + self.into[(way, 3) + tag].astype(F32)
        return total

    def drain(self):
        for tag in self.tags:
            for way in (0, 1):
                for step in range(1 if way == self.long_way(tag) else 2, 5):
                    self.copy(way, step, tag).wait_send()


class RingGather:
    def __init__(self, place, buf, send, recv, x_send, x_recv):
        self.place, self.buf, self.send, self.recv = place, buf, send, recv
        self.x_send, self.x_recv = x_send, x_recv

    def copy(self, way, step, mine, arriving=False):
        place = self.place
        sign = 1 - 2 * way
        block = lax.rem(place.z - sign * (step if arriving else step - 1) + Z, Z)
        x = place.x if mine else 1 - place.x
        part = self.buf.at[block, x]
        at = (way, step - 1, mine)
        return remote(part, part, self.send.at[at], self.recv.at[at], place.z_next[way])

    def x_copy(self, arriving=False):
        place = self.place
        part = self.buf.at[place.z, 1 - place.x if arriving else place.x]
        return remote(part, part, self.x_send, self.x_recv, place.x_other)

    def begin(self):
        self.copy(0, 1, 1).start()
        self.copy(1, 1, 1).start()
        self.x_copy().start()

    def begin_other(self):
        self.x_copy(True).wait_recv()
        self.copy(0, 1, 0).start()
        self.copy(1, 1, 0).start()

    def step(self, step):
        for mine in (1, 0):
            for way in (0, 1):
                self.copy(way, step, mine, True).wait_recv()
                if step < 3 or way == 1 - mine:
                    self.copy(way, step + 1, mine).start()

    def last(self):
        for mine in (1, 0):
            self.copy(1 - mine, 4, mine, True).wait_recv()

    def drain(self):
        self.x_copy().wait_send()
        for mine in (1, 0):
            for way in (0, 1):
                for step in range(1, 5 if way == 1 - mine else 4):
                    self.copy(way, step, mine).wait_send()


class PairRingSum(RingSum):
    def pair(self, other, x_out, x_into, x_send, x_recv):
        self.other, self.x_out, self.x_into, self.x_send, self.x_recv = other, x_out, x_into, x_send, x_recv
        self.got = set()

    def block(self, offset):
        return lax.rem(self.place.z + offset, Z)

    def x_copy(self, offset):
        block = self.block(offset)
        return remote(
            self.x_out.at[block], self.x_into.at[block], self.x_send.at[offset], self.x_recv.at[offset], self.place.x_other
        )

    def exchange(self, offsets):
        for offset in offsets:
            block = self.block(offset)
            for tag in self.tags:
                self.x_out[(block,) + tag] = self.other[tag + (block,)].astype(BF16)
            self.x_copy(offset).start()

    def local(self, tag, offset):
        offset = offset % Z
        if offset not in self.got:
            self.got.add(offset)
            self.x_copy(offset).wait_recv()
        block = self.block(offset)
        return self.part[tag + (block,)] + self.x_into[(block,) + tag].astype(F32)

    def drain(self):
        super().drain()
        for offset in range(Z):
            self.x_copy(offset).wait_send()


class Gather:
    def __init__(self, place, whole, split, w_send, w_recv, s_send, s_recv, x_send, x_recv):
        self.place, self.whole, self.split = place, whole, split
        self.w_send, self.w_recv, self.s_send, self.s_recv = w_send, w_recv, s_send, s_recv
        self.x_send, self.x_recv = x_send, x_recv

    def block(self, way, steps):
        return lax.rem(self.place.z - (1 - 2 * way) * steps + Z, Z)

    def w_copy(self, way, step, arriving=False, source=None):
        part = self.whole.at[self.block(way, step if arriving else step - 1)]
        if step == 4:
            part = part.at[:, way * WHOLE // 2 : (way + 1) * WHOLE // 2]
        at = (way, step - 1)
        return remote(part if source is None else source, part, self.w_send.at[at], self.w_recv.at[at], self.place.z_next[way])

    def s_copy(self, way, step, arriving=False, source=None):
        part = self.split.at[self.block(way, step if arriving else step - 1), self.place.x]
        at = (way, step - 1)
        return remote(part if source is None else source, part, self.s_send.at[at], self.s_recv.at[at], self.place.z_next[way])

    def x_copy(self, way, steps, arriving=False, source=None):
        part = self.split.at[self.block(way, steps), 1 - self.place.x if arriving else self.place.x]
        at = steps + 3 * way if steps else 0
        return remote(
            part if source is None else source, part, self.x_send.at[at], self.x_recv.at[at], self.place.x_other
        )

    def begin_split(self, source=None):
        for way in (0, 1):
            self.s_copy(way, 1, source=source).start()
        self.x_copy(0, 0, source=source).start()

    def begin_whole(self, source=None):
        for way in (0, 1):
            self.w_copy(way, 1, source=source).start()

    def step(self, step):
        for way in (0, 1):
            self.s_copy(way, step, True).wait_recv()
            if step < 3 or way == 1:
                self.s_copy(way, step + 1).start()
            self.x_copy(way, step).start()
        for way in (0, 1):
            self.w_copy(way, step, True).wait_recv()
            self.w_copy(way, step + 1).start()

    def last_split(self):
        self.s_copy(1, 4, True).wait_recv()
        self.x_copy(1, 4).start()

    def last_whole(self):
        for way in (0, 1):
            self.w_copy(way, 4, True).wait_recv()

    def crossings(self):
        return [(0, 0)] + [(way, steps) for steps in (1, 2, 3) for way in (0, 1)] + [(1, 4)]

    def wait_pair(self):
        for way, steps in self.crossings():
            self.x_copy(way, steps, True).wait_recv()

    def drain(self, first=1):
        for way in (0, 1):
            for step in range(first, 5):
                self.w_copy(way, step).wait_send()
                if step < 4 or way == 1:
                    self.s_copy(way, step).wait_send()
        for way, steps in self.crossings():
            self.x_copy(way, steps).wait_send()


class Direct:
    def __init__(self, me, device_of, out, into, send, recv):
        self.me, self.device_of, self.out, self.into, self.send, self.recv = me, device_of, out, into, send, recv

    def copy(self, apart):
        peer = lax.rem(self.me + apart, 8)
        return remote(
            self.out(peer), self.into(self.me), self.send.at[apart - 1], self.recv.at[apart - 1], self.device_of(peer)
        )

    def start(self):
        for apart in (4, 3, 5, 2, 6, 1, 7):
            self.copy(apart).start()

    def wait_one(self, apart):
        source = lax.rem(self.me - apart + 8, 8)
        part = self.into(source)
        remote(part, part, self.send.at[apart - 1], self.recv.at[apart - 1], self.device_of(source)).wait_recv()

    def wait(self):
        for apart in (1, 7, 2, 6, 3, 5, 4):
            self.wait_one(apart)

    def drain(self):
        for apart in range(1, 8):
            self.copy(apart).wait_send()


class Total:
    def __init__(self, place, m, zs, x, x_got, r, r_got, m_s, m_r, z_s, z_r, one_s, one_r):
        self.place, self.m, self.zs, self.x, self.x_got, self.r, self.r_got = place, m, zs, x, x_got, r, r_got
        self.m_all = Direct(place.mp, place.of_mp, lambda peer: m.at[place.mp], lambda source: m.at[source], m_s, m_r)
        self.z_all = Direct(place.z, place.of_z, lambda peer: zs.at[place.z], lambda source: zs.at[source], z_s, z_r)
        self.one_s, self.one_r = one_s, one_r

    def x_copy(self):
        return remote(self.x, self.x_got, self.one_s.at[0], self.one_r.at[0], self.place.x_other)

    def r_copy(self):
        return remote(self.r, self.r_got, self.one_s.at[1], self.one_r.at[1], self.place.partner)

    def in_order(self, slots):
        total = slots[0]
        for source in range(1, 8):
            total = total + slots[source]
        return total

    def start(self, tile):
        self.m[self.place.mp] = tile
        self.m_all.start()

    def over_x(self):
        self.m_all.wait()
        self.x[...] = self.in_order(self.m)
        self.x_copy().start()

    def over_z(self):
        self.x_copy().wait_recv()
        self.zs[self.place.z] = self.x[...] + self.x_got[...]
        self.z_all.start()

    def over_role(self):
        self.z_all.wait()
        self.r[...] = self.in_order(self.zs)
        self.r_copy().start()

    def result(self):
        self.r_copy().wait_recv()
        return self.r[...] + self.r_got[...]

    def drain(self):
        self.m_all.drain()
        self.x_copy().wait_send()
        self.z_all.drain()
        self.r_copy().wait_send()


class Place:
    def __init__(self):
        self.role, self.mp, self.dp = lax.axis_index("role"), lax.axis_index("mp"), lax.axis_index("dp")
        dp = self.dp
        self.z, self.x = dp // 2, lax.rem(dp, 2)
        role, mp, z, x = self.role, self.mp, self.z, self.x
        up, down = lax.rem(z + 1, Z) * 2 + x, lax.rem(z + Z - 1, Z) * 2 + x
        self.z_next = ((role, up, mp), (role, down, mp))
        self.z_next_cross = ((1 - role, up, mp), (1 - role, down, mp))
        self.x_other = (role, z * 2 + 1 - x, mp)
        self.partner = (1 - role, dp, mp)
        self.across = (role, mp * 2 + x, z)
        self.of_z = lambda peer: (role, peer * 2 + x, mp)
        self.of_mp = lambda peer: (role, dp, peer)


def exchange_kernel(
    tok_in, w_in, down_in, lin_in,
    tok_out, cot, s_cot, down_out, linear_out, stat_out,
    tok, w, down, lin, down_turned, tok_turned, hid_out, err_out, lin_out, down_grad, linear_grad,
    part, b_out, b_into, bx_out, bx_into, pre, hid,
    s_part, s_out, s_into, sx_out, sx_into, s_pre, s_hid,
    d_part, d_out, d_into, err, target_out, target,
    lin_part, e_out, e_into, ex_out, ex_into, lin_err,
    k_out, k_into, kx_out, kx_into, gate_out, up_out,
    ks_out, ks_into, ksx_out, ksx_into, s_gate_out, s_up_out,
    m1, z1, x1, x1_got, r1, r1_got, stat,
    load_sem, store_sem,
    tok_s, tok_r, hand_s, hand_r, b_s, b_r, bx_s, bx_r, s_s, s_r, sx_s, sx_r,
    c_s, c_r, cs_s, cs_r, cx_s, cx_r,
    d_s, d_r, one_s, one_r, i_s, i_r, e_s, e_r, k_s, k_r, ks_s, ks_r, ksx_s, ksx_r,
    j_s, j_r, jx_s, jx_r, l_s, l_r, ls_s, ls_r, lx_s, lx_r, g_s, g_r, gn_s,
    m1_s, m1_r, z1_s, z1_r, o1_s, o1_r,
    share_s, share_r,
):
    place = Place()
    role, mp, dp, z, x = place.role, place.mp, place.dp, place.z, place.x
    student, teacher = role == 1, role == 0
    x_of = (1 - x, x)
    halves = (0, 1)

    loads = [
        pltpu.make_async_copy(tok_in.at[:, b * QUARTER : (b + 1) * QUARTER], tok.at[b, mp], load_sem.at[b])
        for b in halves
    ]
    loads += [
        pltpu.make_async_copy(w_in, w, load_sem.at[2]),
        pltpu.make_async_copy(down_in, down, load_sem.at[3]),
    ]
    loads += [
        pltpu.make_async_copy(
            lin_in.at[:, pl.ds(pl.multiple_of(b * 2 * QUARTER + role * QUARTER, QUARTER), QUARTER)],
            lin.at[b],
            load_sem.at[4 + b],
        )
        for b in halves
    ]
    for load in loads:
        load.start()

    barrier = pltpu.get_barrier_semaphore()

    def greet(device):
        pl.semaphore_signal(barrier, inc=1, device_id=device, device_id_type=MESH)

    for apart in range(1, 8):
        greet(place.of_mp(lax.rem(mp + apart, 8)))
        greet((1 - role, dp, lax.rem(mp + apart, 8)))
        greet(place.of_z(lax.rem(z + apart, 8)))
    greet(place.x_other)
    greet(place.partner)
    for way in (0, 1):
        greet(place.z_next_cross[way])

    @pl.when(z != mp)
    def _():
        greet(place.across)
        pl.semaphore_wait(barrier, 26)

    @pl.when(z == mp)
    def _():
        pl.semaphore_wait(barrier, 25)

    for load in loads[:2]:
        load.wait()
    tokens = Direct(mp, place.of_mp, lambda peer: tok.at[role, mp], lambda source: tok.at[role, source], tok_s, tok_r)
    tokens.start()

    def hand(apart, arriving=False):
        source = lax.rem(mp - apart + 8, 8)
        part_of = tok.at[1 - role if arriving else role, source]
        return remote(part_of, part_of, hand_s.at[apart - 1], hand_r.at[apart - 1], place.partner)

    for apart in (1, 7, 2, 6, 3, 5, 4):
        tokens.wait_one(apart)
        hand(apart).start()
    loads[2].wait()
    for apart in (1, 7, 2, 6, 3, 5, 4):
        hand(apart, True).wait_recv()

    def all_tokens():
        return jnp.concatenate([tok[b].reshape(Z * ROWS, QUARTER) for b in halves], axis=1)

    tags = [(0,), (1,)]
    b_sum = RingSum(place, part, b_out, b_into, b_s, b_r, tags, lambda tag: tag[0])
    s_sum = PairRingSum(place, s_part.at[1], s_out, s_into, s_s, s_r, tags, lambda tag: tag[0])
    s_sum.pair(s_part.at[0], sx_out, sx_into, sx_s, sx_r)

    def split_dot(q):
        for g in (0, 1):
            column = pl.multiple_of(g * UNITS + WHOLE + x_of[q] * SPLIT, 128)
            s_part[q, g] = jnp.dot(
                all_tokens(), w[:, pl.ds(column, SPLIT)], preferred_element_type=F32
            ).reshape(Z, ROWS, SPLIT)

    split_dot(0)
    s_sum.exchange((4,))
    for g in (0, 1):
        part[g] = jnp.dot(
            all_tokens(), w[:, g * UNITS : g * UNITS + WHOLE], preferred_element_type=F32
        ).reshape(Z, ROWS, WHOLE)
        b_sum.begin((g,))
        if g == 0:
            s_sum.exchange((3, 5))
    split_dot(1)
    for tag in tags:
        s_sum.begin(tag, False)
    b_sum.step(2)
    s_sum.exchange((2, 6))
    for load in loads[3:]:
        load.wait()
    for q in (0, 1):
        lin_part[q] = jnp.dot(all_tokens(), lin[x_of[q]], preferred_element_type=F32).reshape(Z, ROWS, QUARTER)
    s_sum.step(2, True)
    b_sum.step(3)
    s_sum.exchange((1, 7, 0))
    for c in range(UNITS // QUARTER):
        down_turned[:, c * QUARTER : (c + 1) * QUARTER] = down[c * QUARTER : (c + 1) * QUARTER].T
    for b in halves:
        tok_turned[b * QUARTER : (b + 1) * QUARTER] = tok[b].reshape(Z * ROWS, QUARTER).T
    stores = [pltpu.make_async_copy(tok_turned, tok_out, store_sem.at[0])]
    stores[0].start()
    s_sum.step(3)
    b_sum.step(4)
    s_sum.step(4)

    def bx_copy(g):
        return remote(bx_out.at[g], bx_into.at[g], bx_s.at[g], bx_r.at[g], place.x_other)

    for g in (0, 1):
        bx_out[g] = b_sum.result((g,)).astype(BF16)
        bx_copy(g).start()

    def hidden(inputs):
        return (inputs[0] * jax.nn.sigmoid(inputs[0]) * inputs[1]).astype(BF16)

    c_all = Gather(place, hid, s_hid, c_s, c_r, cs_s, cs_r, cx_s, cx_r)
    for g in (0, 1):
        s_pre[g] = s_sum.result((g,))
    s_hid[z, x] = hidden(s_pre)
    c_all.begin_split()
    for g in (0, 1):
        bx_copy(g).wait_recv()
        pre[g] = bx_out[g].astype(F32) + bx_into[g].astype(F32)
    hid[z] = hidden(pre)
    c_all.begin_whole()
    e_sum = RingSum(place, lin_part, e_out, e_into, e_s, e_r, [(0,), (1,)], lambda tag: tag[0])
    for tag in e_sum.tags:
        e_sum.begin(tag)
    for step in (1, 2, 3):
        c_all.step(step)
        e_sum.step(step + 1)

    c_all.last_split()
    c_all.last_whole()
    d_part[...] = jnp.dot(hid[...].reshape(Z * ROWS, WHOLE), down[:WHOLE], preferred_element_type=F32)
    c_all.wait_pair()

    def d_copy(b, apart):
        peer = lax.rem(mp + apart, 8)
        return remote(
            d_out.at[b, peer], d_into.at[role, mp], d_s.at[b, apart - 1], d_r.at[role, apart - 1], (b, dp, peer)
        )

    def d_arrival(source_role, apart):
        source = lax.rem(mp - apart + 8, 8)
        got = d_into.at[source_role, source]
        return remote(got, got, d_s.at[0, apart - 1], d_r.at[source_role, apart - 1], (source_role, dp, source))

    def d_partner(arriving=False):
        return remote(
            d_out.at[1 - role, mp],
            d_into.at[1 - role if arriving else role, mp],
            one_s.at[0],
            one_r.at[0],
            place.partner,
        )

    for b in halves:
        columns = slice(b * QUARTER, (b + 1) * QUARTER)
        total = d_part[:, columns] + jnp.dot(
            jnp.concatenate([s_hid[:, c].reshape(Z * ROWS, SPLIT) for c in halves], axis=1),
            down[WHOLE:, columns],
            preferred_element_type=F32,
        )
        d_out[b] = total.reshape(Z, ROWS, QUARTER).astype(BF16)
        for apart in (4, 3, 5, 2, 6, 1, 7):
            d_copy(b, apart).start()
    d_partner().start()
    d_into[role, mp] = d_out[role, mp]

    def ex_copy():
        return remote(ex_out, ex_into, one_s.at[3], one_r.at[3], place.x_other)

    ex_out[...] = e_sum.result((0,)).astype(BF16)
    ex_copy().start()
    linear_rows = e_sum.result((1,))
    tokens.drain()
    b_sum.drain()
    s_sum.drain()
    for apart in range(1, 8):
        hand(apart).wait_send()
    for g in (0, 1):
        bx_copy(g).wait_send()
    for apart in (1, 7, 2, 6, 3, 5, 4):
        for source_role in (0, 1):
            d_arrival(source_role, apart).wait_recv()
    d_partner(True).wait_recv()

    def summed(source_role):
        own = d_into[source_role, 0].astype(F32)
        for source in range(1, 8):
            own = own + d_into[source_role, source].astype(F32)
        return own.astype(BF16)

    teacher_rows = summed(0)
    error = summed(1).astype(F32) - teacher_rows.astype(F32)
    err[role, mp] = error.astype(BF16)

    def err_copy(apart):
        peer = lax.rem(mp + apart, 8)
        return remote(
            err.at[role, mp], err.at[role, mp], i_s.at[apart - 1], i_r.at[role, apart - 1], (1, dp, peer)
        )

    def err_arrival(source_role, apart):
        source = lax.rem(mp - apart + 8, 8)
        got = err.at[source_role, source]
        return remote(got, got, i_s.at[apart - 1], i_r.at[source_role, apart - 1], (source_role, dp, source))

    def err_partner():
        return remote(err.at[0, mp], err.at[0, mp], one_s.at[1], one_r.at[1], place.partner)

    for apart in (4, 3, 5, 2, 6, 1, 7):
        err_copy(apart).start()

    @pl.when(teacher)
    def _():
        err_partner().start()

    target_out[...] = teacher_rows

    def target_copy():
        return remote(target_out, target, one_s.at[2], one_r.at[2], place.across)

    @pl.when(z != mp)
    def _():
        target_copy().start()

    @pl.when(z == mp)
    def _():
        target[...] = target_out[...]

    k_sum = RingSum(place, part.at[0], k_out, k_into, k_s, k_r, [()], lambda tag: 0)
    ks_sum = PairRingSum(place, s_part.at[1, 0], ks_out, ks_into, ks_s, ks_r, [()], lambda tag: 1)
    ks_sum.pair(s_part.at[0, 0], ksx_out, ksx_into, ksx_s, ksx_r)

    def err_share():
        return remote(err, err_out, share_s.at[2], share_r.at[2], place.partner)

    def err_store():
        return pltpu.make_async_copy(err, err_out, store_sem.at[3])

    def parts_of(whole, split, out):
        yield whole, out.at[:, :, :WHOLE]
        for b in halves:
            yield split.at[:, b], out.at[:, :, WHOLE + b * SPLIT : WHOLE + (b + 1) * SPLIT]

    def hid_shares():
        return [
            remote(here, there, share_s.at[5 + i], share_r.at[5 + i], place.partner)
            for i, (here, there) in enumerate(parts_of(hid, s_hid, hid_out))
        ]

    def hid_stores():
        return [
            pltpu.make_async_copy(here, there, store_sem.at[7 + i])
            for i, (here, there) in enumerate(parts_of(hid, s_hid, hid_out))
        ]

    def cot_dot(start, size):
        all_err = jnp.concatenate([err[b].reshape(Z * ROWS, QUARTER) for b in halves], axis=1)
        return jnp.dot(all_err, down_turned[:, pl.ds(start, size)], preferred_element_type=F32).reshape(Z, ROWS, size)

    @pl.when(student)
    def _():
        for apart in (1, 7, 2, 6, 3, 5, 4):
            for source_role in (0, 1):
                err_arrival(source_role, apart).wait_recv()
        err_partner().wait_recv()
        s_part[0, 0] = cot_dot(pl.multiple_of(WHOLE + x_of[0] * SPLIT, 128), SPLIT)
        ks_sum.exchange((4,))
        part[0] = cot_dot(0, WHOLE)
        k_sum.begin(())
        ks_sum.exchange((3, 5))
        s_part[1, 0] = cot_dot(pl.multiple_of(WHOLE + x_of[1] * SPLIT, 128), SPLIT)
        ks_sum.exchange((2, 6, 1, 7, 0))

    ex_copy().wait_recv()

    @pl.when(z != mp)
    def _():
        target_copy().wait_recv()

    linear_error = linear_rows + ex_into[...].astype(F32) - target[...].astype(F32)
    lin_err[z, x] = linear_error.astype(BF16)
    j_all = RingGather(place, lin_err, j_s, j_r, jx_s.at[0], jx_r.at[0])
    j_all.begin()
    row = lax.broadcasted_iota(jnp.int32, (8, 128), 0)
    teacher_float = teacher_rows.astype(F32)
    norm = Total(place, m1, z1, x1, x1_got, r1, r1_got, m1_s, m1_r, z1_s, z1_r, o1_s, o1_r)
    target_square = jnp.sum(teacher_float * teacher_float)
    error_square = jnp.sum(error * error)
    linear_square = jnp.sum(linear_error * linear_error)
    norm.start(jnp.where(row == 0, target_square, jnp.where(row == 1, error_square, linear_square)))

    @pl.when(student)
    def _():
        ks_sum.begin((), False)
        k_sum.step(2)

    j_all.begin_other()
    norm.over_x()

    @pl.when(student)
    def _():
        ks_sum.step(2, True)
        k_sum.step(3)

    norm.over_z()
    j_all.step(1)

    @pl.when(student)
    def _():
        ks_sum.step(3)
        k_sum.step(4)
        ks_sum.step(4)
        err_share().start()
        err_store().start()
        for copy in hid_shares() + hid_stores():
            copy.start()

    norm.over_role()
    j_all.step(2)
    stat[...] = norm.result()
    stores.append(pltpu.make_async_copy(stat, stat_out, store_sem.at[4]))
    stores[-1].start()

    def kx_copy():
        return remote(kx_out, kx_into, bx_s.at[2], bx_r.at[2], place.x_other)

    def gate_copy(i):
        return remote(*((s_gate_out, s_cot.at[z, x]), (gate_out, cot.at[z]))[i], g_s.at[i], g_r.at[i], place.partner)

    def up_store(i):
        here, there = ((s_up_out, s_cot.at[z, x]), (up_out, cot.at[z]))[i]
        return pltpu.make_async_copy(here, there, store_sem.at[10 + i])

    l_all = Gather(place, cot, s_cot, l_s, l_r, ls_s, ls_r, lx_s, lx_r)

    def gate_next(way, i):
        ends = ((s_gate_out, s_cot.at[z, x]), (gate_out, cot.at[z]))[i]
        return remote(*ends, gn_s.at[way, i], (ls_r, l_r)[i].at[way, 0], place.z_next_cross[way])

    def cotangents(total, inputs):
        factor = (16.0 * MODEL) / stat[0:1, 0:1]
        hidden_cot = total * factor
        gate_pre, up_pre = inputs[0], inputs[1]
        sig = jax.nn.sigmoid(gate_pre)
        gate_cot = hidden_cot * up_pre * sig * (1.0 + gate_pre * (1.0 - sig))
        return gate_cot.astype(BF16), (hidden_cot * gate_pre * sig).astype(BF16)

    @pl.when(student)
    def _():
        kx_out[...] = k_sum.result(()).astype(BF16)
        kx_copy().start()
        s_gate_out[...], s_up_out[...] = cotangents(ks_sum.result(()), s_pre)
        for way in (0, 1):
            gate_next(way, 0).start()
        gate_copy(0).start()
        l_all.begin_split(s_up_out)
        up_store(0).start()
        kx_copy().wait_recv()
        gate_out[...], up_out[...] = cotangents(kx_out[...].astype(F32) + kx_into[...].astype(F32), pre)
        for way in (0, 1):
            gate_next(way, 1).start()
        l_all.begin_whole(up_out)
        up_store(1).start()
        gate_copy(1).start()

    @pl.when(teacher)
    def _():
        gate_copy(0).wait_recv()
        l_all.x_copy(0, 0).start()

    for apart in range(1, 8):
        err_copy(apart).wait_send()
        for b in halves:
            d_copy(b, apart).wait_send()
    d_partner().wait_send()
    j_all.step(3)
    l_all.step(1)
    j_all.last()

    def lin_columns(b):
        start = pl.multiple_of(b * 2 * QUARTER + role * QUARTER, QUARTER)
        return lin_out.at[:, :, pl.ds(start, QUARTER)]

    def lin_share(b):
        return remote(lin_err.at[:, b], lin_columns(b), share_s.at[3 + b], share_r.at[3 + b], place.partner)

    def lin_arrival(b):
        start = pl.multiple_of(b * 2 * QUARTER + (1 - role) * QUARTER, QUARTER)
        got = lin_out.at[:, :, pl.ds(start, QUARTER)]
        return remote(lin_err.at[:, b], got, share_s.at[3 + b], share_r.at[3 + b], place.partner)

    lin_stores = [pltpu.make_async_copy(lin_err.at[:, b], lin_columns(b), store_sem.at[5 + b]) for b in halves]
    for b in halves:
        lin_share(b).start()
        lin_stores[b].start()

    @pl.when(student)
    def _():
        err_store().wait()
        err_share().wait_send()
        for copy in hid_stores():
            copy.wait()
        for copy in hid_shares():
            copy.wait_send()
        k_sum.drain()
        ks_sum.drain()

    @pl.when(teacher)
    def _():
        err_share().wait_recv()
        for copy in hid_shares():
            copy.wait_recv()

    factor = (16.0 * MODEL) / stat[0:1, 0:1]

    def rows_of(ref, c):
        return ref[:, :, c * QUARTER : (c + 1) * QUARTER].reshape(Z * ROWS, QUARTER)

    def down_piece(c):
        for b in halves:
            product = contract_rows(rows_of(hid_out, c), err_out[b].reshape(Z * ROWS, QUARTER))
            down_grad[c * QUARTER : (c + 1) * QUARTER, b * QUARTER : (b + 1) * QUARTER] = (factor * product).astype(BF16)

    def linear_piece(c):
        for b in halves:
            product = jnp.dot(
                tok_turned[b * QUARTER : (b + 1) * QUARTER], rows_of(lin_out, c), preferred_element_type=F32
            )
            linear_grad[b * QUARTER : (b + 1) * QUARTER, c * QUARTER : (c + 1) * QUARTER] = (factor * product).astype(BF16)

    for c in range(4):
        down_piece(c)
    c_all.drain()
    e_sum.drain()
    l_all.step(2)
    for c in range(4, UNITS // QUARTER):
        down_piece(c)
    stores.append(pltpu.make_async_copy(down_grad, down_out, store_sem.at[12]))
    stores[-1].start()
    ex_copy().wait_send()
    norm.drain()
    j_all.drain()
    l_all.step(3)
    for b in halves:
        lin_arrival(b).wait_recv()
        lin_stores[b].wait()
    for c in range(LIN // QUARTER):
        linear_piece(c)
    stores.append(pltpu.make_async_copy(linear_grad, linear_out, store_sem.at[13]))
    stores[-1].start()

    @pl.when(teacher)
    def _():
        gate_copy(1).wait_recv()

    l_all.last_split()
    l_all.last_whole()
    l_all.wait_pair()

    for b in halves:
        lin_share(b).wait_send()

    @pl.when(z != mp)
    def _():
        target_copy().wait_send()

    @pl.when(student)
    def _():
        l_all.drain()
        kx_copy().wait_send()
        for i in (0, 1):
            up_store(i).wait()
            gate_copy(i).wait_send()
            for way in (0, 1):
                gate_next(way, i).wait_send()

    @pl.when(teacher)
    def _():
        l_all.drain(2)
        err_partner().wait_send()

    for store in stores:
        store.wait()


def exchange(tokens, w, down, linear):
    def vmem(*shape, dtype=BF16):
        return pltpu.VMEM(shape, dtype)

    def sems(*shape):
        return pltpu.SemaphoreType.DMA(shape)

    def array(*shape, dtype=BF16):
        return jax.ShapeDtypeStruct(shape, dtype)

    def total_tiles():
        return [vmem(8, 8, 128, dtype=F32)] * 2 + [vmem(8, 128, dtype=F32)] * 4

    anywhere = pl.BlockSpec(memory_space=pl.ANY)
    return pl.pallas_call(
        exchange_kernel,
        out_shape=[
            array(WIDTH, Z * ROWS),
            array(Z, ROWS, WHOLE),
            array(Z, 2, ROWS, SPLIT),
            array(UNITS, WIDTH),
            array(WIDTH, LIN),
            array(8, 128, dtype=F32),
        ],
        in_specs=[anywhere] * 4,
        out_specs=[anywhere] * 6,
        scratch_shapes=[
            vmem(2, Z, ROWS, QUARTER), vmem(WIDTH, 2 * UNITS), vmem(UNITS, WIDTH), vmem(2, WIDTH, QUARTER), vmem(WIDTH, UNITS), vmem(WIDTH, Z * ROWS),
            vmem(Z, ROWS, UNITS), vmem(2, Z, ROWS, QUARTER), vmem(Z, ROWS, LIN), vmem(UNITS, WIDTH), vmem(WIDTH, LIN),
            vmem(2, Z, ROWS, WHOLE, dtype=F32), vmem(2, 4, 2, ROWS, WHOLE), vmem(2, 4, 2, ROWS, WHOLE),
            vmem(2, ROWS, WHOLE), vmem(2, ROWS, WHOLE), vmem(2, ROWS, WHOLE, dtype=F32), vmem(Z, ROWS, WHOLE),
            vmem(2, 2, Z, ROWS, SPLIT, dtype=F32), vmem(2, 4, 2, ROWS, SPLIT), vmem(2, 4, 2, ROWS, SPLIT),
            vmem(Z, 2, ROWS, SPLIT), vmem(Z, 2, ROWS, SPLIT), vmem(2, ROWS, SPLIT, dtype=F32), vmem(Z, 2, ROWS, SPLIT),
            vmem(Z * ROWS, WIDTH, dtype=F32), vmem(2, 8, ROWS, QUARTER), vmem(2, 8, ROWS, QUARTER),
            vmem(2, 8, ROWS, QUARTER), vmem(ROWS, QUARTER), vmem(ROWS, QUARTER),
            vmem(2, Z, ROWS, QUARTER, dtype=F32), vmem(2, 4, 2, ROWS, QUARTER), vmem(2, 4, 2, ROWS, QUARTER),
            vmem(ROWS, QUARTER), vmem(ROWS, QUARTER), vmem(Z, 2, ROWS, QUARTER),
            vmem(2, 4, ROWS, WHOLE), vmem(2, 4, ROWS, WHOLE), vmem(ROWS, WHOLE), vmem(ROWS, WHOLE),
            vmem(ROWS, WHOLE), vmem(ROWS, WHOLE),
            vmem(2, 4, ROWS, SPLIT), vmem(2, 4, ROWS, SPLIT), vmem(Z, ROWS, SPLIT), vmem(Z, ROWS, SPLIT),
            vmem(ROWS, SPLIT), vmem(ROWS, SPLIT),
            *total_tiles(), vmem(8, 128, dtype=F32),
            sems(6), sems(14),
            sems(7), sems(7), sems(7), sems(7), sems(2, 4, 2), sems(2, 4, 2), sems(3), sems(3),
            sems(2, 4, 2), sems(2, 4, 2), sems(8), sems(8),
            sems(2, 4), sems(2, 4), sems(2, 4), sems(2, 4), sems(8), sems(8),
            sems(2, 7), sems(2, 7), sems(4), sems(4), sems(7), sems(2, 7), sems(2, 4, 2), sems(2, 4, 2),
            sems(2, 4), sems(2, 4), sems(2, 4), sems(2, 4), sems(8), sems(8),
            sems(2, 4, 2), sems(2, 4, 2), sems(1), sems(1),
            sems(2, 4), sems(2, 4), sems(2, 4), sems(2, 4), sems(8), sems(8), sems(2), sems(2), sems(2, 2),
            sems(7), sems(7), sems(7), sems(7), sems(2), sems(2),
            sems(8), sems(8),
        ],
        compiler_params=pltpu.CompilerParams(
            collective_id=0, has_side_effects=True, vmem_limit_bytes=42 * 1024 * 1024
        ),
        name="exchange",
    )(tokens, w, down, linear)


def contract_rows(left, right):
    return lax.dot_general(left, right, (((0,), (0,)), ((), ())), preferred_element_type=F32)


BLOCK = 256


def gradients_kernel(
    turned, cot, s_cot, stat, down, linear, unit_out, down_out, linear_out, losses, unit, sem
):
    copies = []

    def send(here, there):
        copies.append(pltpu.make_async_copy(here, there, sem.at[len(copies)]))
        copies[-1].start()

    send(down, down_out)
    send(linear, linear_out)
    share = stat[...] / stat[0:1, 0:1]
    losses[0] = share[1, 0]
    losses[1] = share[2, 0]
    for i in range(UNITS // BLOCK):
        part = slice(i * BLOCK, (i + 1) * BLOCK)
        split, column = divmod(i * BLOCK - WHOLE, SPLIT)
        if split < 0:
            columns = cot[:, part]
        else:
            columns = s_cot[:, split, :, column : column + BLOCK].reshape(Z * ROWS, BLOCK)
        unit[:, part] = jnp.dot(turned[...], columns, preferred_element_type=F32).astype(BF16)
        send(unit.at[:, part], unit_out.at[:, part])
    for copy in copies:
        copy.wait()


def gradients(turned, cot, s_cot, stat, down, linear):
    shapes = [(WIDTH, UNITS), (UNITS, WIDTH), (WIDTH, LIN)]
    whole = pl.BlockSpec(memory_space=pltpu.VMEM)
    anywhere = pl.BlockSpec(memory_space=pl.ANY)
    return pl.pallas_call(
        gradients_kernel,
        out_shape=[jax.ShapeDtypeStruct(shape, BF16) for shape in shapes] + [jax.ShapeDtypeStruct((2,), F32)],
        in_specs=[whole] * 4 + [anywhere] * 2,
        out_specs=[anywhere] * 3 + [pl.BlockSpec(memory_space=pltpu.SMEM)],
        scratch_shapes=[
            pltpu.VMEM((WIDTH, UNITS), BF16),
            pltpu.SemaphoreType.DMA((2 + UNITS // BLOCK,)),
        ],
        compiler_params=pltpu.CompilerParams(vmem_limit_bytes=24 * 1024 * 1024),
        name="gradients",
    )(turned, cot, s_cot, stat, down, linear)


def body(tokens, gate_up, down, linear):
    w = gate_up.reshape(WIDTH, 2 * UNITS)
    tok, cot, s_cot, down_own, linear_own, stat = exchange(tokens, w, down[0], linear)
    rows = Z * ROWS
    unit_grad, down_grad, linear_grad, losses = gradients(
        tok, cot.reshape(rows, WHOLE), s_cot, stat, down_own, linear_own
    )
    return (unit_grad[None], down_grad, linear_grad, losses)


def solution(mesh):
    return jax.shard_map(
        body,
        mesh=mesh,
        in_specs=(P("mp", "dp"), P("role", "dp", None, "mp"), P("role", "mp", "dp"), P("dp", "mp")),
        out_specs=(P("role", "dp", "mp"), P("mp", "dp"), P("dp", "mp"), P()),
        check_vma=False,
    )
```

```python
import jax
import jax.numpy as jnp
from jax import lax
from jax.experimental import pallas as pl
from jax.experimental.pallas import tpu as pltpu
from jax.sharding import PartitionSpec as P

MESH = pl.DeviceIdType.MESH
BF16, F32 = jnp.bfloat16, jnp.float32
MODEL = 8192
Z = 8
ROWS = 48
WIDTH = 512
UNITS = 1792
WHOLE = 768
SPLIT = 512
LIN = 1024
QUARTER = LIN // 4


def remote(src, dst, send, recv, device):
    return pltpu.make_async_remote_copy(
        src_ref=src, dst_ref=dst, send_sem=send, recv_sem=recv, device_id=device, device_id_type=MESH
    )


class RingSum:
    def __init__(self, place, part, out, into, send, recv, tags, long_way):
        self.place, self.part, self.out, self.into = place, part, out, into
        self.send, self.recv, self.tags, self.long_way = send, recv, tags, long_way

    def copy(self, way, step, tag):
        at = (way, step - 1) + tag
        return remote(
            self.out.at[at], self.into.at[at], self.send.at[at], self.recv.at[at], self.place.z_next[way]
        )

    def push(self, way, step, tag, first):
        sign = 1 - 2 * way
        total = self.local(tag, sign * (5 - step))
        if not first:
            self.copy(way, step - 1, tag).wait_recv()
            total = total + self.into[(way, step - 2) + tag].astype(F32)
        self.out[(way, step - 1) + tag] = total.astype(BF16)
        self.copy(way, step, tag).start()

    def local(self, tag, offset):
        return self.part[tag + (lax.rem(self.place.z + offset + Z, Z),)]

    def begin(self, tag, both=True):
        far = self.long_way(tag)
        self.push(far, 1, tag, True)
        if both:
            self.push(1 - far, 2, tag, True)

    def step(self, step, both=False):
        for tag in self.tags:
            for way in (0, 1):
                if step > 2 or way == self.long_way(tag):
                    self.push(way, step, tag, False)
                elif both:
                    self.push(way, step, tag, True)

    def result(self, tag):
        total = self.local(tag, 0)
        for way in (0, 1):
            self.copy(way, 4, tag).wait_recv()
            total = total + self.into[(way, 3) + tag].astype(F32)
        return total

    def drain(self):
        for tag in self.tags:
            for way in (0, 1):
                for step in range(1 if way == self.long_way(tag) else 2, 5):
                    self.copy(way, step, tag).wait_send()


class RingGather:
    def __init__(self, place, buf, send, recv, x_send, x_recv):
        self.place, self.buf, self.send, self.recv = place, buf, send, recv
        self.x_send, self.x_recv = x_send, x_recv

    def copy(self, way, step, mine, arriving=False):
        place = self.place
        sign = 1 - 2 * way
        block = lax.rem(place.z - sign * (step if arriving else step - 1) + Z, Z)
        x = place.x if mine else 1 - place.x
        part = self.buf.at[block, x]
        at = (way, step - 1, mine)
        return remote(part, part, self.send.at[at], self.recv.at[at], place.z_next[way])

    def x_copy(self, arriving=False):
        place = self.place
        part = self.buf.at[place.z, 1 - place.x if arriving else place.x]
        return remote(part, part, self.x_send, self.x_recv, place.x_other)

    def begin(self):
        self.copy(0, 1, 1).start()
        self.copy(1, 1, 1).start()
        self.x_copy().start()

    def begin_other(self):
        self.x_copy(True).wait_recv()
        self.copy(0, 1, 0).start()
        self.copy(1, 1, 0).start()

    def step(self, step):
        for mine in (1, 0):
            for way in (0, 1):
                self.copy(way, step, mine, True).wait_recv()
                if step < 3 or way == 1 - mine:
                    self.copy(way, step + 1, mine).start()

    def last(self):
        for mine in (1, 0):
            self.copy(1 - mine, 4, mine, True).wait_recv()

    def drain(self):
        self.x_copy().wait_send()
        for mine in (1, 0):
            for way in (0, 1):
                for step in range(1, 5 if way == 1 - mine else 4):
                    self.copy(way, step, mine).wait_send()


class PairRingSum(RingSum):
    def pair(self, other, x_out, x_into, x_send, x_recv):
        self.other, self.x_out, self.x_into, self.x_send, self.x_recv = other, x_out, x_into, x_send, x_recv
        self.got = set()

    def block(self, offset):
        return lax.rem(self.place.z + offset, Z)

    def x_copy(self, offset):
        block = self.block(offset)
        return remote(
            self.x_out.at[block], self.x_into.at[block], self.x_send.at[offset], self.x_recv.at[offset], self.place.x_other
        )

    def exchange(self, offsets):
        for offset in offsets:
            block = self.block(offset)
            for tag in self.tags:
                self.x_out[(block,) + tag] = self.other[tag + (block,)].astype(BF16)
            self.x_copy(offset).start()

    def local(self, tag, offset):
        offset = offset % Z
        if offset not in self.got:
            self.got.add(offset)
            self.x_copy(offset).wait_recv()
        block = self.block(offset)
        return self.part[tag + (block,)] + self.x_into[(block,) + tag].astype(F32)

    def drain(self):
        super().drain()
        for offset in range(Z):
            self.x_copy(offset).wait_send()


class Gather:
    def __init__(self, place, whole, split, w_send, w_recv, s_send, s_recv, x_send, x_recv):
        self.place, self.whole, self.split = place, whole, split
        self.w_send, self.w_recv, self.s_send, self.s_recv = w_send, w_recv, s_send, s_recv
        self.x_send, self.x_recv = x_send, x_recv

    def block(self, way, steps):
        return lax.rem(self.place.z - (1 - 2 * way) * steps + Z, Z)

    def w_copy(self, way, step, arriving=False, source=None):
        part = self.whole.at[self.block(way, step if arriving else step - 1)]
        if step == 4:
            part = part.at[:, way * WHOLE // 2 : (way + 1) * WHOLE // 2]
        at = (way, step - 1)
        return remote(part if source is None else source, part, self.w_send.at[at], self.w_recv.at[at], self.place.z_next[way])

    def s_copy(self, way, step, arriving=False, source=None):
        part = self.split.at[self.block(way, step if arriving else step - 1), self.place.x]
        at = (way, step - 1)
        return remote(part if source is None else source, part, self.s_send.at[at], self.s_recv.at[at], self.place.z_next[way])

    def x_copy(self, way, steps, arriving=False, source=None):
        part = self.split.at[self.block(way, steps), 1 - self.place.x if arriving else self.place.x]
        at = steps + 3 * way if steps else 0
        return remote(
            part if source is None else source, part, self.x_send.at[at], self.x_recv.at[at], self.place.x_other
        )

    def begin_split(self, source=None):
        for way in (0, 1):
            self.s_copy(way, 1, source=source).start()
        self.x_copy(0, 0, source=source).start()

    def begin_whole(self, source=None):
        for way in (0, 1):
            self.w_copy(way, 1, source=source).start()

    def step(self, step):
        for way in (0, 1):
            self.s_copy(way, step, True).wait_recv()
            if step < 3 or way == 1:
                self.s_copy(way, step + 1).start()
            self.x_copy(way, step).start()
        for way in (0, 1):
            self.w_copy(way, step, True).wait_recv()
            self.w_copy(way, step + 1).start()

    def last_split(self):
        self.s_copy(1, 4, True).wait_recv()
        self.x_copy(1, 4).start()

    def last_whole(self):
        for way in (0, 1):
            self.w_copy(way, 4, True).wait_recv()

    def crossings(self):
        return [(0, 0)] + [(way, steps) for steps in (1, 2, 3) for way in (0, 1)] + [(1, 4)]

    def wait_pair(self):
        for way, steps in self.crossings():
            self.x_copy(way, steps, True).wait_recv()

    def drain(self, first=1):
        for way in (0, 1):
            for step in range(first, 5):
                self.w_copy(way, step).wait_send()
                if step < 4 or way == 1:
                    self.s_copy(way, step).wait_send()
        for way, steps in self.crossings():
            self.x_copy(way, steps).wait_send()


class Direct:
    def __init__(self, me, device_of, out, into, send, recv):
        self.me, self.device_of, self.out, self.into, self.send, self.recv = me, device_of, out, into, send, recv

    def copy(self, apart):
        peer = lax.rem(self.me + apart, 8)
        return remote(
            self.out(peer), self.into(self.me), self.send.at[apart - 1], self.recv.at[apart - 1], self.device_of(peer)
        )

    def start(self):
        for apart in (4, 3, 5, 2, 6, 1, 7):
            self.copy(apart).start()

    def wait_one(self, apart):
        source = lax.rem(self.me - apart + 8, 8)
        part = self.into(source)
        remote(part, part, self.send.at[apart - 1], self.recv.at[apart - 1], self.device_of(source)).wait_recv()

    def wait(self):
        for apart in (1, 7, 2, 6, 3, 5, 4):
            self.wait_one(apart)

    def drain(self):
        for apart in range(1, 8):
            self.copy(apart).wait_send()


class Total:
    def __init__(self, place, m, zs, x, x_got, r, r_got, m_s, m_r, z_s, z_r, one_s, one_r):
        self.place, self.m, self.zs, self.x, self.x_got, self.r, self.r_got = place, m, zs, x, x_got, r, r_got
        self.m_all = Direct(place.mp, place.of_mp, lambda peer: m.at[place.mp], lambda source: m.at[source], m_s, m_r)
        self.z_all = Direct(place.z, place.of_z, lambda peer: zs.at[place.z], lambda source: zs.at[source], z_s, z_r)
        self.one_s, self.one_r = one_s, one_r

    def x_copy(self):
        return remote(self.x, self.x_got, self.one_s.at[0], self.one_r.at[0], self.place.x_other)

    def r_copy(self):
        return remote(self.r, self.r_got, self.one_s.at[1], self.one_r.at[1], self.place.partner)

    def in_order(self, slots):
        total = slots[0]
        for source in range(1, 8):
            total = total + slots[source]
        return total

    def start(self, tile):
        self.m[self.place.mp] = tile
        self.m_all.start()

    def over_x(self):
        self.m_all.wait()
        self.x[...] = self.in_order(self.m)
        self.x_copy().start()

    def over_z(self):
        self.x_copy().wait_recv()
        self.zs[self.place.z] = self.x[...] + self.x_got[...]
        self.z_all.start()

    def over_role(self):
        self.z_all.wait()
        self.r[...] = self.in_order(self.zs)
        self.r_copy().start()

    def result(self):
        self.r_copy().wait_recv()
        return self.r[...] + self.r_got[...]

    def drain(self):
        self.m_all.drain()
        self.x_copy().wait_send()
        self.z_all.drain()
        self.r_copy().wait_send()


class Place:
    def __init__(self):
        self.role, self.mp, self.dp = lax.axis_index("role"), lax.axis_index("mp"), lax.axis_index("dp")
        dp = self.dp
        self.z, self.x = dp // 2, lax.rem(dp, 2)
        role, mp, z, x = self.role, self.mp, self.z, self.x
        up, down = lax.rem(z + 1, Z) * 2 + x, lax.rem(z + Z - 1, Z) * 2 + x
        self.z_next = ((role, up, mp), (role, down, mp))
        self.z_next_cross = ((1 - role, up, mp), (1 - role, down, mp))
        self.x_other = (role, z * 2 + 1 - x, mp)
        self.partner = (1 - role, dp, mp)
        self.across = (role, mp * 2 + x, z)
        self.of_z = lambda peer: (role, peer * 2 + x, mp)
        self.of_mp = lambda peer: (role, dp, peer)


def exchange_kernel(
    tok_in, w_in, down_in, lin_in,
    tok_out, cot, s_cot, down_out, linear_out, stat_out,
    tok, w, down, lin, down_turned, tok_turned, hid_out, err_out, lin_out, down_grad, linear_grad,
    part, b_out, b_into, bx_out, bx_into, pre, hid,
    s_part, s_out, s_into, sx_out, sx_into, s_pre, s_hid,
    d_part, d_out, d_into, err, target_out, target,
    lin_part, e_out, e_into, ex_out, ex_into, lin_err,
    k_out, k_into, kx_out, kx_into, gate_out, up_out,
    ks_out, ks_into, ksx_out, ksx_into, s_gate_out, s_up_out,
    m1, z1, x1, x1_got, r1, r1_got, stat,
    load_sem, store_sem,
    tok_s, tok_r, hand_s, hand_r, b_s, b_r, bx_s, bx_r, s_s, s_r, sx_s, sx_r,
    c_s, c_r, cs_s, cs_r, cx_s, cx_r,
    d_s, d_r, one_s, one_r, i_s, i_r, e_s, e_r, k_s, k_r, ks_s, ks_r, ksx_s, ksx_r,
    j_s, j_r, jx_s, jx_r, l_s, l_r, ls_s, ls_r, lx_s, lx_r, g_s, g_r, gn_s,
    m1_s, m1_r, z1_s, z1_r, o1_s, o1_r,
    share_s, share_r,
):
    place = Place()
    role, mp, dp, z, x = place.role, place.mp, place.dp, place.z, place.x
    student, teacher = role == 1, role == 0
    x_of = (1 - x, x)
    halves = (0, 1)

    loads = [
        pltpu.make_async_copy(tok_in.at[:, b * QUARTER : (b + 1) * QUARTER], tok.at[b, mp], load_sem.at[b])
        for b in halves
    ]
    loads += [
        pltpu.make_async_copy(w_in, w, load_sem.at[2]),
        pltpu.make_async_copy(down_in, down, load_sem.at[3]),
    ]
    loads += [
        pltpu.make_async_copy(
            lin_in.at[:, pl.ds(pl.multiple_of(b * 2 * QUARTER + role * QUARTER, QUARTER), QUARTER)],
            lin.at[b],
            load_sem.at[4 + b],
        )
        for b in halves
    ]
    for load in loads:
        load.start()

    barrier = pltpu.get_barrier_semaphore()

    def greet(device):
        pl.semaphore_signal(barrier, inc=1, device_id=device, device_id_type=MESH)

    for apart in range(1, 8):
        greet(place.of_mp(lax.rem(mp + apart, 8)))
        greet((1 - role, dp, lax.rem(mp + apart, 8)))
        greet(place.of_z(lax.rem(z + apart, 8)))
    greet(place.x_other)
    greet(place.partner)
    for way in (0, 1):
        greet(place.z_next_cross[way])

    @pl.when(z != mp)
    def _():
        greet(place.across)
        pl.semaphore_wait(barrier, 26)

    @pl.when(z == mp)
    def _():
        pl.semaphore_wait(barrier, 25)

    for load in loads[:2]:
        load.wait()
    tokens = Direct(mp, place.of_mp, lambda peer: tok.at[role, mp], lambda source: tok.at[role, source], tok_s, tok_r)
    tokens.start()

    def hand(apart, arriving=False):
        source = lax.rem(mp - apart + 8, 8)
        part_of = tok.at[1 - role if arriving else role, source]
        return remote(part_of, part_of, hand_s.at[apart - 1], hand_r.at[apart - 1], place.partner)

    for apart in (1, 7, 2, 6, 3, 5, 4):
        tokens.wait_one(apart)
        hand(apart).start()
    loads[2].wait()
    for apart in (1, 7, 2, 6, 3, 5, 4):
        hand(apart, True).wait_recv()

    def all_tokens():
        return jnp.concatenate([tok[b].reshape(Z * ROWS, QUARTER) for b in halves], axis=1)

    tags = [(0,), (1,)]
    b_sum = RingSum(place, part, b_out, b_into, b_s, b_r, tags, lambda tag: tag[0])
    s_sum = PairRingSum(place, s_part.at[1], s_out, s_into, s_s, s_r, tags, lambda tag: tag[0])
    s_sum.pair(s_part.at[0], sx_out, sx_into, sx_s, sx_r)

    def split_dot(q):
        for g in (0, 1):
            column = pl.multiple_of(g * UNITS + WHOLE + x_of[q] * SPLIT, 128)
            s_part[q, g] = jnp.dot(
                all_tokens(), w[:, pl.ds(column, SPLIT)], preferred_element_type=F32
            ).reshape(Z, ROWS, SPLIT)

    split_dot(0)
    s_sum.exchange((4,))
    for g in (0, 1):
        part[g] = jnp.dot(
            all_tokens(), w[:, g * UNITS : g * UNITS + WHOLE], preferred_element_type=F32
        ).reshape(Z, ROWS, WHOLE)
        b_sum.begin((g,))
        if g == 0:
            s_sum.exchange((3, 5))
    split_dot(1)
    for tag in tags:
        s_sum.begin(tag, False)
    b_sum.step(2)
    s_sum.exchange((2, 6))
    for load in loads[3:]:
        load.wait()
    for q in (0, 1):
        lin_part[q] = jnp.dot(all_tokens(), lin[x_of[q]], preferred_element_type=F32).reshape(Z, ROWS, QUARTER)
    s_sum.step(2, True)
    b_sum.step(3)
    s_sum.exchange((1, 7, 0))
    for c in range(UNITS // QUARTER):
        down_turned[:, c * QUARTER : (c + 1) * QUARTER] = down[c * QUARTER : (c + 1) * QUARTER].T
    for b in halves:
        tok_turned[b * QUARTER : (b + 1) * QUARTER] = tok[b].reshape(Z * ROWS, QUARTER).T
    stores = [pltpu.make_async_copy(tok_turned, tok_out, store_sem.at[0])]
    stores[0].start()
    s_sum.step(3)
    b_sum.step(4)
    s_sum.step(4)

    def bx_copy(g):
        return remote(bx_out.at[g], bx_into.at[g], bx_s.at[g], bx_r.at[g], place.x_other)

    for g in (0, 1):
        bx_out[g] = b_sum.result((g,)).astype(BF16)
        bx_copy(g).start()

    def hidden(inputs):
        return (inputs[0] * jax.nn.sigmoid(inputs[0]) * inputs[1]).astype(BF16)

    c_all = Gather(place, hid, s_hid, c_s, c_r, cs_s, cs_r, cx_s, cx_r)
    for g in (0, 1):
        s_pre[g] = s_sum.result((g,))
    s_hid[z, x] = hidden(s_pre)
    c_all.begin_split()
    for g in (0, 1):
        bx_copy(g).wait_recv()
        pre[g] = bx_out[g].astype(F32) + bx_into[g].astype(F32)
    hid[z] = hidden(pre)
    c_all.begin_whole()
    e_sum = RingSum(place, lin_part, e_out, e_into, e_s, e_r, [(0,), (1,)], lambda tag: tag[0])
    for tag in e_sum.tags:
        e_sum.begin(tag)
    for step in (1, 2, 3):
        c_all.step(step)
        e_sum.step(step + 1)

    c_all.last_split()
    c_all.last_whole()
    d_part[...] = jnp.dot(hid[...].reshape(Z * ROWS, WHOLE), down[:WHOLE], preferred_element_type=F32)
    c_all.wait_pair()

    def d_copy(b, apart):
        peer = lax.rem(mp + apart, 8)
        return remote(
            d_out.at[b, peer], d_into.at[role, mp], d_s.at[b, apart - 1], d_r.at[role, apart - 1], (b, dp, peer)
        )

    def d_arrival(source_role, apart):
        source = lax.rem(mp - apart + 8, 8)
        got = d_into.at[source_role, source]
        return remote(got, got, d_s.at[0, apart - 1], d_r.at[source_role, apart - 1], (source_role, dp, source))

    def d_partner(arriving=False):
        return remote(
            d_out.at[1 - role, mp],
            d_into.at[1 - role if arriving else role, mp],
            one_s.at[0],
            one_r.at[0],
            place.partner,
        )

    for b in halves:
        columns = slice(b * QUARTER, (b + 1) * QUARTER)
        total = d_part[:, columns] + jnp.dot(
            jnp.concatenate([s_hid[:, c].reshape(Z * ROWS, SPLIT) for c in halves], axis=1),
            down[WHOLE:, columns],
            preferred_element_type=F32,
        )
        d_out[b] = total.reshape(Z, ROWS, QUARTER).astype(BF16)
        for apart in (4, 3, 5, 2, 6, 1, 7):
            d_copy(b, apart).start()
    d_partner().start()
    d_into[role, mp] = d_out[role, mp]

    def ex_copy():
        return remote(ex_out, ex_into, one_s.at[3], one_r.at[3], place.x_other)

    ex_out[...] = e_sum.result((0,)).astype(BF16)
    ex_copy().start()
    linear_rows = e_sum.result((1,))
    tokens.drain()
    b_sum.drain()
    s_sum.drain()
    for apart in range(1, 8):
        hand(apart).wait_send()
    for g in (0, 1):
        bx_copy(g).wait_send()
    for apart in (1, 7, 2, 6, 3, 5, 4):
        for source_role in (0, 1):
            d_arrival(source_role, apart).wait_recv()
    d_partner(True).wait_recv()

    def summed(source_role):
        own = d_into[source_role, 0].astype(F32)
        for source in range(1, 8):
            own = own + d_into[source_role, source].astype(F32)
        return own.astype(BF16)

    teacher_rows = summed(0)
    error = summed(1).astype(F32) - teacher_rows.astype(F32)
    err[role, mp] = error.astype(BF16)

    def err_copy(apart):
        peer = lax.rem(mp + apart, 8)
        return remote(
            err.at[role, mp], err.at[role, mp], i_s.at[apart - 1], i_r.at[role, apart - 1], (1, dp, peer)
        )

    def err_arrival(source_role, apart):
        source = lax.rem(mp - apart + 8, 8)
        got = err.at[source_role, source]
        return remote(got, got, i_s.at[apart - 1], i_r.at[source_role, apart - 1], (source_role, dp, source))

    def err_partner():
        return remote(err.at[0, mp], err.at[0, mp], one_s.at[1], one_r.at[1], place.partner)

    for apart in (4, 3, 5, 2, 6, 1, 7):
        err_copy(apart).start()

    @pl.when(teacher)
    def _():
        err_partner().start()

    target_out[...] = teacher_rows

    def target_copy():
        return remote(target_out, target, one_s.at[2], one_r.at[2], place.across)

    @pl.when(z != mp)
    def _():
        target_copy().start()

    @pl.when(z == mp)
    def _():
        target[...] = target_out[...]

    k_sum = RingSum(place, part.at[0], k_out, k_into, k_s, k_r, [()], lambda tag: 0)
    ks_sum = PairRingSum(place, s_part.at[1, 0], ks_out, ks_into, ks_s, ks_r, [()], lambda tag: 1)
    ks_sum.pair(s_part.at[0, 0], ksx_out, ksx_into, ksx_s, ksx_r)

    def err_share():
        return remote(err, err_out, share_s.at[2], share_r.at[2], place.partner)

    def err_store():
        return pltpu.make_async_copy(err, err_out, store_sem.at[3])

    def parts_of(whole, split, out):
        yield whole, out.at[:, :, :WHOLE]
        for b in halves:
            yield split.at[:, b], out.at[:, :, WHOLE + b * SPLIT : WHOLE + (b + 1) * SPLIT]

    def hid_shares():
        return [
            remote(here, there, share_s.at[5 + i], share_r.at[5 + i], place.partner)
            for i, (here, there) in enumerate(parts_of(hid, s_hid, hid_out))
        ]

    def hid_stores():
        return [
            pltpu.make_async_copy(here, there, store_sem.at[7 + i])
            for i, (here, there) in enumerate(parts_of(hid, s_hid, hid_out))
        ]

    def cot_dot(start, size):
        all_err = jnp.concatenate([err[b].reshape(Z * ROWS, QUARTER) for b in halves], axis=1)
        return jnp.dot(all_err, down_turned[:, pl.ds(start, size)], preferred_element_type=F32).reshape(Z, ROWS, size)

    @pl.when(student)
    def _():
        for apart in (1, 7, 2, 6, 3, 5, 4):
            for source_role in (0, 1):
                err_arrival(source_role, apart).wait_recv()
        err_partner().wait_recv()
        s_part[0, 0] = cot_dot(pl.multiple_of(WHOLE + x_of[0] * SPLIT, 128), SPLIT)
        ks_sum.exchange((4,))
        part[0] = cot_dot(0, WHOLE)
        k_sum.begin(())
        ks_sum.exchange((3, 5))
        s_part[1, 0] = cot_dot(pl.multiple_of(WHOLE + x_of[1] * SPLIT, 128), SPLIT)
        ks_sum.exchange((2, 6, 1, 7, 0))

    ex_copy().wait_recv()

    @pl.when(z != mp)
    def _():
        target_copy().wait_recv()

    linear_error = linear_rows + ex_into[...].astype(F32) - target[...].astype(F32)
    lin_err[z, x] = linear_error.astype(BF16)
    j_all = RingGather(place, lin_err, j_s, j_r, jx_s.at[0], jx_r.at[0])
    j_all.begin()
    row = lax.broadcasted_iota(jnp.int32, (8, 128), 0)
    teacher_float = teacher_rows.astype(F32)
    norm = Total(place, m1, z1, x1, x1_got, r1, r1_got, m1_s, m1_r, z1_s, z1_r, o1_s, o1_r)
    target_square = jnp.sum(teacher_float * teacher_float)
    error_square = jnp.sum(error * error)
    linear_square = jnp.sum(linear_error * linear_error)
    norm.start(jnp.where(row == 0, target_square, jnp.where(row == 1, error_square, linear_square)))

    @pl.when(student)
    def _():
        ks_sum.begin((), False)
        k_sum.step(2)

    j_all.begin_other()
    norm.over_x()

    @pl.when(student)
    def _():
        ks_sum.step(2, True)
        k_sum.step(3)

    norm.over_z()
    j_all.step(1)

    @pl.when(student)
    def _():
        ks_sum.step(3)
        k_sum.step(4)
        ks_sum.step(4)
        err_share().start()
        err_store().start()
        for copy in hid_shares() + hid_stores():
            copy.start()

    norm.over_role()
    j_all.step(2)
    stat[...] = norm.result()
    stores.append(pltpu.make_async_copy(stat, stat_out, store_sem.at[4]))
    stores[-1].start()

    def kx_copy():
        return remote(kx_out, kx_into, bx_s.at[2], bx_r.at[2], place.x_other)

    def gate_copy(i):
        return remote(*((s_gate_out, s_cot.at[z, x]), (gate_out, cot.at[z]))[i], g_s.at[i], g_r.at[i], place.partner)

    def up_store(i):
        here, there = ((s_up_out, s_cot.at[z, x]), (up_out, cot.at[z]))[i]
        return pltpu.make_async_copy(here, there, store_sem.at[10 + i])

    l_all = Gather(place, cot, s_cot, l_s, l_r, ls_s, ls_r, lx_s, lx_r)

    def gate_next(way, i):
        ends = ((s_gate_out, s_cot.at[z, x]), (gate_out, cot.at[z]))[i]
        return remote(*ends, gn_s.at[way, i], (ls_r, l_r)[i].at[way, 0], place.z_next_cross[way])

    def cotangents(total, inputs):
        factor = (16.0 * MODEL) / stat[0:1, 0:1]
        hidden_cot = total * factor
        gate_pre, up_pre = inputs[0], inputs[1]
        sig = jax.nn.sigmoid(gate_pre)
        gate_cot = hidden_cot * up_pre * sig * (1.0 + gate_pre * (1.0 - sig))
        return gate_cot.astype(BF16), (hidden_cot * gate_pre * sig).astype(BF16)

    @pl.when(student)
    def _():
        kx_out[...] = k_sum.result(()).astype(BF16)
        kx_copy().start()
        s_gate_out[...], s_up_out[...] = cotangents(ks_sum.result(()), s_pre)
        for way in (0, 1):
            gate_next(way, 0).start()
        gate_copy(0).start()
        l_all.begin_split(s_up_out)
        up_store(0).start()
        kx_copy().wait_recv()
        gate_out[...], up_out[...] = cotangents(kx_out[...].astype(F32) + kx_into[...].astype(F32), pre)
        for way in (0, 1):
            gate_next(way, 1).start()
        l_all.begin_whole(up_out)
        up_store(1).start()
        gate_copy(1).start()

    @pl.when(teacher)
    def _():
        gate_copy(0).wait_recv()
        l_all.x_copy(0, 0).start()

    for apart in range(1, 8):
        err_copy(apart).wait_send()
        for b in halves:
            d_copy(b, apart).wait_send()
    d_partner().wait_send()
    j_all.step(3)
    l_all.step(1)
    j_all.last()

    def lin_columns(b):
        start = pl.multiple_of(b * 2 * QUARTER + role * QUARTER, QUARTER)
        return lin_out.at[:, :, pl.ds(start, QUARTER)]

    def lin_share(b):
        return remote(lin_err.at[:, b], lin_columns(b), share_s.at[3 + b], share_r.at[3 + b], place.partner)

    def lin_arrival(b):
        start = pl.multiple_of(b * 2 * QUARTER + (1 - role) * QUARTER, QUARTER)
        got = lin_out.at[:, :, pl.ds(start, QUARTER)]
        return remote(lin_err.at[:, b], got, share_s.at[3 + b], share_r.at[3 + b], place.partner)

    lin_stores = [pltpu.make_async_copy(lin_err.at[:, b], lin_columns(b), store_sem.at[5 + b]) for b in halves]
    for b in halves:
        lin_share(b).start()
        lin_stores[b].start()

    @pl.when(student)
    def _():
        err_store().wait()
        err_share().wait_send()
        for copy in hid_stores():
            copy.wait()
        for copy in hid_shares():
            copy.wait_send()
        k_sum.drain()
        ks_sum.drain()

    @pl.when(teacher)
    def _():
        err_share().wait_recv()
        for copy in hid_shares():
            copy.wait_recv()

    factor = (16.0 * MODEL) / stat[0:1, 0:1]

    def rows_of(ref, c):
        return ref[:, :, c * QUARTER : (c + 1) * QUARTER].reshape(Z * ROWS, QUARTER)

    def down_piece(c):
        for b in halves:
            product = contract_rows(rows_of(hid_out, c), err_out[b].reshape(Z * ROWS, QUARTER))
            down_grad[c * QUARTER : (c + 1) * QUARTER, b * QUARTER : (b + 1) * QUARTER] = (factor * product).astype(BF16)

    def linear_piece(c):
        for b in halves:
            product = jnp.dot(
                tok_turned[b * QUARTER : (b + 1) * QUARTER], rows_of(lin_out, c), preferred_element_type=F32
            )
            linear_grad[b * QUARTER : (b + 1) * QUARTER, c * QUARTER : (c + 1) * QUARTER] = (factor * product).astype(BF16)

    for c in range(2):
        down_piece(c)
    c_all.drain()
    e_sum.drain()
    l_all.step(2)
    for c in range(2, 5):
        down_piece(c)
    ex_copy().wait_send()
    norm.drain()
    j_all.drain()
    l_all.step(3)
    for c in range(5, UNITS // QUARTER):
        down_piece(c)
    stores.append(pltpu.make_async_copy(down_grad, down_out, store_sem.at[12]))
    stores[-1].start()
    for b in halves:
        lin_arrival(b).wait_recv()
        lin_stores[b].wait()
    for c in range(LIN // QUARTER):
        linear_piece(c)
    stores.append(pltpu.make_async_copy(linear_grad, linear_out, store_sem.at[13]))
    stores[-1].start()

    @pl.when(teacher)
    def _():
        gate_copy(1).wait_recv()

    l_all.last_split()
    l_all.last_whole()
    l_all.wait_pair()

    for b in halves:
        lin_share(b).wait_send()

    @pl.when(z != mp)
    def _():
        target_copy().wait_send()

    @pl.when(student)
    def _():
        l_all.drain()
        kx_copy().wait_send()
        for i in (0, 1):
            up_store(i).wait()
            gate_copy(i).wait_send()
            for way in (0, 1):
                gate_next(way, i).wait_send()

    @pl.when(teacher)
    def _():
        l_all.drain(2)
        err_partner().wait_send()

    for store in stores:
        store.wait()


def exchange(tokens, w, down, linear):
    def vmem(*shape, dtype=BF16):
        return pltpu.VMEM(shape, dtype)

    def sems(*shape):
        return pltpu.SemaphoreType.DMA(shape)

    def array(*shape, dtype=BF16):
        return jax.ShapeDtypeStruct(shape, dtype)

    def total_tiles():
        return [vmem(8, 8, 128, dtype=F32)] * 2 + [vmem(8, 128, dtype=F32)] * 4

    anywhere = pl.BlockSpec(memory_space=pl.ANY)
    return pl.pallas_call(
        exchange_kernel,
        out_shape=[
            array(WIDTH, Z * ROWS),
            array(Z, ROWS, WHOLE),
            array(Z, 2, ROWS, SPLIT),
            array(UNITS, WIDTH),
            array(WIDTH, LIN),
            array(8, 128, dtype=F32),
        ],
        in_specs=[anywhere] * 4,
        out_specs=[anywhere] * 6,
        scratch_shapes=[
            vmem(2, Z, ROWS, QUARTER), vmem(WIDTH, 2 * UNITS), vmem(UNITS, WIDTH), vmem(2, WIDTH, QUARTER), vmem(WIDTH, UNITS), vmem(WIDTH, Z * ROWS),
            vmem(Z, ROWS, UNITS), vmem(2, Z, ROWS, QUARTER), vmem(Z, ROWS, LIN), vmem(UNITS, WIDTH), vmem(WIDTH, LIN),
            vmem(2, Z, ROWS, WHOLE, dtype=F32), vmem(2, 4, 2, ROWS, WHOLE), vmem(2, 4, 2, ROWS, WHOLE),
            vmem(2, ROWS, WHOLE), vmem(2, ROWS, WHOLE), vmem(2, ROWS, WHOLE, dtype=F32), vmem(Z, ROWS, WHOLE),
            vmem(2, 2, Z, ROWS, SPLIT, dtype=F32), vmem(2, 4, 2, ROWS, SPLIT), vmem(2, 4, 2, ROWS, SPLIT),
            vmem(Z, 2, ROWS, SPLIT), vmem(Z, 2, ROWS, SPLIT), vmem(2, ROWS, SPLIT, dtype=F32), vmem(Z, 2, ROWS, SPLIT),
            vmem(Z * ROWS, WIDTH, dtype=F32), vmem(2, 8, ROWS, QUARTER), vmem(2, 8, ROWS, QUARTER),
            vmem(2, 8, ROWS, QUARTER), vmem(ROWS, QUARTER), vmem(ROWS, QUARTER),
            vmem(2, Z, ROWS, QUARTER, dtype=F32), vmem(2, 4, 2, ROWS, QUARTER), vmem(2, 4, 2, ROWS, QUARTER),
            vmem(ROWS, QUARTER), vmem(ROWS, QUARTER), vmem(Z, 2, ROWS, QUARTER),
            vmem(2, 4, ROWS, WHOLE), vmem(2, 4, ROWS, WHOLE), vmem(ROWS, WHOLE), vmem(ROWS, WHOLE),
            vmem(ROWS, WHOLE), vmem(ROWS, WHOLE),
            vmem(2, 4, ROWS, SPLIT), vmem(2, 4, ROWS, SPLIT), vmem(Z, ROWS, SPLIT), vmem(Z, ROWS, SPLIT),
            vmem(ROWS, SPLIT), vmem(ROWS, SPLIT),
            *total_tiles(), vmem(8, 128, dtype=F32),
            sems(6), sems(14),
            sems(7), sems(7), sems(7), sems(7), sems(2, 4, 2), sems(2, 4, 2), sems(3), sems(3),
            sems(2, 4, 2), sems(2, 4, 2), sems(8), sems(8),
            sems(2, 4), sems(2, 4), sems(2, 4), sems(2, 4), sems(8), sems(8),
            sems(2, 7), sems(2, 7), sems(4), sems(4), sems(7), sems(2, 7), sems(2, 4, 2), sems(2, 4, 2),
            sems(2, 4), sems(2, 4), sems(2, 4), sems(2, 4), sems(8), sems(8),
            sems(2, 4, 2), sems(2, 4, 2), sems(1), sems(1),
            sems(2, 4), sems(2, 4), sems(2, 4), sems(2, 4), sems(8), sems(8), sems(2), sems(2), sems(2, 2),
            sems(7), sems(7), sems(7), sems(7), sems(2), sems(2),
            sems(8), sems(8),
        ],
        compiler_params=pltpu.CompilerParams(
            collective_id=0, has_side_effects=True, vmem_limit_bytes=42 * 1024 * 1024
        ),
        name="exchange",
    )(tokens, w, down, linear)


def contract_rows(left, right):
    return lax.dot_general(left, right, (((0,), (0,)), ((), ())), preferred_element_type=F32)


BLOCK = 256


def gradients_kernel(
    turned, cot, s_cot, stat, down, linear, unit_out, down_out, linear_out, losses, unit, sem
):
    copies = []

    def send(here, there):
        copies.append(pltpu.make_async_copy(here, there, sem.at[len(copies)]))
        copies[-1].start()

    send(down, down_out)
    send(linear, linear_out)
    share = stat[...] / stat[0:1, 0:1]
    losses[0] = share[1, 0]
    losses[1] = share[2, 0]
    for i in range(UNITS // BLOCK):
        part = slice(i * BLOCK, (i + 1) * BLOCK)
        split, column = divmod(i * BLOCK - WHOLE, SPLIT)
        if split < 0:
            columns = cot[:, part]
        else:
            columns = s_cot[:, split, :, column : column + BLOCK].reshape(Z * ROWS, BLOCK)
        unit[:, part] = jnp.dot(turned[...], columns, preferred_element_type=F32).astype(BF16)
        send(unit.at[:, part], unit_out.at[:, part])
    for copy in copies:
        copy.wait()


def gradients(turned, cot, s_cot, stat, down, linear):
    shapes = [(WIDTH, UNITS), (UNITS, WIDTH), (WIDTH, LIN)]
    whole = pl.BlockSpec(memory_space=pltpu.VMEM)
    anywhere = pl.BlockSpec(memory_space=pl.ANY)
    return pl.pallas_call(
        gradients_kernel,
        out_shape=[jax.ShapeDtypeStruct(shape, BF16) for shape in shapes] + [jax.ShapeDtypeStruct((2,), F32)],
        in_specs=[whole] * 4 + [anywhere] * 2,
        out_specs=[anywhere] * 3 + [pl.BlockSpec(memory_space=pltpu.SMEM)],
        scratch_shapes=[
            pltpu.VMEM((WIDTH, UNITS), BF16),
            pltpu.SemaphoreType.DMA((2 + UNITS // BLOCK,)),
        ],
        compiler_params=pltpu.CompilerParams(vmem_limit_bytes=24 * 1024 * 1024),
        name="gradients",
    )(turned, cot, s_cot, stat, down, linear)


def body(tokens, gate_up, down, linear):
    w = gate_up.reshape(WIDTH, 2 * UNITS)
    tok, cot, s_cot, down_own, linear_own, stat = exchange(tokens, w, down[0], linear)
    rows = Z * ROWS
    unit_grad, down_grad, linear_grad, losses = gradients(
        tok, cot.reshape(rows, WHOLE), s_cot, stat, down_own, linear_own
    )
    return (unit_grad[None], down_grad, linear_grad, losses)


def solution(mesh):
    return jax.shard_map(
        body,
        mesh=mesh,
        in_specs=(P("mp", "dp"), P("role", "dp", None, "mp"), P("role", "mp", "dp"), P("dp", "mp")),
        out_specs=(P("role", "dp", "mp"), P("mp", "dp"), P("dp", "mp"), P()),
        check_vma=False,
    )
```
